32 devices in a mesh: seq: 8 (over z, core), tp: 4 (over y, x).
Axes of the slice: x: 2, y: 2, z: 4, core: 2. Of those that a mesh axis runs over, the one named last changes fastest.
Arguments:
- inputs: bfloat16 [4096, 1536], P(('seq', 'tp')), may hold values from -6 to 6
- positions: int32 [4096], P(('seq', 'tp')), may hold values from 0 to 4095, as said below
- attn_gain: float32 [1536], replicated, may hold values from 0.25 to 1.75
- w_query: bfloat16 [1536, 1536], replicated, may hold values from -0.15625 to 0.15625
- w_key: bfloat16 [1536, 1536], replicated, may hold values from -0.15625 to 0.15625
- w_value: bfloat16 [1536, 1536], replicated, may hold values from -0.15625 to 0.15625
- w_out: bfloat16 [1536, 1536], replicated, may hold values from -0.75 to 0.75
- lambda_params: float32 [4, 64], replicated, may hold values from -0.5 to 0.5
- sub_gain: float32 [128], replicated, may hold values from 0.25 to 1.75
- ffn_gain: float32 [1536], replicated, may hold values from 0.25 to 1.75
- w_gate: bfloat16 [1536, 4096], P(None, 'tp'), may hold values from -0.15625 to 0.15625
- w_up: bfloat16 [1536, 4096], P(None, 'tp'), may hold values from -0.15625 to 0.15625
- w_down: bfloat16 [4096, 1536], P('tp'), may hold values from -0.1875 to 0.1875
- cotangent: bfloat16 [4096, 1536], P(('seq', 'tp')), may hold values from -8 to 8
Outputs:
- output: bfloat16 [4096, 1536], P(('seq', 'tp'))
- input_grad: float32 [4096, 1536], P(('seq', 'tp'))
- attn_gain_grad: float32 [1536], P(('seq', 'tp'))
- query_grad: float32 [1536, 1536], P(('seq', 'tp'))
- key_grad: float32 [1536, 1536], P(('seq', 'tp'))
- value_grad: float32 [1536, 1536], P(('seq', 'tp'))
- out_grad: float32 [1536, 1536], P(('seq', 'tp'))
- lambda_grads: float32 [4, 64], replicated
- sub_gain_grad: float32 [128], replicated
- ffn_gain_grad: float32 [1536], P(('seq', 'tp'))
- gate_grad: float32 [1536, 4096], P('seq', 'tp')
- up_grad: float32 [1536, 4096], P('seq', 'tp')
- down_grad: float32 [4096, 1536], P('tp', 'seq')
- lambda_total: float32 [], replicated
- lambda_norm: float32 [], replicated
The draws below stay inside these ranges and needn't reach their ends.
Inputs may be any that keep to these rules, and one draw needn't show every extreme that they name: positions holds each of 0 to 4095 once; each aligned run of 64 rows holds consecutive positions in rising order.
All inputs are finite; a program needn't handle non-finite values.
Results may differ from the reference program's by a relative error of at most 0.033.
Values may be sent and summed in bfloat16 or wider, within the bound.
A program may use at most 448 MiB of HBM per device.

```python
import math
import jax
import jax.numpy as jnp
from jax import lax

D = 1536
H = 12
HALF = 64
FF = 4096
TOK_DEV = 128
VW = 128
HW = 1536
TOKENS = 4096


def draw_positions(key, part):
    key = jax.random.fold_in(key, 7)
    half_rows = TOK_DEV // 2
    run_count = TOKENS // half_rows
    run_order = jax.random.permutation(key, run_count).astype(jnp.int32)
    offsets = jnp.arange(half_rows, dtype=jnp.int32)
    return (run_order[:, None] * half_rows + offsets[None, :]).reshape(TOKENS).astype(jnp.int32)


def draw_cotangent(key, part):
    key = jax.random.fold_in(key, 11)
    first_key, second_key = jax.random.split(key)
    ramp_rows = jnp.arange(TOKENS, dtype=jnp.float32) / max(TOKENS - 1, 1)
    base_draw = jax.random.normal(first_key, (TOKENS, D), jnp.float32)
    shared = 0.8 * jax.random.normal(second_key, (1, D), jnp.float32)
    values = (base_draw + shared) * (1.0 + 2.0 * ramp_rows)[:, None]
    return jnp.clip(values, -8.0, 8.0).astype(jnp.bfloat16)


def block_scale(key, extent, pieces, least, high):
    def one(dim, parts):
        steps = jax.random.uniform(jax.random.fold_in(jax.random.fold_in(key, 6), dim), (parts,), jnp.float32, least / len(pieces), high / len(pieces))
        return jnp.repeat(jnp.exp(steps), extent[dim] // parts).reshape((-1,) + (1,) * (len(extent) - dim - 1))

    factor_of = one(*pieces[0])
    for cut in pieces[1:]:
        factor_of = factor_of * one(*cut)
    return factor_of


def bell_draw(stream_key, shape, scale, most, shards=(), kind=jnp.bfloat16):
    loudness = block_scale(stream_key, shape, shards, -0.22, 0.18) if shards else 1.0
    array = jax.random.normal(stream_key, shape, jnp.float32) * scale * loudness
    return jnp.minimum(jnp.maximum(array, -most), most).astype(kind)


def setup_inputs(seed: int = 0) -> dict:
    arg_keys = jax.random.split(jax.random.key(seed), 15)
    inputs = bell_draw(arg_keys[0], (TOKENS, D), 1.0, 6.0, ((0, 32),))
    positions = draw_positions(jax.random.fold_in(arg_keys[14], 71), 0)
    attn_gain = jnp.clip(1.0 + 0.15 * jax.random.normal(arg_keys[2], (D,), jnp.float32), 0.25, 1.75)
    w_query = bell_draw(arg_keys[3], (D, HW), D ** -0.5, 0.15625)
    w_key = bell_draw(arg_keys[4], (D, HW), D ** -0.5, 0.15625)
    w_value = bell_draw(arg_keys[5], (D, HW), D ** -0.5, 0.15625)
    w_out = bell_draw(arg_keys[6], (HW, D), (HW // 24) ** -0.5, 0.75)
    lambda_params = bell_draw(arg_keys[7], (4, HALF), 0.1, 0.5, (), jnp.float32)
    sub_gain = jnp.clip(1.0 + 0.15 * jax.random.normal(arg_keys[8], (VW,), jnp.float32), 0.25, 1.75)
    ffn_gain = jnp.clip(1.0 + 0.15 * jax.random.normal(arg_keys[9], (D,), jnp.float32), 0.25, 1.75)
    w_gate = bell_draw(arg_keys[10], (D, FF), D ** -0.5, 0.15625, ((1, 4),))
    w_up = bell_draw(arg_keys[11], (D, FF), D ** -0.5, 0.15625, ((1, 4),))
    w_down = bell_draw(arg_keys[12], (FF, D), (FF // 4) ** -0.5, 0.1875, ((0, 4),))
    cotangent = draw_cotangent(jax.random.fold_in(arg_keys[14], 71), 0)
    return dict(inputs=inputs, positions=positions, attn_gain=attn_gain, w_query=w_query, w_key=w_key, w_value=w_value, w_out=w_out, lambda_params=lambda_params, sub_gain=sub_gain, ffn_gain=ffn_gain, w_gate=w_gate, w_up=w_up, w_down=w_down, cotangent=cotangent)


@jax.custom_vjp
def low(v):
    return lax.optimization_barrier(v.astype(jnp.bfloat16)).astype(jnp.float32)

@jax.custom_vjp
def low_back(v):
    return v

def low_keep(v):
    return (low(v), None)

def low_pass(kept, grad):
    return (grad,)

def back_keep(v):
    return (v, None)

def back_low(kept, grad):
    return (low(grad),)
low.defvjp(low_keep, low_pass)
low_back.defvjp(back_keep, back_low)
eps = 1e-05
lambda_init = 0.8 - 0.6 * math.exp(-3.3)
masked_score = -1e+30
highest = lax.Precision.HIGHEST

def matmul(left, right):
    return jnp.dot(left, right, precision=highest)

def rms_rows(values, gain_vec):
    return values * lax.rsqrt(lax.optimization_barrier(jnp.mean(values * values, axis=-1, keepdims=True)) + eps) * gain_vec

def attend_block(query_rows, query_pos, key_rows, value_rows, key_pos, lambda_value):
    allowed = (key_pos[None, :] <= query_pos[:, None])[None]
    score_scale = HALF ** (-0.5)
    mixes = []
    for half_index in range(2):
        lower_col = half_index * HALF
        raw_scores = low_back(jnp.einsum('qhd,khd->hqk', query_rows[:, :, lower_col:lower_col + HALF], key_rows[:, :, lower_col:lower_col + HALF], precision=highest) * score_scale)
        weights_map = low(jax.nn.softmax(jnp.where(allowed, raw_scores, masked_score), axis=-1))
        mixes.append(jnp.einsum('hqk,khd->qhd', weights_map, value_rows, precision=highest))
    return low_back(mixes[0] - lambda_value * mixes[1])

def layer(inputs, positions, attn_gain, w_query, w_key, w_value, w_out, lambda_value, sub_gain, ffn_gain, w_gate, w_up, w_down):
    attn_normed = low(rms_rows(inputs, attn_gain))
    queries = low(low_back(matmul(attn_normed, w_query))).reshape(TOKENS, H, VW)
    key_rows = low(low_back(matmul(attn_normed, w_key))).reshape(TOKENS, H, VW)
    value_rows = low(low_back(matmul(attn_normed, w_value))).reshape(TOKENS, H, VW)
    block_rows = math.gcd(TOKENS, 512)
    block_count = TOKENS // block_rows

    def attend_one(pair_in):
        return attend_block(pair_in[0], pair_in[1], key_rows, value_rows, positions, lambda_value)
    heads_out = lax.map(jax.checkpoint(attend_one), (queries.reshape(block_count, block_rows, H, VW), positions.reshape(block_count, block_rows))).reshape(TOKENS, H, VW)
    mixed_heads = low((rms_rows(heads_out, sub_gain) * (1.0 - lambda_init)).reshape(TOKENS, HW))
    middle = inputs + low_back(matmul(mixed_heads, w_out))
    ffn_in = low(rms_rows(middle, ffn_gain))
    gate_proj = low_back(matmul(ffn_in, w_gate))
    up_proj = low_back(matmul(ffn_in, w_up))
    hidden = low(jax.nn.silu(gate_proj) * up_proj)
    return middle + low_back(matmul(hidden, w_down))

def reference(inputs, positions, attn_gain, w_query, w_key, w_value, w_out, lambda_params, sub_gain, ffn_gain, w_gate, w_up, w_down, cotangent):

    def lambda_of(params):
        return jnp.exp(jnp.sum(params[0] * params[1])) - jnp.exp(jnp.sum(params[2] * params[3])) + lambda_init
    lambda_value, lambda_back = jax.vjp(lambda_of, lambda_params)

    def whole(inputs_f, gain_a, query_f, key_f, value_f, out_f, lambda_f, gain_s, gain_f, gate_f, up_f, down_f):
        return layer(inputs_f, positions, gain_a, query_f, key_f, value_f, out_f, lambda_f, gain_s, gain_f, gate_f, up_f, down_f)
    result, back = jax.vjp(whole, inputs.astype(jnp.float32), attn_gain, w_query.astype(jnp.float32), w_key.astype(jnp.float32), w_value.astype(jnp.float32), w_out.astype(jnp.float32), lambda_value, sub_gain, ffn_gain, w_gate.astype(jnp.float32), w_up.astype(jnp.float32), w_down.astype(jnp.float32))
    grads = back(cotangent.astype(jnp.float32))
    param_grads, = lambda_back(grads[6])
    lambda_norm = jnp.sqrt(jnp.sum(param_grads * param_grads))
    return (result.astype(jnp.bfloat16), grads[0], grads[1], grads[2], grads[3], grads[4], grads[5], param_grads, grads[7], grads[8], grads[9], grads[10], grads[11], grads[6], lambda_norm)
```

```python
import functools
import math

import jax
import jax.numpy as jnp
from jax import lax
from jax.experimental import pallas as pl
from jax.experimental.pallas import tpu as pltpu
from jax.sharding import PartitionSpec as P

H = 12
HALF = 64
VW = 128
HW = 1536

eps = 1e-05
lambda_init = 0.8 - 0.6 * math.exp(-3.3)
masked_score = -1e30
MESH = pl.DeviceIdType.MESH
ANY = pl.BlockSpec(memory_space=pl.ANY)
VMEM = pl.BlockSpec(memory_space=pltpu.VMEM)
SMEM = pl.BlockSpec(memory_space=pltpu.SMEM)
bf16 = jnp.bfloat16
f32 = jnp.float32
vmem_cap = 60 * 1024 * 1024


def dot(left, right):
    return jnp.dot(left, right, preferred_element_type=f32)


def dot_tn(left, right):
    return lax.dot_general(left, right, (((0,), (0,)), ((), ())), preferred_element_type=f32)


def dot_nt(left, right):
    return lax.dot_general(left, right, (((1,), (1,)), ((), ())), preferred_element_type=f32)


def rms_scale(values):
    return lax.rsqrt(jnp.mean(values * values, axis=-1, keepdims=True) + eps)


def rms_back(values, inv_rms, gain_vec, upstream):
    weighted = upstream * gain_vec
    inner_mean = jnp.mean(weighted * values, axis=-1, keepdims=True)
    return inv_rms * weighted - values * (inv_rms * inv_rms * inv_rms) * inner_mean


class Place:
    def __init__(self, seq, tp):
        self.seq, self.tp, self.n = seq, tp, seq * tp
        self.per = -(-H // (seq // 2))
        assert self.per <= tp and seq % 2 == 0

    def me(self):
        s, t = lax.axis_index("seq"), lax.axis_index("tp")
        head = (s // 2) * self.per + t
        active = jnp.logical_and(t < self.per, head < H)
        return s, t, lax.rem(s, 2), head, active

    def head_device(self, index):
        head, core = index // 2, lax.rem(index, 2)
        return 2 * (head // self.per) + core, lax.rem(head, self.per)

    def device(self, linear):
        return linear // self.tp, lax.rem(linear, self.tp)


def remote(src, dst, send, recv, where):
    return pltpu.make_async_remote_copy(
        src_ref=src, dst_ref=dst, send_sem=send, recv_sem=recv, device_id=where, device_id_type=MESH
    )


def loop(count, step):
    def one(k, carry):
        step(k)
        return carry

    lax.fori_loop(0, count, one, 0)


class Dispatch:
    def __init__(self, place):
        self.p = place
        self.sems = [2 * H, place.n, 1]

    def start(self, x, o, send, recv, here):
        p = self.p
        s, t, c, head, active = p.me()
        lin = s * p.tp + t

        def step(k):
            index = lax.rem(k + lin, 2 * H)
            ds, dt = p.head_device(index)
            mine = jnp.logical_and(ds == s, dt == t)

            @pl.when(jnp.logical_not(mine))
            def _():
                remote(
                    x.at[index // 2, lax.rem(index, 2)],
                    o.at[lin],
                    send.at[index],
                    recv.at[lin],
                    (ds, dt),
                ).start()

            @pl.when(mine)
            def _():
                pltpu.make_async_copy(
                    x.at[index // 2, lax.rem(index, 2)], o.at[lin], here.at[0]
                ).start()

        loop(2 * H, step)

    def finish(self, x, o, send, recv, here, arrived=None):
        p = self.p
        s, t, c, head, active = p.me()
        lin = s * p.tp + t

        @pl.when(active)
        def _():
            pltpu.make_async_copy(x.at[0, 0], o.at[lin], here.at[0]).wait()
            if arrived is not None:
                arrived(lin)

            def got(k):
                other = lax.rem(lin + 1 + k, p.n)
                remote(o.at[other], o.at[other], send.at[0], recv.at[other], (s, t)).wait_recv()
                if arrived is not None:
                    arrived(other)

            loop(p.n - 1, got)

        def sent(k):
            ds, dt = p.head_device(k)

            @pl.when(jnp.logical_not(jnp.logical_and(ds == s, dt == t)))
            def _():
                remote(
                    x.at[k // 2, lax.rem(k, 2)], o.at[0], send.at[k], recv.at[0], (ds, dt)
                ).wait_send()

        loop(2 * H, sent)


class Collect:
    def __init__(self, place, halves=False, grouped=False):
        self.p = place
        self.halves = halves
        self.grouped = grouped
        self.sems = [place.n, 2 * H, 1]

    def start(self, x, o, send, recv, here):
        p = self.p
        s, t, c, head, active = p.me()
        lin = s * p.tp + t
        count = p.n // 2 if self.halves else p.n

        @pl.when(active)
        def _():
            def step(k):
                slot = lax.rem(k + lin, count)
                other = slot + c * count if self.halves else slot
                into = o.at[lax.rem(other, p.tp)] if self.grouped else o
                into = into.at[head] if self.halves else into.at[head, c]

                @pl.when(other != lin)
                def _():
                    remote(
                        x.at[slot], into, send.at[slot], recv.at[head * 2 + c], p.device(other)
                    ).start()

                @pl.when(other == lin)
                def _():
                    pltpu.make_async_copy(x.at[slot], into, here.at[0]).start()

            loop(count, step)

    def finish(self, x, o, send, recv, here):
        p = self.p
        s, t, c, head, active = p.me()
        lin = s * p.tp + t
        count = p.n // 2 if self.halves else p.n
        half = lin // count if self.halves else 0
        o = o.at[t] if self.grouped else o

        def got(k):
            index = 2 * k + half if self.halves else k
            into = o.at[k] if self.halves else o.at[k // 2, lax.rem(k, 2)]
            ds, dt = p.head_device(index)
            mine = jnp.logical_and(ds == s, dt == t)

            @pl.when(jnp.logical_not(mine))
            def _():
                remote(into, into, send.at[0], recv.at[index], (s, t)).wait_recv()

            @pl.when(mine)
            def _():
                pltpu.make_async_copy(x.at[0], into, here.at[0]).wait()

        loop(H if self.halves else 2 * H, got)

        @pl.when(active)
        def _():
            def sent(k):
                other = k + c * count if self.halves else k

                @pl.when(other != lin)
                def _():
                    remote(
                        x.at[k], x.at[k], send.at[k], recv.at[0], p.device(other)
                    ).wait_send()

            loop(count, sent)


class Everyone:
    def __init__(self, place, whole):
        self.p, self.whole = place, whole
        self.sems = [place.n, place.n, 1]

    def start(self, x, o, send, recv, here):
        p = self.p
        s, t = lax.axis_index("seq"), lax.axis_index("tp")
        lin = s * p.tp + t
        pltpu.make_async_copy(x if self.whole else x.at[lin], o.at[lin], here.at[0]).start()

        def step(k):
            other = lax.rem(lin + 1 + k, p.n)
            remote(
                x if self.whole else x.at[other],
                o.at[lin],
                send.at[other],
                recv.at[lin],
                p.device(other),
            ).start()

        loop(p.n - 1, step)

    def finish(self, x, o, send, recv, here):
        p = self.p
        s, t = lax.axis_index("seq"), lax.axis_index("tp")
        lin = s * p.tp + t
        pltpu.make_async_copy(x if self.whole else x.at[lin], o.at[lin], here.at[0]).wait()

        def done(k):
            other = lax.rem(lin + 1 + k, p.n)
            both = remote(
                x if self.whole else x.at[other],
                o.at[other],
                send.at[other],
                recv.at[other],
                p.device(other),
            )
            both.wait_recv()
            both.wait_send()

        loop(p.n - 1, done)


class Group:
    def __init__(self, place, whole):
        self.p, self.whole = place, whole
        self.sems = [place.tp, place.tp, 1]

    def start(self, x, o, send, recv, here):
        p = self.p
        s, t = lax.axis_index("seq"), lax.axis_index("tp")
        pltpu.make_async_copy(x if self.whole else x.at[t], o.at[t], here.at[0]).start()
        for k in range(1, p.tp):
            other = lax.rem(t + k, p.tp)
            remote(
                x if self.whole else x.at[other], o.at[t], send.at[other], recv.at[t], (s, other)
            ).start()

    def finish(self, x, o, send, recv, here):
        p = self.p
        s, t = lax.axis_index("seq"), lax.axis_index("tp")
        pltpu.make_async_copy(x if self.whole else x.at[t], o.at[t], here.at[0]).wait()
        for k in range(1, p.tp):
            other = lax.rem(t + k, p.tp)
            both = remote(
                x if self.whole else x.at[other],
                o.at[other],
                send.at[other],
                recv.at[other],
                (s, other),
            )
            both.wait_recv()
            both.wait_send()


def greet(place):
    s, t = lax.axis_index("seq"), lax.axis_index("tp")
    lin = s * place.tp + t
    barrier = pltpu.get_barrier_semaphore()

    def hello(k):
        pl.semaphore_signal(
            barrier,
            inc=1,
            device_id=place.device(lax.rem(lin + 1 + k, place.n)),
            device_id_type=MESH,
        )

    loop(place.n - 1, hello)
    pl.semaphore_wait(barrier, place.n - 1)


def moves(place, parts, arrays, shapes, ident, cost=0):
    count = len(parts)

    def kernel(*refs):
        ins, outs, sems = refs[:count], refs[count : 2 * count], refs[2 * count :]
        greet(place)
        for i, part in enumerate(parts):
            part.start(ins[i], outs[i], *sems[3 * i : 3 * i + 3])
        for i, part in enumerate(parts):
            part.finish(ins[i], outs[i], *sems[3 * i : 3 * i + 3])

    return pl.pallas_call(
        kernel,
        out_shape=[jax.ShapeDtypeStruct(s, a.dtype) for s, a in zip(shapes, arrays)],
        in_specs=[ANY] * count,
        out_specs=[ANY] * count,
        scratch_shapes=[pltpu.SemaphoreType.DMA((k,)) for part in parts for k in part.sems],
        compiler_params=pltpu.CompilerParams(collective_id=ident, has_side_effects=True),
    )(*arrays)


def send_heads(place, payload, run_pos, ident):
    n, rows = place.n, payload.shape[2]
    give, tell = Dispatch(place), Everyone(place, True)

    def kernel(x, r, own, sib, pos, *sems):
        s, t, c, head, active = place.me()
        send, recv = sems[6], sems[7]
        greet(place)
        give.start(x, own, *sems[:3])
        tell.start(r, pos, *sems[3:6])

        def pass_on(k):
            return remote(
                own.at[k, :, VW : 3 * VW], sib.at[k], send.at[k], recv.at[k], (s + 1 - 2 * c, t)
            )

        give.finish(x, own, *sems[:3], arrived=lambda k: pass_on(k).start())

        @pl.when(active)
        def _():
            def done(k):
                pass_on(k).wait_recv()
                pass_on(k).wait_send()

            loop(n, done)

        tell.finish(r, pos, *sems[3:6])

    return pl.pallas_call(
        kernel,
        out_shape=[
            jax.ShapeDtypeStruct((n, rows, 3 * VW), payload.dtype),
            jax.ShapeDtypeStruct((n, rows, 2 * VW), payload.dtype),
            jax.ShapeDtypeStruct((n,) + run_pos.shape, run_pos.dtype),
        ],
        in_specs=[ANY] * 2,
        out_specs=[ANY] * 3,
        scratch_shapes=[pltpu.SemaphoreType.DMA((k,)) for k in give.sems + tell.sems + [n, n]],
        compiler_params=pltpu.CompilerParams(collective_id=ident, has_side_effects=True),
    )(payload, run_pos)


def return_heads(place, mixed, ident):
    n = place.n
    back, share = Collect(place, grouped=True), Group(place, True)

    def kernel(x, o, *sems):
        t = lax.axis_index("tp")
        s = lax.axis_index("seq")
        greet(place)
        own = o.at[t]
        back.start(x, o, *sems[:3])
        back.finish(x, o, *sems[:3])
        send, recv = sems[3], sems[4]
        for k in range(1, place.tp):
            other = lax.rem(t + k, place.tp)
            remote(own, o.at[t], send.at[other], recv.at[t], (s, other)).start()
        for k in range(1, place.tp):
            other = lax.rem(t + k, place.tp)
            both = remote(own, o.at[other], send.at[other], recv.at[other], (s, other))
            both.wait_recv()
            both.wait_send()

    return pl.pallas_call(
        kernel,
        out_shape=jax.ShapeDtypeStruct((place.tp, H, 2) + mixed.shape[1:], mixed.dtype),
        in_specs=[ANY],
        out_specs=ANY,
        scratch_shapes=[pltpu.SemaphoreType.DMA((k,)) for k in back.sems + share.sems[:2]],
        compiler_params=pltpu.CompilerParams(collective_id=ident, has_side_effects=True),
    )(mixed)


def query_rows(n):
    return 256 if n <= 64 else 128


def two_maps(rows):
    lane = lax.broadcasted_iota(jnp.int32, rows.shape, 1)
    zero = jnp.zeros_like(rows)
    return jnp.concatenate(
        [jnp.where(lane < HALF, rows, zero), jnp.where(lane < HALF, zero, rows)], axis=0
    )


def fwd_kernel(n, order, core, lam, own, sib, gain, mixed, mix, lse, qs, ks, vs, score):
    qb = query_rows(n)
    kb_rows = 2 * qb
    c = core[0]
    lambda_value = lam[0]

    def sort(p):
        run = order[p]
        i, b = run // 2, lax.rem(run, 2)
        b = pl.multiple_of(32 * b, 32)
        mine = own[i, pl.ds(b, 32), :]
        other = sib[i, pl.ds(b, 32), :]
        qs[pl.ds(pl.multiple_of(32 * p, 32), 32), :] = mine[:, :VW] * jnp.asarray(0.125, bf16)
        low = pl.multiple_of(64 * p + 32 * c, 32)
        high = pl.multiple_of(64 * p + 32 * (1 - c), 32)
        ks[pl.ds(low, 32), :] = mine[:, VW : 2 * VW]
        vs[pl.ds(low, 32), :] = mine[:, 2 * VW :]
        ks[pl.ds(high, 32), :] = other[:, :VW]
        vs[pl.ds(high, 32), :] = other[:, VW:]

    loop(2 * n, sort)

    def block(j):
        at = pl.ds(pl.multiple_of(qb * j, qb), qb)
        q2 = two_maps(qs[at, :])

        def scores(kb):
            return dot_nt(q2, ks[pl.ds(pl.multiple_of(kb_rows * kb, kb_rows), kb_rows), :])

        def lanes(top, s):
            for i in range(kb_rows // 128):
                top = jnp.maximum(top, s[:, 128 * i : 128 * i + 128])
            return top

        def first(kb, top):
            s = scores(kb)
            score[:, pl.ds(pl.multiple_of(kb_rows * kb, kb_rows), kb_rows)] = s
            return lanes(top, s)

        top = lax.fori_loop(0, j, first, jnp.full((2 * qb, 128), masked_score, f32))
        s = scores(j)
        row = lax.broadcasted_iota(jnp.int32, s.shape, 0)
        row = lax.rem(row, qb)
        allowed = (
            lax.broadcasted_iota(jnp.int32, s.shape, 1)
            <= 64 * (row // 32) + lax.rem(row, 32) + 32 * c
        )
        s = jnp.where(allowed, s, masked_score)
        score[:, pl.ds(pl.multiple_of(kb_rows * j, kb_rows), kb_rows)] = s
        high = jnp.max(lanes(top, s), axis=1, keepdims=True)
        ones = jnp.ones((kb_rows, VW), bf16)

        def second(kb, acc):
            here = pl.ds(pl.multiple_of(kb_rows * kb, kb_rows), kb_rows)
            weights = jnp.exp(score[:, here] - high).astype(bf16)
            return acc + dot(weights, jnp.concatenate([vs[here, :], ones], axis=1))

        acc = lax.fori_loop(0, j + 1, second, jnp.zeros((2 * qb, 2 * VW), f32))
        total = acc[:, VW:]
        mixes = acc[:, :VW] / total
        lse[j] = jnp.transpose(high + jnp.log(total))[:8, :]
        mix[0, at, :] = mixes[:qb]
        mix[1, at, :] = mixes[qb:]
        out = mixes[:qb] - lambda_value * mixes[qb:]
        out = (out * rms_scale(out) * gain[...]).astype(bf16)
        for i in range(qb // 32):
            run = order[j * (qb // 32) + i]
            b = pl.multiple_of(32 * lax.rem(run, 2), 32)
            mixed[run // 2, pl.ds(b, 32), :] = out[32 * i : 32 * i + 32]

    loop(n * 64 // qb, block)


def attend(place, order, core, lam, own, sib, gain):
    n = place.n
    rows = 64 * n
    qb = query_rows(n)
    return pl.pallas_call(
        functools.partial(fwd_kernel, n),
        out_shape=[
            jax.ShapeDtypeStruct((n, 64, VW), bf16),
            jax.ShapeDtypeStruct((2, rows, VW), f32),
            jax.ShapeDtypeStruct((rows // qb, 8, 2 * qb), f32),
            jax.ShapeDtypeStruct((rows, VW), bf16),
            jax.ShapeDtypeStruct((2 * rows, VW), bf16),
            jax.ShapeDtypeStruct((2 * rows, VW), bf16),
        ],
        in_specs=[SMEM, SMEM, SMEM, VMEM, VMEM, VMEM],
        out_specs=[VMEM] * 6,
        scratch_shapes=[pltpu.VMEM((2 * qb, 2 * rows), f32)],
        compiler_params=pltpu.CompilerParams(vmem_limit_bytes=vmem_cap),
        cost_estimate=pl.CostEstimate(
            flops=12 * rows * rows * VW, bytes_accessed=12 * rows * VW, transcendentals=0
        ),
    )(order, core, lam, own, sib, gain)


def bwd_kernel(
    n,
    order,
    core,
    lam,
    grad,
    mix,
    lse,
    qs,
    ks,
    vs,
    gain,
    dq,
    dkv,
    dkv_sib,
    sums,
    dk,
    dv,
):
    qb = query_rows(n)
    kb_rows = 2 * qb
    c = core[0]
    lambda_value = lam[0]
    dk[...] = jnp.zeros_like(dk)
    dv[...] = jnp.zeros_like(dv)
    sums[...] = jnp.zeros_like(sums)

    def block(j):
        at = pl.ds(pl.multiple_of(qb * j, qb), qb)
        pieces = []
        for i in range(qb // 32):
            run = order[j * (qb // 32) + i]
            b = pl.multiple_of(32 * lax.rem(run, 2), 32)
            pieces.append(grad[run // 2, pl.ds(b, 32), :])
        mixed_grad = jnp.concatenate(pieces, axis=0).astype(f32)
        mix_1, mix_2 = mix[0, at, :], mix[1, at, :]
        out = mix_1 - lambda_value * mix_2
        scale = rms_scale(out)
        sums[0:1, :] += jnp.sum(mixed_grad * out * scale, axis=0, keepdims=True) * (
            1.0 - lambda_init
        )
        heads_grad = rms_back(out, scale, gain[...], mixed_grad).astype(bf16)
        grad_f = heads_grad.astype(f32)
        dot_2 = grad_f * mix_2
        sums[1:2, :] += -jnp.sum(dot_2, axis=0, keepdims=True)
        delta_1 = jnp.sum(jnp.transpose(grad_f * mix_1), axis=0, keepdims=True)
        delta_2 = -lambda_value * jnp.sum(jnp.transpose(dot_2), axis=0, keepdims=True)
        q2 = two_maps(qs[at, :])
        lse_now = lse[j][0:1, :]

        def piece(kb, acc, diagonal):
            here = pl.ds(pl.multiple_of(kb_rows * kb, kb_rows), kb_rows)
            keys = ks[here, :]
            s = dot_nt(keys, q2) - lse_now
            if diagonal:
                col = lax.rem(lax.broadcasted_iota(jnp.int32, s.shape, 1), qb)
                allowed = (
                    lax.broadcasted_iota(jnp.int32, s.shape, 0)
                    <= 64 * (col // 32) + lax.rem(col, 32) + 32 * c
                )
                s = jnp.where(allowed, s, masked_score)
            prob = jnp.exp(s)
            prob_1, prob_2 = prob[:, :qb], prob[:, qb:]
            value_dot = dot_nt(vs[here, :], heads_grad)
            grads = jnp.concatenate(
                [
                    (prob_1 * (value_dot - delta_1)).astype(bf16),
                    (prob_2 * (-lambda_value * value_dot - delta_2)).astype(bf16),
                ],
                axis=1,
            )
            dv[here, :] += dot((prob_1 - lambda_value * prob_2).astype(bf16), heads_grad)
            dk[here, :] += dot(grads, q2)
            return acc + dot_tn(grads, keys)

        acc = lax.fori_loop(
            0, j, lambda kb, a: piece(kb, a, False), jnp.zeros((2 * qb, VW), f32)
        )
        acc = piece(j, acc, True)
        lane = lax.broadcasted_iota(jnp.int32, (qb, VW), 1)
        done = (jnp.where(lane < HALF, acc[:qb], acc[qb:]) * 0.125).astype(bf16)
        for i in range(qb // 32):
            run = order[j * (qb // 32) + i]
            b = pl.multiple_of(32 * lax.rem(run, 2), 32)
            dq[run // 2, pl.ds(b, 32), :] = done[32 * i : 32 * i + 32]

    loop(n * 64 // qb, block)

    def unsort(p):
        run = order[p]
        b = pl.multiple_of(32 * lax.rem(run, 2), 32)
        low = pl.multiple_of(64 * p + 32 * c, 32)
        high = pl.multiple_of(64 * p + 32 * (1 - c), 32)
        dkv[run // 2, pl.ds(b, 32), :VW] = dk[pl.ds(low, 32), :]
        dkv[run // 2, pl.ds(b, 32), VW:] = dv[pl.ds(low, 32), :]
        dkv_sib[run // 2, pl.ds(b, 32), :VW] = dk[pl.ds(high, 32), :]
        dkv_sib[run // 2, pl.ds(b, 32), VW:] = dv[pl.ds(high, 32), :]

    loop(2 * n, unsort)


def attend_back(place, order, core, lam, grad, saved, gain):
    n = place.n
    rows = 64 * n
    qb = query_rows(n)
    return pl.pallas_call(
        functools.partial(bwd_kernel, n),
        out_shape=[
            jax.ShapeDtypeStruct((n, 64, VW), bf16),
            jax.ShapeDtypeStruct((n, 64, 2 * VW), f32),
            jax.ShapeDtypeStruct((n, 64, 2 * VW), f32),
            jax.ShapeDtypeStruct((8, VW), f32),
        ],
        in_specs=[SMEM, SMEM, SMEM] + [VMEM] * 7,
        out_specs=[VMEM] * 4,
        scratch_shapes=[pltpu.VMEM((2 * rows, VW), f32)] * 2,
        compiler_params=pltpu.CompilerParams(vmem_limit_bytes=vmem_cap),
        cost_estimate=pl.CostEstimate(
            flops=30 * rows * rows * VW, bytes_accessed=30 * rows * VW, transcendentals=0
        ),
    )(order, core, lam, grad, *saved, gain)


def to_heads(rows):
    return rows.reshape(2, 2, 32, H, VW).transpose(3, 1, 0, 2, 4).reshape(H, 2, 64, VW)


def from_heads(blocks):
    lead = blocks.shape[:-4]
    k = len(lead)
    split = blocks.reshape(lead + (H, 2, 2, 32, VW))
    order = tuple(range(k)) + (k + 2, k + 1, k + 3, k, k + 4)
    return split.transpose(order).reshape(lead + (128, HW))


def body(
    place,
    inputs,
    positions,
    attn_gain,
    w_query,
    w_key,
    w_value,
    w_out,
    lambda_params,
    sub_gain,
    ffn_gain,
    w_gate,
    w_up,
    w_down,
    cotangent,
):
    n, tp, seq = place.n, place.tp, place.seq
    s, t, core, head, active = place.me()
    lin = s * tp + t
    row_count, width = inputs.shape
    part = width // n
    inputs_f = inputs.astype(f32)
    attn_scale = rms_scale(inputs_f)
    attn_normed = (inputs_f * attn_scale * attn_gain).astype(bf16)
    group_rows = lax.all_gather(
        jnp.concatenate([inputs, cotangent], axis=1), "tp", axis=0, tiled=True
    )
    inputs_all, cotangent_all = group_rows[:, :width], group_rows[:, width:]
    first_exp = jnp.exp(jnp.sum(lambda_params[0] * lambda_params[1]))
    second_exp = jnp.exp(jnp.sum(lambda_params[2] * lambda_params[3]))
    lambda_value = first_exp - second_exp + lambda_init
    lam = lambda_value.reshape(1)

    payload = jnp.concatenate(
        [to_heads(dot(attn_normed, w).astype(bf16)) for w in (w_query, w_key, w_value)], axis=3
    )
    own, sib, pos = send_heads(place, payload, positions.reshape(1, row_count), 1)
    blocks = pos.reshape(2 * n, 64)[:, 0] // 64
    run = jnp.arange(2 * n, dtype=jnp.int32)
    order = jnp.sum(jnp.where(blocks[None, :] == run[:, None], run[None, :], 0), axis=1)
    core_1 = core.reshape(1).astype(jnp.int32)
    head_gain = (sub_gain * (1.0 - lambda_init)).reshape(1, VW)
    mixed, *saved = attend(place, order, core_1, lam, own, sib, head_gain)
    normed_all = lax.all_gather(attn_normed, ("seq", "tp"), axis=0, tiled=True)
    mixed_all = from_heads(return_heads(place, mixed, 2)).reshape(tp * row_count, HW)

    middle_all = inputs_all.astype(f32) + dot(mixed_all, w_out)
    scale_all = rms_scale(middle_all)
    ffn_rows = (middle_all * scale_all * ffn_gain).astype(bf16)
    middle = lax.dynamic_slice_in_dim(middle_all, t * row_count, row_count, 0)
    ffn_scale = rms_scale(middle)
    gate_proj = dot(ffn_rows, w_gate)
    up_proj = dot(ffn_rows, w_up)
    gate_sig = jax.nn.sigmoid(gate_proj)
    gate_act = gate_proj * gate_sig
    hidden = (gate_act * up_proj).astype(bf16)
    hidden_grad = dot_nt(cotangent_all, w_down)
    gate_rows_grad = (
        hidden_grad * up_proj * gate_sig * (1.0 + gate_proj * (1.0 - gate_sig))
    ).astype(bf16)
    up_rows_grad = (hidden_grad * gate_act).astype(bf16)
    ffn_partial = dot_nt(gate_rows_grad, w_gate) + dot_nt(up_rows_grad, w_up)
    (grad_parts,) = moves(
        place,
        [Group(place, False)],
        [ffn_partial.astype(bf16).reshape(tp, row_count, width)],
        [(tp, row_count, width)],
        3,
    )
    own_partial = lax.dynamic_slice_in_dim(ffn_partial, t * row_count, row_count, 0)
    member = jnp.arange(tp)[:, None, None]
    ffn_in_grad = own_partial + jnp.sum(
        jnp.where(member == t, 0.0, grad_parts.astype(f32)), axis=0
    )
    ffn_gain_part = jnp.sum(ffn_in_grad * middle * ffn_scale, axis=0)
    middle_grad = cotangent.astype(f32) + rms_back(middle, ffn_scale, ffn_gain, ffn_in_grad)
    branch_grad = middle_grad.astype(bf16)

    down_part = dot_tn(cotangent_all, hidden).astype(bf16)
    gate_part = dot_tn(ffn_rows, gate_rows_grad).astype(bf16)
    up_part = dot_tn(ffn_rows, up_rows_grad).astype(bf16)

    def scatter_rows(array):
        return lax.psum_scatter(array, "seq", scatter_dimension=0, tiled=True)

    down_grad = scatter_rows(down_part).astype(f32).T
    gate_grad = scatter_rows(gate_part).astype(f32)
    up_grad = scatter_rows(up_part).astype(f32)

    mixed_grad = to_heads(dot_nt(branch_grad, w_out).astype(bf16))
    grad_heads, branch_all = moves(
        place,
        [Dispatch(place), Group(place, True)],
        [mixed_grad, branch_grad],
        [(n, 64, VW), (tp, row_count, width)],
        4,
    )
    mixed_cols = lax.dynamic_index_in_dim(
        mixed_all.reshape(tp * row_count, seq, tp, part), t, 2, keepdims=False
    ).reshape(tp * row_count, seq * part)
    out_part = dot_tn(mixed_cols, branch_all.reshape(tp * row_count, width)).astype(bf16)
    out_grad = scatter_rows(out_part).astype(f32)

    dq, dkv, dkv_sib, sums = attend_back(place, order, core_1, lam, grad_heads, saved, head_gain)
    swap = [(i, i ^ 1) for i in range(seq)]
    dkv = dkv + lax.ppermute(dkv_sib, "seq", swap)
    back = jnp.concatenate([dq, dkv.astype(bf16)], axis=2)

    ffn_out = dot(hidden, w_down)
    rows_back, out_parts = moves(
        place,
        [Collect(place), Group(place, False)],
        [back, ffn_out.astype(bf16).reshape(tp, row_count, width)],
        [(H, 2, 64, 3 * VW), (tp, row_count, width)],
        5,
    )
    output = (middle + jnp.sum(out_parts.astype(f32), axis=0)).astype(bf16)

    normed_half = lax.dynamic_index_in_dim(
        normed_all.reshape(n, 2, 2, 32, width), core, 2, keepdims=False
    ).reshape(n * 64, width)
    weight_part = dot_tn(normed_half, back.reshape(n * 64, 3 * VW))
    keep = lax.dynamic_slice_in_dim(weight_part, core * (width // 2), width // 2, 0)
    away = lax.dynamic_slice_in_dim(weight_part, (1 - core) * (width // 2), width // 2, 0)
    weight_half = (keep + lax.ppermute(away, "seq", swap)).astype(bf16)

    normed_grad = sum(
        dot_nt(from_heads(rows_back[..., i * VW : (i + 1) * VW]), w)
        for i, w in enumerate((w_query, w_key, w_value))
    )
    attn_gain_part = jnp.sum(normed_grad * inputs_f * attn_scale, axis=0)
    input_grad = middle_grad + rms_back(inputs_f, attn_scale, attn_gain, normed_grad)

    sums = jnp.where(active, sums, 0.0)
    pad = ((0, 0), (0, 128 - part))
    small = jnp.stack(
        [
            jnp.pad(attn_gain_part.reshape(n, part), pad),
            jnp.pad(ffn_gain_part.reshape(n, part), pad),
            jnp.broadcast_to(sums[0], (n, VW)),
            jnp.broadcast_to(sums[1], (n, VW)),
        ]
        + [jnp.zeros((n, VW), f32)] * 4,
        axis=1,
    )
    weight_rows, small_all = moves(
        place,
        [Collect(place, True), Everyone(place, False)],
        [weight_half.reshape(n // 2, part, 3 * VW), small],
        [(H, part, 3 * VW), (n, 8, VW)],
        6,
    )
    weight_rows = weight_rows.astype(f32).reshape(H, part, 3, VW).transpose(2, 1, 0, 3)
    weight_rows = weight_rows.reshape(3, part, HW)
    small_sum = jnp.sum(small_all, axis=0)
    lambda_total = jnp.sum(small_sum[3])
    lambda_grads = jnp.stack(
        [
            lambda_total * first_exp * lambda_params[1],
            lambda_total * first_exp * lambda_params[0],
            -lambda_total * second_exp * lambda_params[3],
            -lambda_total * second_exp * lambda_params[2],
        ]
    )
    lambda_norm = jnp.sqrt(jnp.sum(lambda_grads * lambda_grads))
    return (
        output,
        input_grad,
        small_sum[0, :part],
        weight_rows[0],
        weight_rows[1],
        weight_rows[2],
        out_grad,
        lambda_grads,
        small_sum[2],
        small_sum[1, :part],
        gate_grad,
        up_grad,
        down_grad,
        lambda_total,
        lambda_norm,
    )


def solution(mesh):
    place = Place(mesh.shape["seq"], mesh.shape["tp"])
    both = ("seq", "tp")
    placed = (
        P(both, None),
        P(both),
        P(),
        P(),
        P(),
        P(),
        P(),
        P(),
        P(),
        P(),
        P(None, "tp"),
        P(None, "tp"),
        P("tp", None),
        P(both, None),
    )
    return jax.shard_map(
        functools.partial(body, place),
        mesh=mesh,
        in_specs=placed,
        out_specs=(
            P(both, None),
            P(both, None),
            P(both),
            P(both, None),
            P(both, None),
            P(both, None),
            P(both, None),
            P(),
            P(),
            P(both),
            P("seq", "tp"),
            P("seq", "tp"),
            P("tp", "seq"),
            P(),
            P(),
        ),
        check_vma=False,
    )
```

```python
import functools
import math

import jax
import jax.numpy as jnp
from jax import lax
from jax.experimental import pallas as pl
from jax.experimental.pallas import tpu as pltpu
from jax.sharding import PartitionSpec as P

H = 12
HALF = 64
VW = 128
HW = 1536

eps = 1e-05
lambda_init = 0.8 - 0.6 * math.exp(-3.3)
masked_score = -1e30
MESH = pl.DeviceIdType.MESH
ANY = pl.BlockSpec(memory_space=pl.ANY)
VMEM = pl.BlockSpec(memory_space=pltpu.VMEM)
SMEM = pl.BlockSpec(memory_space=pltpu.SMEM)
bf16 = jnp.bfloat16
f32 = jnp.float32
vmem_cap = 60 * 1024 * 1024


def dot(left, right):
    return jnp.dot(left, right, preferred_element_type=f32)


def dot_tn(left, right):
    return lax.dot_general(left, right, (((0,), (0,)), ((), ())), preferred_element_type=f32)


def dot_nt(left, right):
    return lax.dot_general(left, right, (((1,), (1,)), ((), ())), preferred_element_type=f32)


def rms_scale(values):
    return lax.rsqrt(jnp.mean(values * values, axis=-1, keepdims=True) + eps)


def rms_back(values, inv_rms, gain_vec, upstream):
    weighted = upstream * gain_vec
    inner_mean = jnp.mean(weighted * values, axis=-1, keepdims=True)
    return inv_rms * weighted - values * (inv_rms * inv_rms * inv_rms) * inner_mean


class Place:
    def __init__(self, seq, tp):
        self.seq, self.tp, self.n = seq, tp, seq * tp
        self.per = -(-H // (seq // 2))
        assert self.per <= tp and seq % 2 == 0

    def me(self):
        s, t = lax.axis_index("seq"), lax.axis_index("tp")
        head = (s // 2) * self.per + t
        active = jnp.logical_and(t < self.per, head < H)
        return s, t, lax.rem(s, 2), head, active

    def head_device(self, index):
        head, core = index // 2, lax.rem(index, 2)
        return 2 * (head // self.per) + core, lax.rem(head, self.per)

    def device(self, linear):
        return linear // self.tp, lax.rem(linear, self.tp)


def busy(microseconds):
    return pl.CostEstimate(
        flops=int(microseconds * 1e9), bytes_accessed=int(microseconds * 3e6), transcendentals=0
    )


def remote(src, dst, send, recv, where):
    return pltpu.make_async_remote_copy(
        src_ref=src, dst_ref=dst, send_sem=send, recv_sem=recv, device_id=where, device_id_type=MESH
    )


def loop(count, step):
    def one(k, carry):
        step(k)
        return carry

    lax.fori_loop(0, count, one, 0)


class Dispatch:
    def __init__(self, place, cut):
        self.p, self.cut = place, cut
        self.sems = [2 * H, place.n, 1]

    def start_one(self, index, x, o, send, recv, here):
        p = self.p
        s, t, c, head, active = p.me()
        lin = s * p.tp + t
        ds, dt = p.head_device(index)
        mine = jnp.logical_and(ds == s, dt == t)
        source = self.cut(x, index // 2, lax.rem(index, 2))

        @pl.when(jnp.logical_not(mine))
        def _():
            remote(source, o.at[lin], send.at[index], recv.at[lin], (ds, dt)).start()

        @pl.when(mine)
        def _():
            pltpu.make_async_copy(source, o.at[lin], here.at[0]).start()

    def start(self, *refs):
        p = self.p
        lin = lax.axis_index("seq") * p.tp + lax.axis_index("tp")
        loop(2 * H, lambda k: self.start_one(lax.rem(k + lin, 2 * H), *refs))

    def finish(self, x, o, send, recv, here, arrived=None):
        p = self.p
        s, t, c, head, active = p.me()
        lin = s * p.tp + t

        @pl.when(active)
        def _():
            pltpu.make_async_copy(self.cut(x, head, c), o.at[lin], here.at[0]).wait()
            if arrived is not None:
                arrived(lin)

            def got(k):
                other = lax.rem(lin + 1 + k, p.n)
                remote(o.at[other], o.at[other], send.at[0], recv.at[other], (s, t)).wait_recv()
                if arrived is not None:
                    arrived(other)

            loop(p.n - 1, got)

        def sent(k):
            ds, dt = p.head_device(k)

            @pl.when(jnp.logical_not(jnp.logical_and(ds == s, dt == t)))
            def _():
                remote(
                    self.cut(x, k // 2, lax.rem(k, 2)), o.at[0], send.at[k], recv.at[0], (ds, dt)
                ).wait_send()

        loop(2 * H, sent)


class Collect:
    def __init__(self, place, into, halves=False):
        self.p, self.into, self.halves = place, into, halves
        self.sems = [place.n, 2 * H, 1]

    def start(self, x, o, send, recv, here):
        p = self.p
        s, t, c, head, active = p.me()
        lin = s * p.tp + t
        count = p.n // 2 if self.halves else p.n

        @pl.when(active)
        def _():
            def step(k):
                slot = lax.rem(k + lin, count)
                other = slot + c * count if self.halves else slot
                into = self.into(o, lax.rem(other, p.tp), head, c)

                @pl.when(other != lin)
                def _():
                    remote(
                        x.at[slot], into, send.at[slot], recv.at[head * 2 + c], p.device(other)
                    ).start()

                @pl.when(other == lin)
                def _():
                    pltpu.make_async_copy(x.at[slot], into, here.at[0]).start()

            loop(count, step)

    def got(self, index, x, o, send, recv, here):
        p = self.p
        s, t = lax.axis_index("seq"), lax.axis_index("tp")
        into = self.into(o, t, index // 2, lax.rem(index, 2))
        ds, dt = p.head_device(index)
        mine = jnp.logical_and(ds == s, dt == t)

        @pl.when(jnp.logical_not(mine))
        def _():
            remote(into, into, send.at[0], recv.at[index], (s, t)).wait_recv()

        @pl.when(mine)
        def _():
            pltpu.make_async_copy(x.at[0], into, here.at[0]).wait()

    def sent(self, x, o, send, recv, here):
        p = self.p
        s, t, c, head, active = p.me()
        lin = s * p.tp + t
        count = p.n // 2 if self.halves else p.n

        @pl.when(active)
        def _():
            def one(k):
                other = k + c * count if self.halves else k

                @pl.when(other != lin)
                def _():
                    remote(
                        x.at[k], x.at[k], send.at[k], recv.at[0], p.device(other)
                    ).wait_send()

            loop(count, one)

    def finish(self, *refs):
        p = self.p
        if self.halves:
            lin = lax.axis_index("seq") * p.tp + lax.axis_index("tp")
            half = lin // (p.n // 2)
            loop(H, lambda k: self.got(2 * k + half, *refs))
        else:
            loop(2 * H, lambda k: self.got(k, *refs))
        self.sent(*refs)


class Everyone:
    def __init__(self, place, whole):
        self.p, self.whole = place, whole
        self.sems = [place.n, place.n, 1]

    def start(self, x, o, send, recv, here):
        p = self.p
        s, t = lax.axis_index("seq"), lax.axis_index("tp")
        lin = s * p.tp + t
        pltpu.make_async_copy(x if self.whole else x.at[lin], o.at[lin], here.at[0]).start()

        def step(k):
            other = lax.rem(lin + 1 + k, p.n)
            remote(
                x if self.whole else x.at[other],
                o.at[lin],
                send.at[other],
                recv.at[lin],
                p.device(other),
            ).start()

        loop(p.n - 1, step)

    def finish(self, x, o, send, recv, here):
        p = self.p
        s, t = lax.axis_index("seq"), lax.axis_index("tp")
        lin = s * p.tp + t
        pltpu.make_async_copy(x if self.whole else x.at[lin], o.at[lin], here.at[0]).wait()

        def done(k):
            other = lax.rem(lin + 1 + k, p.n)
            both = remote(
                x if self.whole else x.at[other],
                o.at[other],
                send.at[other],
                recv.at[other],
                p.device(other),
            )
            both.wait_recv()
            both.wait_send()

        loop(p.n - 1, done)


class Group:
    def __init__(self, place, whole):
        self.p, self.whole = place, whole
        self.sems = [place.tp, place.tp, 1]

    def start(self, x, o, send, recv, here):
        p = self.p
        s, t = lax.axis_index("seq"), lax.axis_index("tp")
        pltpu.make_async_copy(x if self.whole else x.at[t], o.at[t], here.at[0]).start()
        for k in range(1, p.tp):
            other = lax.rem(t + k, p.tp)
            remote(
                x if self.whole else x.at[other], o.at[t], send.at[other], recv.at[t], (s, other)
            ).start()

    def finish(self, x, o, send, recv, here):
        p = self.p
        s, t = lax.axis_index("seq"), lax.axis_index("tp")
        pltpu.make_async_copy(x if self.whole else x.at[t], o.at[t], here.at[0]).wait()
        for k in range(1, p.tp):
            other = lax.rem(t + k, p.tp)
            both = remote(
                x if self.whole else x.at[other],
                o.at[other],
                send.at[other],
                recv.at[other],
                (s, other),
            )
            both.wait_recv()
            both.wait_send()


def greet(place):
    s, t = lax.axis_index("seq"), lax.axis_index("tp")
    lin = s * place.tp + t
    barrier = pltpu.get_barrier_semaphore()

    def hello(k):
        pl.semaphore_signal(
            barrier,
            inc=1,
            device_id=place.device(lax.rem(lin + 1 + k, place.n)),
            device_id_type=MESH,
        )

    loop(place.n - 1, hello)
    pl.semaphore_wait(barrier, place.n - 1)


def moves(place, parts, arrays, outs, ident, cost, work=None, operands=(), results=(), scratch=()):
    count, extra = len(parts), len(operands)

    def kernel(*refs):
        ins, given = refs[:count], refs[count : count + extra]
        refs = refs[count + extra :]
        into, made = refs[:count], refs[count : count + len(results)]
        refs = refs[count + len(results) :]
        sems, rest = refs[: 3 * count], refs[3 * count :]
        greet(place)
        for i, part in enumerate(parts):
            part.start(ins[i], into[i], *sems[3 * i : 3 * i + 3])
        if work is not None:
            work(given, made, rest)
        for i, part in enumerate(parts):
            part.finish(ins[i], into[i], *sems[3 * i : 3 * i + 3])

    return pl.pallas_call(
        kernel,
        out_shape=[jax.ShapeDtypeStruct(s, a.dtype) for s, a in zip(outs, arrays)]
        + [shape for shape, spec in results],
        in_specs=[ANY] * count + [spec for array, spec in operands],
        out_specs=[ANY] * count + [spec for shape, spec in results],
        scratch_shapes=[pltpu.SemaphoreType.DMA((k,)) for part in parts for k in part.sems]
        + list(scratch),
        compiler_params=pltpu.CompilerParams(
            collective_id=ident, has_side_effects=True, vmem_limit_bytes=vmem_cap
        ),
        cost_estimate=busy(cost),
    )(*arrays, *[array for array, spec in operands])


def send_heads(place, normed, weights, run_pos, cotangent, ident):
    n, rows = place.n, normed.shape[0] // 2
    width = normed.shape[1]
    give = Dispatch(place, lambda x, h, c: x.at[h, c])
    tell = Everyone(place, True)
    share = Group(place, True)

    def turn(k):
        lin = lax.axis_index("seq") * place.tp + lax.axis_index("tp")
        return lax.rem(k + lin, H)

    def kernel(x, wq, wk, wv, r, cot, own, sib, pos, cot_all, made, *sems):
        s, t, c, head, active = place.me()
        send, recv = sems[9], sems[10]
        k = pl.program_id(0)

        @pl.when(k == 0)
        def _():
            greet(place)
            tell.start(r, pos, *sems[3:6])
            share.start(cot, cot_all, *sems[6:9])

        now = turn(k)
        for i, w in enumerate((wq, wk, wv)):
            out = dot(x[...], w[...]).astype(bf16)
            made[now, 0, :, i * VW : (i + 1) * VW] = out[:rows]
            made[now, 1, :, i * VW : (i + 1) * VW] = out[rows:]
        give.start_one(2 * now, made, own, *sems[:3])
        give.start_one(2 * now + 1, made, own, *sems[:3])

        @pl.when(k == H - 1)
        def _():
            def pass_on(j):
                return remote(
                    own.at[j, :, VW : 3 * VW],
                    sib.at[j],
                    send.at[j],
                    recv.at[j],
                    (s + 1 - 2 * c, t),
                )

            give.finish(made, own, *sems[:3], arrived=lambda j: pass_on(j).start())

            @pl.when(active)
            def _():
                def done(j):
                    pass_on(j).wait_recv()
                    pass_on(j).wait_send()

                loop(n, done)

            tell.finish(r, pos, *sems[3:6])
            share.finish(cot, cot_all, *sems[6:9])

    columns = pl.BlockSpec((width, VW), lambda k: (0, turn(k)))
    return pl.pallas_call(
        kernel,
        grid=(H,),
        out_shape=[
            jax.ShapeDtypeStruct((n, rows, 3 * VW), bf16),
            jax.ShapeDtypeStruct((n, rows, 2 * VW), bf16),
            jax.ShapeDtypeStruct((n,) + run_pos.shape, run_pos.dtype),
            jax.ShapeDtypeStruct((place.tp,) + cotangent.shape, bf16),
        ],
        in_specs=[pl.BlockSpec(normed.shape, lambda k: (0, 0))] + [columns] * 3 + [ANY] * 2,
        out_specs=[ANY] * 4,
        scratch_shapes=[pltpu.VMEM((H, 2, rows, 3 * VW), bf16)]
        + [pltpu.SemaphoreType.DMA((k,)) for k in give.sems + tell.sems + share.sems + [n, n]],
        compiler_params=pltpu.CompilerParams(
            collective_id=ident, has_side_effects=True, vmem_limit_bytes=vmem_cap
        ),
        cost_estimate=busy(35),
    )(normed, *weights, run_pos, cotangent)


def return_heads(place, mixed, ident):
    n, rows = place.n, mixed.shape[1]

    def into(o, t, h, c):
        return o.at[
            t,
            pl.ds(pl.multiple_of(rows * c, rows), rows),
            pl.ds(pl.multiple_of(VW * h, VW), VW),
        ]

    back = Collect(place, into)

    def kernel(x, o, *sems):
        s, t = lax.axis_index("seq"), lax.axis_index("tp")
        greet(place)
        back.start(x, o, *sems[:3])
        send, recv = sems[3], sems[4]

        def share(k, c, slot):
            other = lax.rem(t + k, place.tp)
            return remote(
                o.at[t, rows * c : rows * c + rows, :],
                o.at[slot(other), rows * c : rows * c + rows, :],
                send.at[2 * other + c],
                recv.at[2 * slot(other) + c],
                (s, other),
            )

        for c in range(2):
            loop(H, lambda h: back.got(2 * h + c, x, o, *sems[:3]))
            for k in range(1, place.tp):
                share(k, c, lambda other: t).start()
        for c in range(2):
            for k in range(1, place.tp):
                both = share(k, c, lambda other: other)
                both.wait_recv()
                both.wait_send()
        back.sent(x, o, *sems[:3])

    return pl.pallas_call(
        kernel,
        out_shape=jax.ShapeDtypeStruct((place.tp, 2 * rows, HW), mixed.dtype),
        in_specs=[ANY],
        out_specs=ANY,
        scratch_shapes=[
            pltpu.SemaphoreType.DMA((k,)) for k in back.sems + [2 * place.tp, 2 * place.tp]
        ],
        compiler_params=pltpu.CompilerParams(collective_id=ident, has_side_effects=True),
        cost_estimate=busy(35),
    )(mixed)


def finish_heads(
    place, dq, dkv, dkv_sib, rows_all, gain, weights, ffn_out, branch_grad, ident
):
    n, half = place.n, dq.shape[1]
    width = rows_all.shape[2]
    part, chunk, lot = width // n, 256, 8

    def into(o, t, h, c):
        return o.at[
            pl.ds(pl.multiple_of(half * c, half), half),
            pl.ds(pl.multiple_of(3 * VW * h, 3 * VW), 3 * VW),
        ]

    back, ffn, share = Collect(place, into), Group(place, False), Group(place, True)

    def kernel(*refs):
        dq, dkv, dkv_sib, rows_all, gain, *refs = refs
        weights, refs = refs[:3], refs[3:]
        ffn_out, branch, normed_grad, weight_half, ffn_parts, branch_all, *refs = refs
        other_dkv, grads, rows_back, raw, held, away, other, w_all, *sems = refs
        s, t = lax.axis_index("seq"), lax.axis_index("tp")
        c = lax.rem(s, 2)
        send, recv, raw_sem, w_sem = sems[9:]
        sibling = (s + 1 - 2 * c, t)
        greet(place)
        swap = remote(dkv_sib, other_dkv, send.at[0], recv.at[0], sibling)
        swap.start()

        def fetch(i):
            return pltpu.make_async_copy(
                rows_all.at[
                    pl.ds(lot * i, lot), pl.ds(pl.multiple_of(half * c, half), half), :
                ],
                raw.at[lax.rem(i, 2)],
                raw_sem.at[lax.rem(i, 2)],
            )

        fetch(0).start()
        loads = [
            pltpu.make_async_copy(w, w_all.at[i], w_sem.at[i]) for i, w in enumerate(weights)
        ]
        for load in loads:
            load.start()
        swap.wait_recv()

        def join(i):
            grads[i, :, :VW] = dq[i]
            grads[i, :, VW:] = (dkv[i] + other_dkv[i].astype(f32)).astype(bf16)

        loop(n, join)
        back.start(grads, rows_back, *sems[:3])
        share.start(branch, branch_all, *sems[6:9])
        ffn.start(ffn_out, ffn_parts, *sems[3:6])
        held[...] = jnp.zeros_like(held)

        def rows(i):
            @pl.when(i + 1 < n // lot)
            def _():
                fetch(i + 1).start()

            fetch(i).wait()
            x = raw[lax.rem(i, 2)].reshape(lot * half, width).astype(f32)
            x = (x * rms_scale(x) * gain[...]).astype(bf16)
            g = grads[pl.ds(lot * i, lot)].reshape(lot * half, 3 * VW)
            for k in range(width // chunk):
                held[k * chunk : (k + 1) * chunk, :] += dot_tn(
                    x[:, k * chunk : (k + 1) * chunk], g
                )

        loop(n // lot, rows)
        low = pl.multiple_of(c * (width // 2), width // 2)
        high = pl.multiple_of((1 - c) * (width // 2), width // 2)
        away[...] = held[pl.ds(high, width // 2), :].astype(bf16)
        cross = remote(away, other, send.at[1], recv.at[1], sibling)
        cross.start()
        back.finish(grads, rows_back, *sems[:3])
        for load in loads:
            load.wait()
        total = None
        for h in range(0, H, 2):
            for i in range(3):
                at = (3 * h + i) * VW
                x = jnp.concatenate(
                    [rows_back[:, at : at + VW], rows_back[:, at + 3 * VW : at + 4 * VW]], axis=1
                )
                new = dot_nt(x, w_all[i, :, h * VW : (h + 2) * VW])
                total = new if total is None else total + new
        normed_grad[...] = total
        cross.wait_recv()
        weight_half[...] = (held[pl.ds(low, width // 2), :] + other[...].astype(f32)).astype(bf16)
        share.finish(branch, branch_all, *sems[6:9])
        ffn.finish(ffn_out, ffn_parts, *sems[3:6])
        swap.wait_send()
        cross.wait_send()

    return pl.pallas_call(
        kernel,
        out_shape=[
            jax.ShapeDtypeStruct((2 * half, width), f32),
            jax.ShapeDtypeStruct((width // 2, 3 * VW), bf16),
            jax.ShapeDtypeStruct(ffn_out.shape, bf16),
            jax.ShapeDtypeStruct((place.tp,) + branch_grad.shape, bf16),
        ],
        in_specs=[VMEM, VMEM, ANY, ANY, VMEM] + [ANY] * 5,
        out_specs=[VMEM, VMEM, ANY, ANY],
        scratch_shapes=[
            pltpu.VMEM((n, half, 2 * VW), bf16),
            pltpu.VMEM((n, half, 3 * VW), bf16),
            pltpu.VMEM((2 * half, 3 * HW), bf16),
            pltpu.VMEM((2, lot, half, width), bf16),
            pltpu.VMEM((width, 3 * VW), f32),
            pltpu.VMEM((width // 2, 3 * VW), bf16),
            pltpu.VMEM((width // 2, 3 * VW), bf16),
            pltpu.VMEM((3,) + weights[0].shape, bf16),
        ]
        + [pltpu.SemaphoreType.DMA((k,)) for k in back.sems + ffn.sems + share.sems + [2, 2, 2, 3]],
        compiler_params=pltpu.CompilerParams(
            collective_id=ident, has_side_effects=True, vmem_limit_bytes=vmem_cap
        ),
        cost_estimate=busy(40),
    )(dq, dkv, dkv_sib, rows_all, gain, *weights, ffn_out, branch_grad)


def query_rows(n):
    return 256 if n <= 64 else 128


def two_maps(rows):
    lane = lax.broadcasted_iota(jnp.int32, rows.shape, 1)
    zero = jnp.zeros_like(rows)
    return jnp.concatenate(
        [jnp.where(lane < HALF, rows, zero), jnp.where(lane < HALF, zero, rows)], axis=0
    )


def fwd_kernel(n, pos, lam, own, sib, gain, mixed, mix, lse, qs, ks, vs, order, score):
    qb = query_rows(n)
    kb_rows = 2 * qb
    c = lax.rem(lax.axis_index("seq"), 2)

    def place_run(run):
        order[pos[run // 2, lax.rem(run, 2) * 64] // 64] = run

    loop(2 * n, place_run)
    lambda_value = lam[0]

    def sort(p):
        run = order[p]
        i, b = run // 2, lax.rem(run, 2)
        b = pl.multiple_of(32 * b, 32)
        mine = own[i, pl.ds(b, 32), :]
        other = sib[i, pl.ds(b, 32), :]
        qs[pl.ds(pl.multiple_of(32 * p, 32), 32), :] = mine[:, :VW] * jnp.asarray(0.125, bf16)
        low = pl.multiple_of(64 * p + 32 * c, 32)
        high = pl.multiple_of(64 * p + 32 * (1 - c), 32)
        ks[pl.ds(low, 32), :] = mine[:, VW : 2 * VW]
        vs[pl.ds(low, 32), :] = mine[:, 2 * VW :]
        ks[pl.ds(high, 32), :] = other[:, :VW]
        vs[pl.ds(high, 32), :] = other[:, VW:]

    loop(2 * n, sort)

    def block(j):
        at = pl.ds(pl.multiple_of(qb * j, qb), qb)
        q2 = two_maps(qs[at, :])

        def scores(kb):
            return dot_nt(q2, ks[pl.ds(pl.multiple_of(kb_rows * kb, kb_rows), kb_rows), :])

        def lanes(top, s):
            for i in range(kb_rows // 128):
                top = jnp.maximum(top, s[:, 128 * i : 128 * i + 128])
            return top

        def first(kb, top):
            s = scores(kb)
            score[:, pl.ds(pl.multiple_of(kb_rows * kb, kb_rows), kb_rows)] = s
            return lanes(top, s)

        top = lax.fori_loop(0, j, first, jnp.full((2 * qb, 128), masked_score, f32))
        s = scores(j)
        row = lax.broadcasted_iota(jnp.int32, s.shape, 0)
        row = lax.rem(row, qb)
        allowed = (
            lax.broadcasted_iota(jnp.int32, s.shape, 1)
            <= 64 * (row // 32) + lax.rem(row, 32) + 32 * c
        )
        s = jnp.where(allowed, s, masked_score)
        score[:, pl.ds(pl.multiple_of(kb_rows * j, kb_rows), kb_rows)] = s
        high = jnp.max(lanes(top, s), axis=1, keepdims=True)
        ones = jnp.ones((kb_rows, VW), bf16)

        def second(kb, acc):
            here = pl.ds(pl.multiple_of(kb_rows * kb, kb_rows), kb_rows)
            weights = jnp.exp(score[:, here] - high).astype(bf16)
            return acc + dot(weights, jnp.concatenate([vs[here, :], ones], axis=1))

        acc = lax.fori_loop(0, j + 1, second, jnp.zeros((2 * qb, 2 * VW), f32))
        total = acc[:, VW:]
        mixes = acc[:, :VW] / total
        lse[j] = jnp.transpose(high + jnp.log(total))[:8, :]
        mix[0, at, :] = mixes[:qb]
        mix[1, at, :] = mixes[qb:]
        out = mixes[:qb] - lambda_value * mixes[qb:]
        out = (out * rms_scale(out) * gain[...]).astype(bf16)
        for i in range(qb // 32):
            run = order[j * (qb // 32) + i]
            b = pl.multiple_of(32 * lax.rem(run, 2), 32)
            mixed[run // 2, pl.ds(b, 32), :] = out[32 * i : 32 * i + 32]

    loop(n * 64 // qb, block)


def attend(place, pos, lam, own, sib, gain):
    n = place.n
    rows = 64 * n
    qb = query_rows(n)
    return pl.pallas_call(
        functools.partial(fwd_kernel, n),
        out_shape=[
            jax.ShapeDtypeStruct((n, 64, VW), bf16),
            jax.ShapeDtypeStruct((2, rows, VW), f32),
            jax.ShapeDtypeStruct((rows // qb, 8, 2 * qb), f32),
            jax.ShapeDtypeStruct((rows, VW), bf16),
            jax.ShapeDtypeStruct((2 * rows, VW), bf16),
            jax.ShapeDtypeStruct((2 * rows, VW), bf16),
            jax.ShapeDtypeStruct((2 * n,), jnp.int32),
        ],
        in_specs=[SMEM, SMEM, VMEM, VMEM, VMEM],
        out_specs=[VMEM] * 6 + [SMEM],
        scratch_shapes=[pltpu.VMEM((2 * qb, 2 * rows), f32)],
        compiler_params=pltpu.CompilerParams(vmem_limit_bytes=vmem_cap),
        cost_estimate=busy(30),
    )(pos, lam, own, sib, gain)


def bwd_kernel(
    n,
    lam,
    grad,
    mix,
    lse,
    qs,
    ks,
    vs,
    order,
    gain,
    dq,
    dkv,
    dkv_sib,
    sums,
    dk,
    dv,
):
    qb = query_rows(n)
    kb_rows = 2 * qb
    c = lax.rem(lax.axis_index("seq"), 2)
    lambda_value = lam[0]
    dk[...] = jnp.zeros_like(dk)
    dv[...] = jnp.zeros_like(dv)
    sums[...] = jnp.zeros_like(sums)

    def block(j):
        at = pl.ds(pl.multiple_of(qb * j, qb), qb)
        pieces = []
        for i in range(qb // 32):
            run = order[j * (qb // 32) + i]
            b = pl.multiple_of(32 * lax.rem(run, 2), 32)
            pieces.append(grad[run // 2, pl.ds(b, 32), :])
        mixed_grad = jnp.concatenate(pieces, axis=0).astype(f32)
        mix_1, mix_2 = mix[0, at, :], mix[1, at, :]
        out = mix_1 - lambda_value * mix_2
        scale = rms_scale(out)
        sums[0:1, :] += jnp.sum(mixed_grad * out * scale, axis=0, keepdims=True) * (
            1.0 - lambda_init
        )
        heads_grad = rms_back(out, scale, gain[...], mixed_grad).astype(bf16)
        grad_f = heads_grad.astype(f32)
        dot_2 = grad_f * mix_2
        sums[1:2, :] += -jnp.sum(dot_2, axis=0, keepdims=True)
        delta_1 = jnp.sum(jnp.transpose(grad_f * mix_1), axis=0, keepdims=True)
        delta_2 = -lambda_value * jnp.sum(jnp.transpose(dot_2), axis=0, keepdims=True)
        q2 = two_maps(qs[at, :])
        lse_now = lse[j][0:1, :]

        def piece(kb, acc, diagonal):
            here = pl.ds(pl.multiple_of(kb_rows * kb, kb_rows), kb_rows)
            keys = ks[here, :]
            s = dot_nt(keys, q2) - lse_now
            if diagonal:
                col = lax.rem(lax.broadcasted_iota(jnp.int32, s.shape, 1), qb)
                allowed = (
                    lax.broadcasted_iota(jnp.int32, s.shape, 0)
                    <= 64 * (col // 32) + lax.rem(col, 32) + 32 * c
                )
                s = jnp.where(allowed, s, masked_score)
            prob = jnp.exp(s)
            prob_1, prob_2 = prob[:, :qb], prob[:, qb:]
            value_dot = dot_nt(vs[here, :], heads_grad)
            grads = jnp.concatenate(
                [
                    (prob_1 * (value_dot - delta_1)).astype(bf16),
                    (prob_2 * (-lambda_value * value_dot - delta_2)).astype(bf16),
                ],
                axis=1,
            )
            dv[here, :] += dot((prob_1 - lambda_value * prob_2).astype(bf16), heads_grad)
            dk[here, :] += dot(grads, q2)
            return acc + dot_tn(grads, keys)

        acc = lax.fori_loop(
            0, j, lambda kb, a: piece(kb, a, False), jnp.zeros((2 * qb, VW), f32)
        )
        acc = piece(j, acc, True)
        lane = lax.broadcasted_iota(jnp.int32, (qb, VW), 1)
        done = (jnp.where(lane < HALF, acc[:qb], acc[qb:]) * 0.125).astype(bf16)
        for i in range(qb // 32):
            run = order[j * (qb // 32) + i]
            b = pl.multiple_of(32 * lax.rem(run, 2), 32)
            dq[run // 2, pl.ds(b, 32), :] = done[32 * i : 32 * i + 32]

    loop(n * 64 // qb, block)

    def unsort(p):
        run = order[p]
        b = pl.multiple_of(32 * lax.rem(run, 2), 32)
        low = pl.multiple_of(64 * p + 32 * c, 32)
        high = pl.multiple_of(64 * p + 32 * (1 - c), 32)
        dkv[run // 2, pl.ds(b, 32), :VW] = dk[pl.ds(low, 32), :]
        dkv[run // 2, pl.ds(b, 32), VW:] = dv[pl.ds(low, 32), :]
        dkv_sib[run // 2, pl.ds(b, 32), :VW] = dk[pl.ds(high, 32), :].astype(bf16)
        dkv_sib[run // 2, pl.ds(b, 32), VW:] = dv[pl.ds(high, 32), :].astype(bf16)

    loop(2 * n, unsort)


def attend_back(place, lam, grad, saved, gain):
    n = place.n
    rows = 64 * n
    qb = query_rows(n)
    return pl.pallas_call(
        functools.partial(bwd_kernel, n),
        out_shape=[
            jax.ShapeDtypeStruct((n, 64, VW), bf16),
            jax.ShapeDtypeStruct((n, 64, 2 * VW), f32),
            jax.ShapeDtypeStruct((n, 64, 2 * VW), bf16),
            jax.ShapeDtypeStruct((8, VW), f32),
        ],
        in_specs=[SMEM] + [VMEM] * 6 + [SMEM, VMEM],
        out_specs=[VMEM] * 4,
        scratch_shapes=[pltpu.VMEM((2 * rows, VW), f32)] * 2,
        compiler_params=pltpu.CompilerParams(vmem_limit_bytes=vmem_cap),
        cost_estimate=busy(35),
    )(lam, grad, *saved, gain)


def swap_halves(rows):
    count, width = rows.shape
    return rows.reshape(2, 2, count // 4, width).transpose(1, 0, 2, 3).reshape(count, width)


def body(
    place,
    inputs,
    positions,
    attn_gain,
    w_query,
    w_key,
    w_value,
    w_out,
    lambda_params,
    sub_gain,
    ffn_gain,
    w_gate,
    w_up,
    w_down,
    cotangent,
):
    n, tp, seq = place.n, place.tp, place.seq
    s, t, core, head, active = place.me()
    inputs, cotangent = swap_halves(inputs), swap_halves(cotangent)
    row_count, width = inputs.shape
    half = row_count // 2
    part = width // n
    inputs_f = inputs.astype(f32)
    attn_scale = rms_scale(inputs_f)
    attn_normed = (inputs_f * attn_scale * attn_gain).astype(bf16)
    rows_all = lax.all_gather(inputs, ("seq", "tp"), axis=0, tiled=False)
    first_exp = jnp.exp(jnp.sum(lambda_params[0] * lambda_params[1]))
    second_exp = jnp.exp(jnp.sum(lambda_params[2] * lambda_params[3]))
    lambda_value = first_exp - second_exp + lambda_init
    lam = lambda_value.reshape(1)

    weights = (w_query, w_key, w_value)
    own, sib, pos, cotangent_all = send_heads(
        place, attn_normed, weights, positions.reshape(1, row_count), cotangent, 1
    )
    cotangent_all = cotangent_all.reshape(tp * row_count, width)
    head_gain = (sub_gain * (1.0 - lambda_init)).reshape(1, VW)
    mixed, *saved = attend(place, pos.reshape(n, row_count), lam, own, sib, head_gain)
    mixed_all = return_heads(place, mixed, 2).reshape(tp * row_count, HW)

    inputs_all = lax.dynamic_slice_in_dim(rows_all, s * tp, tp, 0).reshape(tp * row_count, width)
    middle_all = inputs_all.astype(f32) + dot(mixed_all, w_out)
    scale_all = rms_scale(middle_all)
    ffn_rows = (middle_all * scale_all * ffn_gain).astype(bf16)
    middle = lax.dynamic_slice_in_dim(middle_all, t * row_count, row_count, 0)
    ffn_scale = rms_scale(middle)
    gate_proj = dot(ffn_rows, w_gate)
    up_proj = dot(ffn_rows, w_up)
    gate_sig = jax.nn.sigmoid(gate_proj)
    gate_act = gate_proj * gate_sig
    hidden = (gate_act * up_proj).astype(bf16)
    hidden_grad = dot_nt(cotangent_all, w_down)
    gate_rows_grad = (
        hidden_grad * up_proj * gate_sig * (1.0 + gate_proj * (1.0 - gate_sig))
    ).astype(bf16)
    up_rows_grad = (hidden_grad * gate_act).astype(bf16)
    ffn_partial = dot_nt(gate_rows_grad, w_gate) + dot_nt(up_rows_grad, w_up)
    hidden_width = hidden.shape[1]
    chunk = 256

    def ffn_weights(given, made, rest):
        cot, rows, hid, gate, up = given
        (out,) = made
        held, sem = rest

        def copy(i):
            at = pl.ds(pl.multiple_of(chunk * i, chunk), chunk)
            return pltpu.make_async_copy(held.at[at], out.at[at], sem.at[i])

        def step(i):
            at = pl.ds(pl.multiple_of(chunk * i, chunk), chunk)
            for k, (left, right) in enumerate(((cot, hid), (rows, gate), (rows, up))):
                held[at, k * hidden_width : (k + 1) * hidden_width] = dot_tn(
                    left[:, at], right[...]
                ).astype(bf16)
            copy(i).start()

        loop(width // chunk, step)
        loop(width // chunk, lambda i: copy(i).wait())

    grad_parts, ffn_parts = moves(
        place,
        [Group(place, False)],
        [ffn_partial.astype(bf16).reshape(tp, row_count, width)],
        [(tp, row_count, width)],
        3,
        30,
        work=ffn_weights,
        operands=[
            (a, VMEM) for a in (cotangent_all, ffn_rows, hidden, gate_rows_grad, up_rows_grad)
        ],
        results=[(jax.ShapeDtypeStruct((width, 3 * hidden_width), bf16), ANY)],
        scratch=[
            pltpu.VMEM((width, 3 * hidden_width), bf16),
            pltpu.SemaphoreType.DMA((width // chunk,)),
        ],
    )
    own_partial = lax.dynamic_slice_in_dim(ffn_partial, t * row_count, row_count, 0)
    member = jnp.arange(tp)[:, None, None]
    ffn_in_grad = own_partial + jnp.sum(
        jnp.where(member == t, 0.0, grad_parts.astype(f32)), axis=0
    )
    ffn_gain_part = jnp.sum(ffn_in_grad * middle * ffn_scale, axis=0)
    middle_grad = cotangent.astype(f32) + rms_back(middle, ffn_scale, ffn_gain, ffn_in_grad)
    branch_grad = middle_grad.astype(bf16)

    def scatter_rows(array):
        return lax.psum_scatter(array, "seq", scatter_dimension=0, tiled=True)

    ffn_grads = scatter_rows(ffn_parts)

    mixed_grad = dot_nt(branch_grad, w_out).astype(bf16)

    def head_block(x, h, c):
        return x.at[
            pl.ds(pl.multiple_of(half * c, half), half), pl.ds(pl.multiple_of(VW * h, VW), VW)
        ]

    def ffn_result(given, made, rest):
        hid, weight = given
        (out,) = made
        for i in range(tp):
            out[i] = dot(hid[i * row_count : (i + 1) * row_count, :], weight[...]).astype(bf16)

    grad_heads, ffn_out = moves(
        place,
        [Dispatch(place, head_block)],
        [mixed_grad],
        [(n, half, VW)],
        4,
        20,
        work=ffn_result,
        operands=[(hidden, VMEM), (w_down, VMEM)],
        results=[(jax.ShapeDtypeStruct((tp, row_count, width), bf16), VMEM)],
    )
    dq, dkv, dkv_sib, sums = attend_back(place, lam, grad_heads, saved, head_gain)
    normed_grad, weight_half, out_parts, branch_all = finish_heads(
        place,
        dq,
        dkv,
        dkv_sib,
        rows_all,
        attn_gain.reshape(1, width),
        weights,
        ffn_out,
        branch_grad,
        5,
    )
    out_part = dot_tn(mixed_all, branch_all.reshape(tp * row_count, width)).astype(bf16)
    out_part = lax.dynamic_index_in_dim(
        out_part.reshape(seq, tp, part, width), t, 1, keepdims=False
    ).reshape(seq * part, width)
    out_part, ffn_grads = lax.optimization_barrier((out_part, ffn_grads))

    output = (middle + jnp.sum(out_parts.astype(f32), axis=0)).astype(bf16)
    attn_gain_part = jnp.sum(normed_grad * inputs_f * attn_scale, axis=0)
    input_grad = middle_grad + rms_back(inputs_f, attn_scale, attn_gain, normed_grad)

    sums = jnp.where(active, sums, 0.0)
    pad = ((0, 0), (0, 128 - part))
    small = jnp.stack(
        [
            jnp.pad(attn_gain_part.reshape(n, part), pad),
            jnp.pad(ffn_gain_part.reshape(n, part), pad),
            jnp.broadcast_to(sums[0], (n, VW)),
            jnp.broadcast_to(sums[1], (n, VW)),
        ]
        + [jnp.zeros((n, VW), f32)] * 4,
        axis=1,
    )
    small, out_part = lax.optimization_barrier((small, out_part))
    weight_rows, small_all = moves(
        place,
        [Collect(place, lambda o, t, h, c: o.at[h], True), Everyone(place, False)],
        [weight_half.reshape(n // 2, part, 3 * VW), small],
        [(H, part, 3 * VW), (n, 8, VW)],
        6,
        20,
    )
    out_grad = scatter_rows(out_part).astype(f32)
    ffn_grads = ffn_grads.astype(f32)
    down_grad = ffn_grads[:, :hidden_width].T
    gate_grad = ffn_grads[:, hidden_width : 2 * hidden_width]
    up_grad = ffn_grads[:, 2 * hidden_width :]
    weight_rows = weight_rows.astype(f32).reshape(H, part, 3, VW).transpose(2, 1, 0, 3)
    weight_rows = weight_rows.reshape(3, part, HW)
    small_sum = jnp.sum(small_all, axis=0)
    lambda_total = jnp.sum(small_sum[3])
    lambda_grads = jnp.stack(
        [
            lambda_total * first_exp * lambda_params[1],
            lambda_total * first_exp * lambda_params[0],
            -lambda_total * second_exp * lambda_params[3],
            -lambda_total * second_exp * lambda_params[2],
        ]
    )
    lambda_norm = jnp.sqrt(jnp.sum(lambda_grads * lambda_grads))
    output, input_grad = swap_halves(output), swap_halves(input_grad)
    return (
        output,
        input_grad,
        small_sum[0, :part],
        weight_rows[0],
        weight_rows[1],
        weight_rows[2],
        out_grad,
        lambda_grads,
        small_sum[2],
        small_sum[1, :part],
        gate_grad,
        up_grad,
        down_grad,
        lambda_total,
        lambda_norm,
    )


def solution(mesh):
    place = Place(mesh.shape["seq"], mesh.shape["tp"])
    both = ("seq", "tp")
    placed = (
        P(both, None),
        P(both),
        P(),
        P(),
        P(),
        P(),
        P(),
        P(),
        P(),
        P(),
        P(None, "tp"),
        P(None, "tp"),
        P("tp", None),
        P(both, None),
    )
    return jax.shard_map(
        functools.partial(body, place),
        mesh=mesh,
        in_specs=placed,
        out_specs=(
            P(both, None),
            P(both, None),
            P(both),
            P(both, None),
            P(both, None),
            P(both, None),
            P(both, None),
            P(),
            P(),
            P(both),
            P("seq", "tp"),
            P("seq", "tp"),
            P("tp", "seq"),
            P(),
            P(),
        ),
        check_vma=False,
    )
```

```python
import functools
import math

import jax
import jax.numpy as jnp
from jax import lax
from jax.experimental import pallas as pl
from jax.experimental.pallas import tpu as pltpu
from jax.sharding import PartitionSpec as P

H = 12
HALF = 64
VW = 128
HW = 1536

eps = 1e-05
lambda_init = 0.8 - 0.6 * math.exp(-3.3)
masked_score = -1e30
MESH = pl.DeviceIdType.MESH
ANY = pl.BlockSpec(memory_space=pl.ANY)
VMEM = pl.BlockSpec(memory_space=pltpu.VMEM)
SMEM = pl.BlockSpec(memory_space=pltpu.SMEM)
bf16 = jnp.bfloat16
f32 = jnp.float32
vmem_cap = 60 * 1024 * 1024


def dot(left, right):
    return jnp.dot(left, right, preferred_element_type=f32)


def dot_tn(left, right):
    return lax.dot_general(left, right, (((0,), (0,)), ((), ())), preferred_element_type=f32)


def dot_nt(left, right):
    return lax.dot_general(left, right, (((1,), (1,)), ((), ())), preferred_element_type=f32)


def rms_scale(values):
    return lax.rsqrt(jnp.mean(values * values, axis=-1, keepdims=True) + eps)


def rms_back(values, inv_rms, gain_vec, upstream):
    weighted = upstream * gain_vec
    inner_mean = jnp.mean(weighted * values, axis=-1, keepdims=True)
    return inv_rms * weighted - values * (inv_rms * inv_rms * inv_rms) * inner_mean


class Place:
    def __init__(self, seq, tp):
        self.seq, self.tp, self.n = seq, tp, seq * tp
        self.per = -(-H // (seq // 2))
        assert self.per <= tp and seq % 2 == 0

    def me(self):
        s, t = lax.axis_index("seq"), lax.axis_index("tp")
        head = (s // 2) * self.per + t
        active = jnp.logical_and(t < self.per, head < H)
        return s, t, lax.rem(s, 2), head, active

    def head_device(self, index):
        head, core = index // 2, lax.rem(index, 2)
        return 2 * (head // self.per) + core, lax.rem(head, self.per)

    def device(self, linear):
        return linear // self.tp, lax.rem(linear, self.tp)


def busy(microseconds):
    return pl.CostEstimate(
        flops=int(microseconds * 1e9), bytes_accessed=int(microseconds * 3e6), transcendentals=0
    )


def remote(src, dst, send, recv, where):
    return pltpu.make_async_remote_copy(
        src_ref=src, dst_ref=dst, send_sem=send, recv_sem=recv, device_id=where, device_id_type=MESH
    )


def loop(count, step):
    def one(k, carry):
        step(k)
        return carry

    lax.fori_loop(0, count, one, 0)


class Dispatch:
    def __init__(self, place, cut):
        self.p, self.cut = place, cut
        self.sems = [2 * H, place.n, 1]

    def start_one(self, index, x, o, send, recv, here):
        p = self.p
        s, t, c, head, active = p.me()
        lin = s * p.tp + t
        ds, dt = p.head_device(index)
        mine = jnp.logical_and(ds == s, dt == t)
        source = self.cut(x, index // 2, lax.rem(index, 2))

        @pl.when(jnp.logical_not(mine))
        def _():
            remote(source, o.at[lin], send.at[index], recv.at[lin], (ds, dt)).start()

        @pl.when(mine)
        def _():
            pltpu.make_async_copy(source, o.at[lin], here.at[0]).start()

    def start(self, *refs):
        p = self.p
        lin = lax.axis_index("seq") * p.tp + lax.axis_index("tp")
        loop(2 * H, lambda k: self.start_one(lax.rem(k + lin, 2 * H), *refs))

    def finish(self, x, o, send, recv, here, arrived=None):
        p = self.p
        s, t, c, head, active = p.me()
        lin = s * p.tp + t

        @pl.when(active)
        def _():
            pltpu.make_async_copy(self.cut(x, head, c), o.at[lin], here.at[0]).wait()
            if arrived is not None:
                arrived(lin)

            def got(k):
                other = lax.rem(lin + 1 + k, p.n)
                remote(o.at[other], o.at[other], send.at[0], recv.at[other], (s, t)).wait_recv()
                if arrived is not None:
                    arrived(other)

            loop(p.n - 1, got)

        def sent(k):
            ds, dt = p.head_device(k)

            @pl.when(jnp.logical_not(jnp.logical_and(ds == s, dt == t)))
            def _():
                remote(
                    self.cut(x, k // 2, lax.rem(k, 2)), o.at[0], send.at[k], recv.at[0], (ds, dt)
                ).wait_send()

        loop(2 * H, sent)


class Collect:
    def __init__(self, place, into, halves=False):
        self.p, self.into, self.halves = place, into, halves
        self.sems = [place.n, 2 * H, 1]

    def start(self, x, o, send, recv, here):
        p = self.p
        s, t, c, head, active = p.me()
        lin = s * p.tp + t
        count = p.n // 2 if self.halves else p.n

        @pl.when(active)
        def _():
            def step(k):
                slot = lax.rem(k + lin, count)
                other = slot + c * count if self.halves else slot
                into = self.into(o, lax.rem(other, p.tp), head, c)

                @pl.when(other != lin)
                def _():
                    remote(
                        x.at[slot], into, send.at[slot], recv.at[head * 2 + c], p.device(other)
                    ).start()

                @pl.when(other == lin)
                def _():
                    pltpu.make_async_copy(x.at[slot], into, here.at[0]).start()

            loop(count, step)

    def got(self, index, x, o, send, recv, here):
        p = self.p
        s, t = lax.axis_index("seq"), lax.axis_index("tp")
        into = self.into(o, t, index // 2, lax.rem(index, 2))
        ds, dt = p.head_device(index)
        mine = jnp.logical_and(ds == s, dt == t)

        @pl.when(jnp.logical_not(mine))
        def _():
            remote(into, into, send.at[0], recv.at[index], (s, t)).wait_recv()

        @pl.when(mine)
        def _():
            pltpu.make_async_copy(x.at[0], into, here.at[0]).wait()

    def sent(self, x, o, send, recv, here):
        p = self.p
        s, t, c, head, active = p.me()
        lin = s * p.tp + t
        count = p.n // 2 if self.halves else p.n

        @pl.when(active)
        def _():
            def one(k):
                other = k + c * count if self.halves else k

                @pl.when(other != lin)
                def _():
                    remote(
                        x.at[k], x.at[k], send.at[k], recv.at[0], p.device(other)
                    ).wait_send()

            loop(count, one)

    def finish(self, *refs):
        p = self.p
        if self.halves:
            lin = lax.axis_index("seq") * p.tp + lax.axis_index("tp")
            half = lin // (p.n // 2)
            loop(H, lambda k: self.got(2 * k + half, *refs))
        else:
            loop(2 * H, lambda k: self.got(k, *refs))
        self.sent(*refs)


class Everyone:
    def __init__(self, place, whole):
        self.p, self.whole = place, whole
        self.sems = [place.n, place.n, 1]

    def start(self, x, o, send, recv, here):
        p = self.p
        s, t = lax.axis_index("seq"), lax.axis_index("tp")
        lin = s * p.tp + t
        pltpu.make_async_copy(x if self.whole else x.at[lin], o.at[lin], here.at[0]).start()

        def step(k):
            other = lax.rem(lin + 1 + k, p.n)
            remote(
                x if self.whole else x.at[other],
                o.at[lin],
                send.at[other],
                recv.at[lin],
                p.device(other),
            ).start()

        loop(p.n - 1, step)

    def finish(self, x, o, send, recv, here):
        p = self.p
        s, t = lax.axis_index("seq"), lax.axis_index("tp")
        lin = s * p.tp + t
        pltpu.make_async_copy(x if self.whole else x.at[lin], o.at[lin], here.at[0]).wait()

        def done(k):
            other = lax.rem(lin + 1 + k, p.n)
            both = remote(
                x if self.whole else x.at[other],
                o.at[other],
                send.at[other],
                recv.at[other],
                p.device(other),
            )
            both.wait_recv()
            both.wait_send()

        loop(p.n - 1, done)


class Group:
    def __init__(self, place, whole):
        self.p, self.whole = place, whole
        self.sems = [place.tp, place.tp, 1]

    def start(self, x, o, send, recv, here):
        p = self.p
        s, t = lax.axis_index("seq"), lax.axis_index("tp")
        pltpu.make_async_copy(x if self.whole else x.at[t], o.at[t], here.at[0]).start()
        for k in range(1, p.tp):
            other = lax.rem(t + k, p.tp)
            remote(
                x if self.whole else x.at[other], o.at[t], send.at[other], recv.at[t], (s, other)
            ).start()

    def finish(self, x, o, send, recv, here):
        p = self.p
        s, t = lax.axis_index("seq"), lax.axis_index("tp")
        pltpu.make_async_copy(x if self.whole else x.at[t], o.at[t], here.at[0]).wait()
        for k in range(1, p.tp):
            other = lax.rem(t + k, p.tp)
            both = remote(
                x if self.whole else x.at[other],
                o.at[other],
                send.at[other],
                recv.at[other],
                (s, other),
            )
            both.wait_recv()
            both.wait_send()


def greet(place):
    s, t = lax.axis_index("seq"), lax.axis_index("tp")
    lin = s * place.tp + t
    barrier = pltpu.get_barrier_semaphore()

    def hello(k):
        pl.semaphore_signal(
            barrier,
            inc=1,
            device_id=place.device(lax.rem(lin + 1 + k, place.n)),
            device_id_type=MESH,
        )

    loop(place.n - 1, hello)
    pl.semaphore_wait(barrier, place.n - 1)


def moves(place, parts, arrays, outs, ident, cost, work=None, operands=(), results=(), scratch=()):
    count, extra = len(parts), len(operands)

    def kernel(*refs):
        ins, given = refs[:count], refs[count : count + extra]
        refs = refs[count + extra :]
        into, made = refs[:count], refs[count : count + len(results)]
        refs = refs[count + len(results) :]
        sems, rest = refs[: 3 * count], refs[3 * count :]
        greet(place)
        for i, part in enumerate(parts):
            part.start(ins[i], into[i], *sems[3 * i : 3 * i + 3])
        if work is not None:
            work(given, made, rest)
        for i, part in enumerate(parts):
            part.finish(ins[i], into[i], *sems[3 * i : 3 * i + 3])

    return pl.pallas_call(
        kernel,
        out_shape=[jax.ShapeDtypeStruct(s, a.dtype) for s, a in zip(outs, arrays)]
        + [shape for shape, spec in results],
        in_specs=[ANY] * count + [spec for array, spec in operands],
        out_specs=[ANY] * count + [spec for shape, spec in results],
        scratch_shapes=[pltpu.SemaphoreType.DMA((k,)) for part in parts for k in part.sems]
        + list(scratch),
        compiler_params=pltpu.CompilerParams(
            collective_id=ident, has_side_effects=True, vmem_limit_bytes=vmem_cap
        ),
        cost_estimate=busy(cost),
    )(*arrays, *[array for array, spec in operands])


def gather_all(place, rows, run_pos, gain, weights, ident):
    n, tp, depth = place.n, place.tp, place.seq // 2
    count, width = rows.shape
    half = count // 2
    tell = Everyone(place, True)

    def relay(first, use, x, o, full, halves, z_up, z_down, by_x, by_y, half_x, half_y, across, here):
        s, t = lax.axis_index("seq"), lax.axis_index("tp")
        z, c = s // 2, lax.rem(s, 2)
        t_x = t + 1 - 2 * lax.rem(t, 2)
        t_y = lax.rem(t + 2, 4)
        t_d = t_x + 2 - 4 * (t_x // 2)

        def slot(zs, core, ts):
            return (2 * zs + core) * tp + ts

        def line(zs, source, step):
            at = slot(zs, c, t)
            sem = z_up if step > 0 else z_down
            return remote(source, o.at[at], sem.at[zs], full.at[at], (s + 2 * step, t))

        def side(zs, source, sem, ts):
            at = slot(zs, c, t)
            return remote(source, o.at[at], sem.at[zs], full.at[at], (s, ts))

        def other_core(zs, ts, source):
            at = slot(zs, c, ts)
            return remote(
                source, o.at[at], across.at[zs * tp + ts], full.at[at], (s + 1 - 2 * c, t)
            )

        def corner(zs, ts, low, sem, to):
            at = slot(zs, c, ts)
            part = o.at[at, low : low + half]
            return remote(
                part, part, sem.at[zs], halves.at[2 * at + low // half], (s, to)
            )

        def arrived(at):
            remote(o.at[at], o.at[at], here.at[0], full.at[at], (s, t)).wait_recv()

        def push(zs, source):
            @pl.when(jnp.logical_and(zs <= z, z < depth - 1))
            def _():
                line(zs, source, 1).start()

            @pl.when(jnp.logical_and(zs >= z, z > 0))
            def _():
                line(zs, source, -1).start()

            side(zs, source, by_x, t_x).start()
            side(zs, source, by_y, t_y).start()
            other_core(zs, t, source).start()

        def each(k, act):
            def one(sign):
                zs = z + (2 * sign - 1) * k
                valid = jnp.logical_and(zs >= 0, zs < depth)
                valid = jnp.logical_and(valid, jnp.logical_and(k >= 0, k + 1 > sign))

                @pl.when(valid)
                def _():
                    act(zs)

            loop(2, one)

        def from_line(zs):
            arrived(slot(zs, c, t))
            push(zs, o.at[slot(zs, c, t)])

        def from_sides(zs):
            arrived(slot(zs, c, t_x))
            corner(zs, t_x, 0, half_y, t_y).start()
            other_core(zs, t_x, o.at[slot(zs, c, t_x)]).start()
            arrived(slot(zs, c, t_y))
            corner(zs, t_y, half, half_x, t_x).start()
            other_core(zs, t_y, o.at[slot(zs, c, t_y)]).start()

        def from_corner(zs):
            at = slot(zs, c, t_d)
            for low in (0, half):
                part = o.at[at, low : low + half]
                remote(
                    part, part, here.at[0], halves.at[2 * at + low // half], (s, t)
                ).wait_recv()
            other_core(zs, t_d, o.at[at]).start()

        keep = pltpu.make_async_copy(x, o.at[slot(z, c, t)], here.at[0])
        keep.start()
        push(z, x)
        first()
        keep.wait()

        def use_block(k):
            def one(i):
                other, v = i // 4, lax.rem(i, 4)
                m_x, m_y = lax.rem(v, 2), v // 2
                x_bit, y_bit = lax.rem(t, 2), t // 2
                ts = 2 * (y_bit + m_y - 2 * y_bit * m_y) + x_bit + m_x - 2 * x_bit * m_x
                core = c + other - 2 * c * other

                def act(zs):
                    at = slot(zs, core, ts)

                    @pl.when(other > 0)
                    def _():
                        arrived(at)

                    use(at)

                each(k - m_x - m_y - other, act)

            loop(8, one)

        def wave(k):
            @pl.when(k > 0)
            def _():
                each(k, from_line)
                each(k - 1, from_sides)
                each(k - 2, from_corner)

            use_block(k)

        loop(depth + 3, wave)

        def sent(k):
            zs = k
            at = slot(zs, c, t)

            @pl.when(jnp.logical_and(zs <= z, z < depth - 1))
            def _():
                line(zs, o.at[at], 1).wait_send()

            @pl.when(jnp.logical_and(zs >= z, z > 0))
            def _():
                line(zs, o.at[at], -1).wait_send()

            side(zs, o.at[at], by_x, t_x).wait_send()
            side(zs, o.at[at], by_y, t_y).wait_send()
            corner(zs, t_x, 0, half_y, t_y).wait_send()
            corner(zs, t_y, half, half_x, t_x).wait_send()
            for ts in range(tp):
                other_core(zs, ts, o.at[at]).wait_send()

        loop(depth, sent)

    sems = [n, 2 * n] + [depth] * 6 + [depth * tp, 1]

    def kernel(x, r, gain, wq, wk, wv, out, pos, qkv, o, out_sem, *refs):
        greet(place)

        def save(at):
            return pltpu.make_async_copy(o.at[at], out.at[at], out_sem.at[at])

        def use(at):
            save(at).start()
            x = o[at].astype(f32)
            x = (x * rms_scale(x) * gain[...]).astype(bf16)
            for i, w in enumerate((wq, wk, wv)):
                qkv[at, :, i * VW : (i + 1) * VW] = dot(x, w[...]).astype(bf16)

        relay(lambda: tell.start(r, pos, *refs[:3]), use, x, o, *refs[3:])
        tell.finish(r, pos, *refs[:3])
        loop(n, lambda k: save(k).wait())

    def column(g):
        s, t, c, head, active = place.me()
        return 0, jnp.minimum(head, H - 1)

    columns = pl.BlockSpec((width, VW), column)
    return pl.pallas_call(
        kernel,
        grid=(1,),
        out_shape=[
            jax.ShapeDtypeStruct((n,) + rows.shape, rows.dtype),
            jax.ShapeDtypeStruct((n,) + run_pos.shape, run_pos.dtype),
            jax.ShapeDtypeStruct((n, count, 3 * VW), bf16),
        ],
        in_specs=[ANY] * 2 + [VMEM] + [columns] * 3,
        out_specs=[ANY] * 2 + [VMEM],
        scratch_shapes=[
            pltpu.VMEM((n,) + rows.shape, rows.dtype),
            pltpu.SemaphoreType.DMA((n,)),
        ]
        + [pltpu.SemaphoreType.DMA((k,)) for k in tell.sems + sems],
        compiler_params=pltpu.CompilerParams(
            collective_id=ident, has_side_effects=True, vmem_limit_bytes=vmem_cap
        ),
        cost_estimate=busy(50),
    )(rows, run_pos, gain, *weights)


def gather_all_plain(place, rows, run_pos, gain, weights):
    axes = ("seq", "tp")
    rows_all = lax.all_gather(rows, axes, axis=0, tiled=False)
    pos = lax.all_gather(run_pos, axes, axis=0, tiled=False)
    x = rows_all.astype(f32)
    x = (x * rms_scale(x) * gain).astype(bf16)
    s, t, c, head, active = place.me()
    column = jnp.minimum(head, H - 1) * VW
    qkv = [
        dot(x, lax.dynamic_slice_in_dim(w, column, VW, 1)).astype(bf16) for w in weights
    ]
    return rows_all, pos, jnp.concatenate(qkv, axis=2)


def return_heads(place, mixed, ident):
    n, rows = place.n, mixed.shape[1]

    def into(o, t, h, c):
        return o.at[
            t,
            pl.ds(pl.multiple_of(rows * c, rows), rows),
            pl.ds(pl.multiple_of(VW * h, VW), VW),
        ]

    back = Collect(place, into)

    def kernel(x, o, *sems):
        s, t = lax.axis_index("seq"), lax.axis_index("tp")
        greet(place)
        back.start(x, o, *sems[:3])
        send, recv = sems[3], sems[4]

        def share(k, c, slot):
            other = lax.rem(t + k, place.tp)
            return remote(
                o.at[t, rows * c : rows * c + rows, :],
                o.at[slot(other), rows * c : rows * c + rows, :],
                send.at[2 * other + c],
                recv.at[2 * slot(other) + c],
                (s, other),
            )

        for c in range(2):
            loop(H, lambda h: back.got(2 * h + c, x, o, *sems[:3]))
            for k in range(1, place.tp):
                share(k, c, lambda other: t).start()
        for c in range(2):
            for k in range(1, place.tp):
                both = share(k, c, lambda other: other)
                both.wait_recv()
                both.wait_send()
        back.sent(x, o, *sems[:3])

    return pl.pallas_call(
        kernel,
        out_shape=jax.ShapeDtypeStruct((place.tp, 2 * rows, HW), mixed.dtype),
        in_specs=[ANY],
        out_specs=ANY,
        scratch_shapes=[
            pltpu.SemaphoreType.DMA((k,)) for k in back.sems + [2 * place.tp, 2 * place.tp]
        ],
        compiler_params=pltpu.CompilerParams(collective_id=ident, has_side_effects=True),
        cost_estimate=busy(35),
    )(mixed)


def finish_heads(
    place, dq, dkv, dkv_sib, rows_all, gain, weights, branch_grad, ident
):
    n, half = place.n, dq.shape[1]
    width = rows_all.shape[2]
    part, chunk, lot = width // n, 256, 8

    def into(o, t, h, c):
        return o.at[
            pl.ds(pl.multiple_of(half * c, half), half),
            pl.ds(pl.multiple_of(3 * VW * h, 3 * VW), 3 * VW),
        ]

    back, share = Collect(place, into), Group(place, True)

    def kernel(*refs):
        dq, dkv, dkv_sib, rows_all, gain, *refs = refs
        weights, refs = refs[:3], refs[3:]
        branch, normed_grad, weight_half, branch_all, *refs = refs
        other_dkv, grads, rows_back, raw, held, away, other, w_all, *sems = refs
        s, t = lax.axis_index("seq"), lax.axis_index("tp")
        c = lax.rem(s, 2)
        send, recv, raw_sem, w_sem = sems[6:]
        sibling = (s + 1 - 2 * c, t)
        greet(place)
        swap = remote(dkv_sib, other_dkv, send.at[0], recv.at[0], sibling)
        swap.start()

        def fetch(i):
            return pltpu.make_async_copy(
                rows_all.at[
                    pl.ds(lot * i, lot), pl.ds(pl.multiple_of(half * c, half), half), :
                ],
                raw.at[lax.rem(i, 2)],
                raw_sem.at[lax.rem(i, 2)],
            )

        fetch(0).start()
        loads = [
            pltpu.make_async_copy(w, w_all.at[i], w_sem.at[i]) for i, w in enumerate(weights)
        ]
        for load in loads:
            load.start()
        swap.wait_recv()

        def join(i):
            grads[i, :, :VW] = dq[i]
            grads[i, :, VW:] = (dkv[i] + other_dkv[i].astype(f32)).astype(bf16)

        loop(n, join)
        back.start(grads, rows_back, *sems[:3])
        share.start(branch, branch_all, *sems[3:6])
        held[...] = jnp.zeros_like(held)

        def rows(i):
            @pl.when(i + 1 < n // lot)
            def _():
                fetch(i + 1).start()

            fetch(i).wait()
            x = raw[lax.rem(i, 2)].reshape(lot * half, width).astype(f32)
            x = (x * rms_scale(x) * gain[...]).astype(bf16)
            g = grads[pl.ds(lot * i, lot)].reshape(lot * half, 3 * VW)
            for k in range(width // chunk):
                held[k * chunk : (k + 1) * chunk, :] += dot_tn(
                    x[:, k * chunk : (k + 1) * chunk], g
                )

        loop(n // lot, rows)
        low = pl.multiple_of(c * (width // 2), width // 2)
        high = pl.multiple_of((1 - c) * (width // 2), width // 2)
        away[...] = held[pl.ds(high, width // 2), :].astype(bf16)
        cross = remote(away, other, send.at[1], recv.at[1], sibling)
        cross.start()
        back.finish(grads, rows_back, *sems[:3])
        for load in loads:
            load.wait()
        total = None
        for h in range(0, H, 2):
            for i in range(3):
                at = (3 * h + i) * VW
                x = jnp.concatenate(
                    [rows_back[:, at : at + VW], rows_back[:, at + 3 * VW : at + 4 * VW]], axis=1
                )
                new = dot_nt(x, w_all[i, :, h * VW : (h + 2) * VW])
                total = new if total is None else total + new
        normed_grad[...] = total
        cross.wait_recv()
        weight_half[...] = (held[pl.ds(low, width // 2), :] + other[...].astype(f32)).astype(bf16)
        share.finish(branch, branch_all, *sems[3:6])
        swap.wait_send()
        cross.wait_send()

    return pl.pallas_call(
        kernel,
        out_shape=[
            jax.ShapeDtypeStruct((2 * half, width), f32),
            jax.ShapeDtypeStruct((width // 2, 3 * VW), bf16),
            jax.ShapeDtypeStruct((place.tp,) + branch_grad.shape, bf16),
        ],
        in_specs=[VMEM, VMEM, ANY, ANY, VMEM] + [ANY] * 4,
        out_specs=[VMEM, VMEM, ANY],
        scratch_shapes=[
            pltpu.VMEM((n, half, 2 * VW), bf16),
            pltpu.VMEM((n, half, 3 * VW), bf16),
            pltpu.VMEM((2 * half, 3 * HW), bf16),
            pltpu.VMEM((2, lot, half, width), bf16),
            pltpu.VMEM((width, 3 * VW), f32),
            pltpu.VMEM((width // 2, 3 * VW), bf16),
            pltpu.VMEM((width // 2, 3 * VW), bf16),
            pltpu.VMEM((3,) + weights[0].shape, bf16),
        ]
        + [pltpu.SemaphoreType.DMA((k,)) for k in back.sems + share.sems + [2, 2, 2, 3]],
        compiler_params=pltpu.CompilerParams(
            collective_id=ident, has_side_effects=True, vmem_limit_bytes=vmem_cap
        ),
        cost_estimate=busy(40),
    )(dq, dkv, dkv_sib, rows_all, gain, *weights, branch_grad)


def spans(n, count, step):
    if n <= 32:
        for j in range(count):
            step(j)
    else:
        loop(count, step)


def fold(n, count, step, carry):
    if n <= 32:
        for k in range(count):
            carry = step(k, carry)
        return carry
    return lax.fori_loop(0, count, step, carry)


def aligned(value, unit):
    return value if isinstance(value, int) else pl.multiple_of(value, unit)


def query_rows(n):
    return 256 if n <= 64 else 128


def two_maps(rows):
    lane = lax.broadcasted_iota(jnp.int32, rows.shape, 1)
    zero = jnp.zeros_like(rows)
    return jnp.concatenate(
        [jnp.where(lane < HALF, rows, zero), jnp.where(lane < HALF, zero, rows)], axis=0
    )


def fwd_kernel(n, pos, lam, qkv, gain, mixed, mix, lse, qs, ks, vs, order, score):
    qb = query_rows(n)
    kb_rows = 2 * qb
    c = lax.rem(lax.axis_index("seq"), 2)

    def place_run(run):
        order[pos[run // 2, lax.rem(run, 2) * 64] // 64] = run

    loop(2 * n, place_run)
    lambda_value = lam[0]

    def sort(p):
        run = order[p]
        i, b = run // 2, pl.multiple_of(32 * lax.rem(run, 2), 32)
        for h in range(2):
            at = pl.ds(pl.multiple_of(64 * p + 32 * h, 32), 32)
            rows = pl.ds(pl.multiple_of(64 * h + b, 32), 32)
            ks[at, :] = qkv[i, rows, VW : 2 * VW]
            vs[at, :] = qkv[i, rows, 2 * VW :]
        mine = qkv[i, pl.ds(pl.multiple_of(64 * c + b, 32), 32), :VW]
        qs[pl.ds(pl.multiple_of(32 * p, 32), 32), :] = mine * jnp.asarray(0.125, bf16)

    loop(2 * n, sort)

    def block(j):
        at = pl.ds(aligned(qb * j, qb), qb)
        q2 = two_maps(qs[at, :])

        def scores(kb):
            return dot_nt(q2, ks[pl.ds(aligned(kb_rows * kb, kb_rows), kb_rows), :])

        def lanes(top, s):
            for i in range(kb_rows // 128):
                top = jnp.maximum(top, s[:, 128 * i : 128 * i + 128])
            return top

        def first(kb, top):
            s = scores(kb)
            score[:, pl.ds(aligned(kb_rows * kb, kb_rows), kb_rows)] = s
            return lanes(top, s)

        top = fold(n, j, first, jnp.full((2 * qb, 128), masked_score, f32))
        s = scores(j)
        row = lax.broadcasted_iota(jnp.int32, s.shape, 0)
        row = lax.rem(row, qb)
        allowed = (
            lax.broadcasted_iota(jnp.int32, s.shape, 1)
            <= 64 * (row // 32) + lax.rem(row, 32) + 32 * c
        )
        s = jnp.where(allowed, s, masked_score)
        score[:, pl.ds(aligned(kb_rows * j, kb_rows), kb_rows)] = s
        high = jnp.max(lanes(top, s), axis=1, keepdims=True)
        ones = jnp.ones((kb_rows, VW), bf16)

        def second(kb, acc):
            here = pl.ds(aligned(kb_rows * kb, kb_rows), kb_rows)
            weights = jnp.exp(score[:, here] - high).astype(bf16)
            return acc + dot(weights, jnp.concatenate([vs[here, :], ones], axis=1))

        acc = fold(n, j + 1, second, jnp.zeros((2 * qb, 2 * VW), f32))
        total = acc[:, VW:]
        mixes = acc[:, :VW] / total
        lse[j] = jnp.transpose(high + jnp.log(total))[:8, :]
        mix[0, at, :] = mixes[:qb]
        mix[1, at, :] = mixes[qb:]
        out = mixes[:qb] - lambda_value * mixes[qb:]
        out = (out * rms_scale(out) * gain[...]).astype(bf16)
        for i in range(qb // 32):
            run = order[j * (qb // 32) + i]
            b = pl.multiple_of(32 * lax.rem(run, 2), 32)
            mixed[run // 2, pl.ds(b, 32), :] = out[32 * i : 32 * i + 32]

    spans(n, n * 64 // qb, block)


def attend(place, pos, lam, qkv, gain):
    n = place.n
    rows = 64 * n
    qb = query_rows(n)
    return pl.pallas_call(
        functools.partial(fwd_kernel, n),
        out_shape=[
            jax.ShapeDtypeStruct((n, 64, VW), bf16),
            jax.ShapeDtypeStruct((2, rows, VW), f32),
            jax.ShapeDtypeStruct((rows // qb, 8, 2 * qb), f32),
            jax.ShapeDtypeStruct((rows, VW), bf16),
            jax.ShapeDtypeStruct((2 * rows, VW), bf16),
            jax.ShapeDtypeStruct((2 * rows, VW), bf16),
            jax.ShapeDtypeStruct((2 * n,), jnp.int32),
        ],
        in_specs=[SMEM, SMEM, VMEM, VMEM],
        out_specs=[VMEM] * 6 + [SMEM],
        scratch_shapes=[pltpu.VMEM((2 * qb, 2 * rows), f32)],
        compiler_params=pltpu.CompilerParams(vmem_limit_bytes=vmem_cap),
        cost_estimate=busy(20),
    )(pos, lam, qkv, gain)


def bwd_kernel(
    n,
    lam,
    grad,
    mix,
    lse,
    qs,
    ks,
    vs,
    order,
    gain,
    dq,
    dkv,
    dkv_sib,
    sums,
    dk,
    dv,
):
    qb = query_rows(n)
    kb_rows = 2 * qb
    c = lax.rem(lax.axis_index("seq"), 2)
    lambda_value = lam[0]
    dk[...] = jnp.zeros_like(dk)
    dv[...] = jnp.zeros_like(dv)
    sums[...] = jnp.zeros_like(sums)

    def block(j):
        at = pl.ds(aligned(qb * j, qb), qb)
        pieces = []
        for i in range(qb // 32):
            run = order[j * (qb // 32) + i]
            b = pl.multiple_of(32 * lax.rem(run, 2), 32)
            pieces.append(grad[run // 2, pl.ds(b, 32), :])
        mixed_grad = jnp.concatenate(pieces, axis=0).astype(f32)
        mix_1, mix_2 = mix[0, at, :], mix[1, at, :]
        out = mix_1 - lambda_value * mix_2
        scale = rms_scale(out)
        sums[0:1, :] += jnp.sum(mixed_grad * out * scale, axis=0, keepdims=True) * (
            1.0 - lambda_init
        )
        heads_grad = rms_back(out, scale, gain[...], mixed_grad).astype(bf16)
        grad_f = heads_grad.astype(f32)
        dot_2 = grad_f * mix_2
        sums[1:2, :] += -jnp.sum(dot_2, axis=0, keepdims=True)
        delta_1 = jnp.sum(jnp.transpose(grad_f * mix_1), axis=0, keepdims=True)
        delta_2 = -lambda_value * jnp.sum(jnp.transpose(dot_2), axis=0, keepdims=True)
        q2 = two_maps(qs[at, :])
        lse_now = lse[j][0:1, :]
        q2_t = jnp.transpose(q2)
        grad_t = jnp.transpose(heads_grad)

        def piece(kb, acc, diagonal):
            here = pl.ds(aligned(kb_rows * kb, kb_rows), kb_rows)
            keys = ks[here, :]
            s = dot(keys, q2_t) - lse_now
            if diagonal:
                col = lax.rem(lax.broadcasted_iota(jnp.int32, s.shape, 1), qb)
                allowed = (
                    lax.broadcasted_iota(jnp.int32, s.shape, 0)
                    <= 64 * (col // 32) + lax.rem(col, 32) + 32 * c
                )
                s = jnp.where(allowed, s, masked_score)
            prob = jnp.exp(s)
            prob_1, prob_2 = prob[:, :qb], prob[:, qb:]
            value_dot = dot(vs[here, :], grad_t)
            grads = jnp.concatenate(
                [
                    (prob_1 * (value_dot - delta_1)).astype(bf16),
                    (prob_2 * (-lambda_value * value_dot - delta_2)).astype(bf16),
                ],
                axis=1,
            )
            dv[here, :] += dot((prob_1 - lambda_value * prob_2).astype(bf16), heads_grad)
            dk[here, :] += dot(grads, q2)
            return acc + dot_tn(keys, grads)

        acc = fold(
            n, j, lambda kb, a: piece(kb, a, False), jnp.zeros((VW, 2 * qb), f32)
        )
        acc = jnp.transpose(piece(j, acc, True))
        lane = lax.broadcasted_iota(jnp.int32, (qb, VW), 1)
        done = (jnp.where(lane < HALF, acc[:qb], acc[qb:]) * 0.125).astype(bf16)
        for i in range(qb // 32):
            run = order[j * (qb // 32) + i]
            b = pl.multiple_of(32 * lax.rem(run, 2), 32)
            dq[run // 2, pl.ds(b, 32), :] = done[32 * i : 32 * i + 32]

    spans(n, n * 64 // qb, block)

    def unsort(p):
        run = order[p]
        b = pl.multiple_of(32 * lax.rem(run, 2), 32)
        low = pl.multiple_of(64 * p + 32 * c, 32)
        high = pl.multiple_of(64 * p + 32 * (1 - c), 32)
        dkv[run // 2, pl.ds(b, 32), :VW] = dk[pl.ds(low, 32), :]
        dkv[run // 2, pl.ds(b, 32), VW:] = dv[pl.ds(low, 32), :]
        dkv_sib[run // 2, pl.ds(b, 32), :VW] = dk[pl.ds(high, 32), :].astype(bf16)
        dkv_sib[run // 2, pl.ds(b, 32), VW:] = dv[pl.ds(high, 32), :].astype(bf16)

    loop(2 * n, unsort)


def attend_back(place, lam, grad, saved, gain):
    n = place.n
    rows = 64 * n
    qb = query_rows(n)
    return pl.pallas_call(
        functools.partial(bwd_kernel, n),
        out_shape=[
            jax.ShapeDtypeStruct((n, 64, VW), bf16),
            jax.ShapeDtypeStruct((n, 64, 2 * VW), f32),
            jax.ShapeDtypeStruct((n, 64, 2 * VW), bf16),
            jax.ShapeDtypeStruct((8, VW), f32),
        ],
        in_specs=[SMEM] + [VMEM] * 6 + [SMEM, VMEM],
        out_specs=[VMEM] * 4,
        scratch_shapes=[pltpu.VMEM((2 * rows, VW), f32)] * 2,
        compiler_params=pltpu.CompilerParams(vmem_limit_bytes=vmem_cap),
        cost_estimate=busy(35),
    )(lam, grad, *saved, gain)


def swap_halves(rows):
    count, width = rows.shape
    return rows.reshape(2, 2, count // 4, width).transpose(1, 0, 2, 3).reshape(count, width)


def body(
    place,
    inputs,
    positions,
    attn_gain,
    w_query,
    w_key,
    w_value,
    w_out,
    lambda_params,
    sub_gain,
    ffn_gain,
    w_gate,
    w_up,
    w_down,
    cotangent,
):
    n, tp, seq = place.n, place.tp, place.seq
    s, t, core, head, active = place.me()
    inputs, cotangent = swap_halves(inputs), swap_halves(cotangent)
    row_count, width = inputs.shape
    half = row_count // 2
    part = width // n
    inputs_f = inputs.astype(f32)
    attn_scale = rms_scale(inputs_f)
    first_exp = jnp.exp(jnp.sum(lambda_params[0] * lambda_params[1]))
    second_exp = jnp.exp(jnp.sum(lambda_params[2] * lambda_params[3]))
    lambda_value = first_exp - second_exp + lambda_init
    lam = lambda_value.reshape(1)

    weights = (w_query, w_key, w_value)
    gain_row = attn_gain.reshape(1, width)
    if tp == 4:
        rows_all, pos, qkv = gather_all(
            place, inputs, positions.reshape(1, row_count), gain_row, weights, 1
        )
    else:
        rows_all, pos, qkv = gather_all_plain(
            place, inputs, positions.reshape(1, row_count), gain_row, weights
        )
    cotangent_late, pos = lax.optimization_barrier((cotangent, pos))
    cotangent_all = lax.all_gather(cotangent_late, "tp", axis=0, tiled=True)
    head_gain = (sub_gain * (1.0 - lambda_init)).reshape(1, VW)
    mixed, *saved = attend(place, pos.reshape(n, row_count), lam, qkv, head_gain)
    mixed_all = return_heads(place, mixed, 2).reshape(tp * row_count, HW)

    inputs_all = lax.dynamic_slice_in_dim(rows_all, s * tp, tp, 0).reshape(tp * row_count, width)
    middle_all = inputs_all.astype(f32) + dot(mixed_all, w_out)
    scale_all = rms_scale(middle_all)
    ffn_rows = (middle_all * scale_all * ffn_gain).astype(bf16)
    middle = lax.dynamic_slice_in_dim(middle_all, t * row_count, row_count, 0)
    ffn_scale = rms_scale(middle)
    gate_proj = dot(ffn_rows, w_gate)
    up_proj = dot(ffn_rows, w_up)
    gate_sig = jax.nn.sigmoid(gate_proj)
    gate_act = gate_proj * gate_sig
    hidden = (gate_act * up_proj).astype(bf16)
    down_part = dot_tn(cotangent_all, hidden).astype(bf16)
    down_part, hidden = lax.optimization_barrier((down_part, hidden))
    hidden_grad = dot_nt(cotangent_all, w_down)
    gate_rows_grad = (
        hidden_grad * up_proj * gate_sig * (1.0 + gate_proj * (1.0 - gate_sig))
    ).astype(bf16)
    up_rows_grad = (hidden_grad * gate_act).astype(bf16)
    ffn_partial = dot_nt(gate_rows_grad, w_gate) + dot_nt(up_rows_grad, w_up)
    hidden_width = hidden.shape[1]
    chunk = 256

    def ffn_weights(given, made, rest):
        rows, gate, up = given
        (out,) = made
        held, sem = rest

        def copy(i):
            at = pl.ds(pl.multiple_of(chunk * i, chunk), chunk)
            return pltpu.make_async_copy(held.at[at], out.at[at], sem.at[i])

        def step(i):
            at = pl.ds(pl.multiple_of(chunk * i, chunk), chunk)
            for k, (left, right) in enumerate(((rows, gate), (rows, up))):
                held[at, k * hidden_width : (k + 1) * hidden_width] = dot_tn(
                    left[:, at], right[...]
                ).astype(bf16)
            copy(i).start()

        loop(width // chunk, step)
        loop(width // chunk, lambda i: copy(i).wait())

    grad_parts, ffn_parts = moves(
        place,
        [Group(place, False)],
        [ffn_partial.astype(bf16).reshape(tp, row_count, width)],
        [(tp, row_count, width)],
        3,
        30,
        work=ffn_weights,
        operands=[
            (a, VMEM) for a in (ffn_rows, gate_rows_grad, up_rows_grad)
        ],
        results=[(jax.ShapeDtypeStruct((width, 2 * hidden_width), bf16), ANY)],
        scratch=[
            pltpu.VMEM((width, 2 * hidden_width), bf16),
            pltpu.SemaphoreType.DMA((width // chunk,)),
        ],
    )
    own_partial = lax.dynamic_slice_in_dim(ffn_partial, t * row_count, row_count, 0)
    member = jnp.arange(tp)[:, None, None]
    ffn_in_grad = own_partial + jnp.sum(
        jnp.where(member == t, 0.0, grad_parts.astype(f32)), axis=0
    )
    ffn_gain_part = jnp.sum(ffn_in_grad * middle * ffn_scale, axis=0)
    middle_grad = cotangent.astype(f32) + rms_back(middle, ffn_scale, ffn_gain, ffn_in_grad)
    branch_grad = middle_grad.astype(bf16)

    def scatter_rows(array):
        return lax.psum_scatter(array, "seq", scatter_dimension=0, tiled=True)

    down_grad = scatter_rows(down_part)
    ffn_grads = scatter_rows(ffn_parts)

    mixed_grad = dot_nt(branch_grad, w_out).astype(bf16)

    def head_block(x, h, c):
        return x.at[
            pl.ds(pl.multiple_of(half * c, half), half), pl.ds(pl.multiple_of(VW * h, VW), VW)
        ]

    def ffn_result(given, made, rest):
        hid, weight = given
        (out,) = made
        for i in range(tp):
            out[i] = dot(hid[i * row_count : (i + 1) * row_count, :], weight[...]).astype(bf16)

    grad_heads, ffn_out = moves(
        place,
        [Dispatch(place, head_block)],
        [mixed_grad],
        [(n, half, VW)],
        4,
        20,
        work=ffn_result,
        operands=[(hidden, VMEM), (w_down, VMEM)],
        results=[(jax.ShapeDtypeStruct((tp, row_count, width), bf16), VMEM)],
    )
    dq, dkv, dkv_sib, sums = attend_back(place, lam, grad_heads, saved, head_gain)
    normed_grad, weight_half, branch_all = finish_heads(
        place,
        dq,
        dkv,
        dkv_sib,
        rows_all,
        gain_row,
        weights,
        branch_grad,
        5,
    )
    out_part = dot_tn(mixed_all, branch_all.reshape(tp * row_count, width)).astype(bf16)
    out_part = lax.dynamic_index_in_dim(
        out_part.reshape(seq, tp, part, width), t, 1, keepdims=False
    ).reshape(seq * part, width)
    out_part, ffn_grads = lax.optimization_barrier((out_part, ffn_grads))

    attn_gain_part = jnp.sum(normed_grad * inputs_f * attn_scale, axis=0)
    input_grad = middle_grad + rms_back(inputs_f, attn_scale, attn_gain, normed_grad)

    sums = jnp.where(active, sums, 0.0)
    pad = ((0, 0), (0, 128 - part))
    small = jnp.stack(
        [
            jnp.pad(attn_gain_part.reshape(n, part), pad),
            jnp.pad(ffn_gain_part.reshape(n, part), pad),
            jnp.broadcast_to(sums[0], (n, VW)),
            jnp.broadcast_to(sums[1], (n, VW)),
        ]
        + [jnp.zeros((n, VW), f32)] * 4,
        axis=1,
    )
    small, out_part = lax.optimization_barrier((small, out_part))
    weight_rows, small_all, out_parts = moves(
        place,
        [
            Collect(place, lambda o, t, h, c: o.at[h], True),
            Everyone(place, False),
            Group(place, False),
        ],
        [weight_half.reshape(n // 2, part, 3 * VW), small, ffn_out],
        [(H, part, 3 * VW), (n, 8, VW), (tp, row_count, width)],
        6,
        20,
    )
    output = (middle + jnp.sum(out_parts.astype(f32), axis=0)).astype(bf16)
    out_grad = scatter_rows(out_part).astype(f32)
    ffn_grads = ffn_grads.astype(f32)
    down_grad = down_grad.astype(f32).T
    gate_grad = ffn_grads[:, :hidden_width]
    up_grad = ffn_grads[:, hidden_width:]
    weight_rows = weight_rows.astype(f32).reshape(H, part, 3, VW).transpose(2, 1, 0, 3)
    weight_rows = weight_rows.reshape(3, part, HW)
    small_sum = jnp.sum(small_all, axis=0)
    lambda_total = jnp.sum(small_sum[3])
    lambda_grads = jnp.stack(
        [
            lambda_total * first_exp * lambda_params[1],
            lambda_total * first_exp * lambda_params[0],
            -lambda_total * second_exp * lambda_params[3],
            -lambda_total * second_exp * lambda_params[2],
        ]
    )
    lambda_norm = jnp.sqrt(jnp.sum(lambda_grads * lambda_grads))
    output, input_grad = swap_halves(output), swap_halves(input_grad)
    return (
        output,
        input_grad,
        small_sum[0, :part],
        weight_rows[0],
        weight_rows[1],
        weight_rows[2],
        out_grad,
        lambda_grads,
        small_sum[2],
        small_sum[1, :part],
        gate_grad,
        up_grad,
        down_grad,
        lambda_total,
        lambda_norm,
    )


def solution(mesh):
    place = Place(mesh.shape["seq"], mesh.shape["tp"])
    both = ("seq", "tp")
    placed = (
        P(both, None),
        P(both),
        P(),
        P(),
        P(),
        P(),
        P(),
        P(),
        P(),
        P(),
        P(None, "tp"),
        P(None, "tp"),
        P("tp", None),
        P(both, None),
    )
    return jax.shard_map(
        functools.partial(body, place),
        mesh=mesh,
        in_specs=placed,
        out_specs=(
            P(both, None),
            P(both, None),
            P(both),
            P(both, None),
            P(both, None),
            P(both, None),
            P(both, None),
            P(),
            P(),
            P(both),
            P("seq", "tp"),
            P("seq", "tp"),
            P("tp", "seq"),
            P(),
            P(),
        ),
        check_vma=False,
    )
```

```python
import functools
import math

import jax
import jax.numpy as jnp
from jax import lax
from jax.experimental import pallas as pl
from jax.experimental.pallas import tpu as pltpu
from jax.sharding import PartitionSpec as P

H = 12
HALF = 64
VW = 128
HW = 1536

eps = 1e-05
lambda_init = 0.8 - 0.6 * math.exp(-3.3)
masked_score = -1e30
MESH = pl.DeviceIdType.MESH
ANY = pl.BlockSpec(memory_space=pl.ANY)
VMEM = pl.BlockSpec(memory_space=pltpu.VMEM)
SMEM = pl.BlockSpec(memory_space=pltpu.SMEM)
bf16 = jnp.bfloat16
f32 = jnp.float32
vmem_cap = 60 * 1024 * 1024


def dot(left, right):
    return jnp.dot(left, right, preferred_element_type=f32)


def dot_tn(left, right):
    return lax.dot_general(left, right, (((0,), (0,)), ((), ())), preferred_element_type=f32)


def dot_nt(left, right):
    return lax.dot_general(left, right, (((1,), (1,)), ((), ())), preferred_element_type=f32)


def rms_scale(values):
    return lax.rsqrt(jnp.mean(values * values, axis=-1, keepdims=True) + eps)


def rms_back(values, inv_rms, gain_vec, upstream):
    weighted = upstream * gain_vec
    inner_mean = jnp.mean(weighted * values, axis=-1, keepdims=True)
    return inv_rms * weighted - values * (inv_rms * inv_rms * inv_rms) * inner_mean


class Place:
    def __init__(self, seq, tp):
        self.seq, self.tp, self.n = seq, tp, seq * tp
        self.per = -(-H // (seq // 2))
        assert self.per <= tp and seq % 2 == 0

    def me(self):
        s, t = lax.axis_index("seq"), lax.axis_index("tp")
        head = (s // 2) * self.per + t
        active = jnp.logical_and(t < self.per, head < H)
        return s, t, lax.rem(s, 2), head, active

    def head_device(self, index):
        head, core = index // 2, lax.rem(index, 2)
        return 2 * (head // self.per) + core, lax.rem(head, self.per)

    def device(self, linear):
        return linear // self.tp, lax.rem(linear, self.tp)


def busy(microseconds):
    return pl.CostEstimate(
        flops=int(microseconds * 1e9), bytes_accessed=int(microseconds * 3e6), transcendentals=0
    )


def remote(src, dst, send, recv, where):
    return pltpu.make_async_remote_copy(
        src_ref=src, dst_ref=dst, send_sem=send, recv_sem=recv, device_id=where, device_id_type=MESH
    )


def loop(count, step):
    def one(k, carry):
        step(k)
        return carry

    lax.fori_loop(0, count, one, 0)


class Dispatch:
    def __init__(self, place, cut):
        self.p, self.cut = place, cut
        self.sems = [2 * H, place.n, 1]

    def start_one(self, index, x, o, send, recv, here):
        p = self.p
        s, t, c, head, active = p.me()
        lin = s * p.tp + t
        ds, dt = p.head_device(index)
        mine = jnp.logical_and(ds == s, dt == t)
        source = self.cut(x, index // 2, lax.rem(index, 2))

        @pl.when(jnp.logical_not(mine))
        def _():
            remote(source, o.at[lin], send.at[index], recv.at[lin], (ds, dt)).start()

        @pl.when(mine)
        def _():
            pltpu.make_async_copy(source, o.at[lin], here.at[0]).start()

    def start(self, *refs):
        p = self.p
        lin = lax.axis_index("seq") * p.tp + lax.axis_index("tp")
        loop(2 * H, lambda k: self.start_one(lax.rem(k + lin, 2 * H), *refs))

    def finish(self, x, o, send, recv, here, arrived=None):
        p = self.p
        s, t, c, head, active = p.me()
        lin = s * p.tp + t

        @pl.when(active)
        def _():
            pltpu.make_async_copy(self.cut(x, head, c), o.at[lin], here.at[0]).wait()
            if arrived is not None:
                arrived(lin)

            def got(k):
                other = lax.rem(lin + 1 + k, p.n)
                remote(o.at[other], o.at[other], send.at[0], recv.at[other], (s, t)).wait_recv()
                if arrived is not None:
                    arrived(other)

            loop(p.n - 1, got)

        def sent(k):
            ds, dt = p.head_device(k)

            @pl.when(jnp.logical_not(jnp.logical_and(ds == s, dt == t)))
            def _():
                remote(
                    self.cut(x, k // 2, lax.rem(k, 2)), o.at[0], send.at[k], recv.at[0], (ds, dt)
                ).wait_send()

        loop(2 * H, sent)


class Collect:
    def __init__(self, place, into, halves=False):
        self.p, self.into, self.halves = place, into, halves
        self.sems = [place.n, 2 * H, 1]

    def start(self, x, o, send, recv, here):
        p = self.p
        s, t, c, head, active = p.me()
        lin = s * p.tp + t
        count = p.n // 2 if self.halves else p.n

        @pl.when(active)
        def _():
            def step(k):
                slot = lax.rem(k + lin, count)
                other = slot + c * count if self.halves else slot
                into = self.into(o, lax.rem(other, p.tp), head, c)

                @pl.when(other != lin)
                def _():
                    remote(
                        x.at[slot], into, send.at[slot], recv.at[head * 2 + c], p.device(other)
                    ).start()

                @pl.when(other == lin)
                def _():
                    pltpu.make_async_copy(x.at[slot], into, here.at[0]).start()

            loop(count, step)

    def got(self, index, x, o, send, recv, here):
        p = self.p
        s, t = lax.axis_index("seq"), lax.axis_index("tp")
        into = self.into(o, t, index // 2, lax.rem(index, 2))
        ds, dt = p.head_device(index)
        mine = jnp.logical_and(ds == s, dt == t)

        @pl.when(jnp.logical_not(mine))
        def _():
            remote(into, into, send.at[0], recv.at[index], (s, t)).wait_recv()

        @pl.when(mine)
        def _():
            pltpu.make_async_copy(x.at[0], into, here.at[0]).wait()

    def sent(self, x, o, send, recv, here):
        p = self.p
        s, t, c, head, active = p.me()
        lin = s * p.tp + t
        count = p.n // 2 if self.halves else p.n

        @pl.when(active)
        def _():
            def one(k):
                other = k + c * count if self.halves else k

                @pl.when(other != lin)
                def _():
                    remote(
                        x.at[k], x.at[k], send.at[k], recv.at[0], p.device(other)
                    ).wait_send()

            loop(count, one)

    def finish(self, *refs):
        p = self.p
        if self.halves:
            lin = lax.axis_index("seq") * p.tp + lax.axis_index("tp")
            half = lin // (p.n // 2)
            loop(H, lambda k: self.got(2 * k + half, *refs))
        else:
            loop(2 * H, lambda k: self.got(k, *refs))
        self.sent(*refs)


class Everyone:
    def __init__(self, place, whole):
        self.p, self.whole = place, whole
        self.sems = [place.n, place.n, 1]

    def start(self, x, o, send, recv, here):
        p = self.p
        s, t = lax.axis_index("seq"), lax.axis_index("tp")
        lin = s * p.tp + t
        pltpu.make_async_copy(x if self.whole else x.at[lin], o.at[lin], here.at[0]).start()

        def step(k):
            other = lax.rem(lin + 1 + k, p.n)
            remote(
                x if self.whole else x.at[other],
                o.at[lin],
                send.at[other],
                recv.at[lin],
                p.device(other),
            ).start()

        loop(p.n - 1, step)

    def finish(self, x, o, send, recv, here):
        p = self.p
        s, t = lax.axis_index("seq"), lax.axis_index("tp")
        lin = s * p.tp + t
        pltpu.make_async_copy(x if self.whole else x.at[lin], o.at[lin], here.at[0]).wait()

        def done(k):
            other = lax.rem(lin + 1 + k, p.n)
            both = remote(
                x if self.whole else x.at[other],
                o.at[other],
                send.at[other],
                recv.at[other],
                p.device(other),
            )
            both.wait_recv()
            both.wait_send()

        loop(p.n - 1, done)


class Group:
    def __init__(self, place, whole):
        self.p, self.whole = place, whole
        self.sems = [place.tp, place.tp, 1]

    def start(self, x, o, send, recv, here):
        p = self.p
        s, t = lax.axis_index("seq"), lax.axis_index("tp")
        pltpu.make_async_copy(x if self.whole else x.at[t], o.at[t], here.at[0]).start()
        for k in range(1, p.tp):
            other = lax.rem(t + k, p.tp)
            remote(
                x if self.whole else x.at[other], o.at[t], send.at[other], recv.at[t], (s, other)
            ).start()

    def finish(self, x, o, send, recv, here):
        p = self.p
        s, t = lax.axis_index("seq"), lax.axis_index("tp")
        pltpu.make_async_copy(x if self.whole else x.at[t], o.at[t], here.at[0]).wait()
        for k in range(1, p.tp):
            other = lax.rem(t + k, p.tp)
            both = remote(
                x if self.whole else x.at[other],
                o.at[other],
                send.at[other],
                recv.at[other],
                (s, other),
            )
            both.wait_recv()
            both.wait_send()


def greet(place):
    s, t = lax.axis_index("seq"), lax.axis_index("tp")
    lin = s * place.tp + t
    barrier = pltpu.get_barrier_semaphore()

    def hello(k):
        pl.semaphore_signal(
            barrier,
            inc=1,
            device_id=place.device(lax.rem(lin + 1 + k, place.n)),
            device_id_type=MESH,
        )

    loop(place.n - 1, hello)
    pl.semaphore_wait(barrier, place.n - 1)


def moves(place, parts, arrays, outs, ident, cost, work=None, operands=(), results=(), scratch=()):
    count, extra = len(parts), len(operands)

    def kernel(*refs):
        ins, given = refs[:count], refs[count : count + extra]
        refs = refs[count + extra :]
        into, made = refs[:count], refs[count : count + len(results)]
        refs = refs[count + len(results) :]
        sems, rest = refs[: 3 * count], refs[3 * count :]
        greet(place)
        for i, part in enumerate(parts):
            part.start(ins[i], into[i], *sems[3 * i : 3 * i + 3])
        if work is not None:
            work(given, made, rest)
        for i, part in enumerate(parts):
            part.finish(ins[i], into[i], *sems[3 * i : 3 * i + 3])

    return pl.pallas_call(
        kernel,
        out_shape=[jax.ShapeDtypeStruct(s, a.dtype) for s, a in zip(outs, arrays)]
        + [shape for shape, spec in results],
        in_specs=[ANY] * count + [spec for array, spec in operands],
        out_specs=[ANY] * count + [spec for shape, spec in results],
        scratch_shapes=[pltpu.SemaphoreType.DMA((k,)) for part in parts for k in part.sems]
        + list(scratch),
        compiler_params=pltpu.CompilerParams(
            collective_id=ident, has_side_effects=True, vmem_limit_bytes=vmem_cap
        ),
        cost_estimate=busy(cost),
    )(*arrays, *[array for array, spec in operands])


def gather_all(place, rows, run_pos, gain, weights, ident):
    n, tp, depth = place.n, place.tp, place.seq // 2
    count, width = rows.shape
    half = count // 2
    tell = Everyone(place, True)

    def relay(first, use, x, o, full, halves, z_up, z_down, by_x, by_y, half_x, half_y, across, here):
        s, t = lax.axis_index("seq"), lax.axis_index("tp")
        z, c = s // 2, lax.rem(s, 2)
        t_x = t + 1 - 2 * lax.rem(t, 2)
        t_y = lax.rem(t + 2, 4)
        t_d = t_x + 2 - 4 * (t_x // 2)

        def slot(zs, core, ts):
            return (2 * zs + core) * tp + ts

        def line(zs, source, step):
            at = slot(zs, c, t)
            sem = z_up if step > 0 else z_down
            return remote(source, o.at[at], sem.at[zs], full.at[at], (s + 2 * step, t))

        def side(zs, source, sem, ts):
            at = slot(zs, c, t)
            return remote(source, o.at[at], sem.at[zs], full.at[at], (s, ts))

        def other_core(zs, ts, source):
            at = slot(zs, c, ts)
            return remote(
                source, o.at[at], across.at[zs * tp + ts], full.at[at], (s + 1 - 2 * c, t)
            )

        def corner(zs, ts, low, sem, to):
            at = slot(zs, c, ts)
            part = o.at[at, low : low + half]
            return remote(
                part, part, sem.at[zs], halves.at[2 * at + low // half], (s, to)
            )

        def arrived(at):
            remote(o.at[at], o.at[at], here.at[0], full.at[at], (s, t)).wait_recv()

        def push(zs, source):
            @pl.when(jnp.logical_and(zs <= z, z < depth - 1))
            def _():
                line(zs, source, 1).start()

            @pl.when(jnp.logical_and(zs >= z, z > 0))
            def _():
                line(zs, source, -1).start()

            side(zs, source, by_x, t_x).start()
            side(zs, source, by_y, t_y).start()
            other_core(zs, t, source).start()

        def each(k, act):
            def one(sign):
                zs = z + (2 * sign - 1) * k
                valid = jnp.logical_and(zs >= 0, zs < depth)
                valid = jnp.logical_and(valid, jnp.logical_and(k >= 0, k + 1 > sign))

                @pl.when(valid)
                def _():
                    act(zs)

            loop(2, one)

        def from_line(zs):
            arrived(slot(zs, c, t))
            push(zs, o.at[slot(zs, c, t)])

        def from_sides(zs):
            arrived(slot(zs, c, t_x))
            corner(zs, t_x, 0, half_y, t_y).start()
            other_core(zs, t_x, o.at[slot(zs, c, t_x)]).start()
            arrived(slot(zs, c, t_y))
            corner(zs, t_y, half, half_x, t_x).start()
            other_core(zs, t_y, o.at[slot(zs, c, t_y)]).start()

        def from_corner(zs):
            at = slot(zs, c, t_d)
            for low in (0, half):
                part = o.at[at, low : low + half]
                remote(
                    part, part, here.at[0], halves.at[2 * at + low // half], (s, t)
                ).wait_recv()
            other_core(zs, t_d, o.at[at]).start()

        keep = pltpu.make_async_copy(x, o.at[slot(z, c, t)], here.at[0])
        keep.start()
        push(z, x)
        first()
        keep.wait()

        def use_block(k):
            def one(i):
                other, v = i // 4, lax.rem(i, 4)
                m_x, m_y = lax.rem(v, 2), v // 2
                x_bit, y_bit = lax.rem(t, 2), t // 2
                ts = 2 * (y_bit + m_y - 2 * y_bit * m_y) + x_bit + m_x - 2 * x_bit * m_x
                core = c + other - 2 * c * other

                def act(zs):
                    at = slot(zs, core, ts)

                    @pl.when(other > 0)
                    def _():
                        arrived(at)

                    use(at)

                each(k - m_x - m_y - other, act)

            loop(8, one)

        def wave(k):
            @pl.when(k > 0)
            def _():
                each(k, from_line)
                each(k - 1, from_sides)
                each(k - 2, from_corner)

            use_block(k)

        loop(depth + 3, wave)

        def sent(k):
            zs = k
            at = slot(zs, c, t)

            @pl.when(jnp.logical_and(zs <= z, z < depth - 1))
            def _():
                line(zs, o.at[at], 1).wait_send()

            @pl.when(jnp.logical_and(zs >= z, z > 0))
            def _():
                line(zs, o.at[at], -1).wait_send()

            side(zs, o.at[at], by_x, t_x).wait_send()
            side(zs, o.at[at], by_y, t_y).wait_send()
            corner(zs, t_x, 0, half_y, t_y).wait_send()
            corner(zs, t_y, half, half_x, t_x).wait_send()
            for ts in range(tp):
                other_core(zs, ts, o.at[at]).wait_send()

        loop(depth, sent)

    sems = [n, 2 * n] + [depth] * 6 + [depth * tp, 1]

    def kernel(x, r, gain, wq, wk, wv, out, pos, qkv, o, out_sem, *refs):
        greet(place)

        def save(at):
            return pltpu.make_async_copy(o.at[at], out.at[at], out_sem.at[at])

        def use(at):
            save(at).start()
            x = o[at].astype(f32)
            x = (x * rms_scale(x) * gain[...]).astype(bf16)
            for i, w in enumerate((wq, wk, wv)):
                qkv[at, :, i * VW : (i + 1) * VW] = dot(x, w[...]).astype(bf16)

        relay(lambda: tell.start(r, pos, *refs[:3]), use, x, o, *refs[3:])
        tell.finish(r, pos, *refs[:3])
        loop(n, lambda k: save(k).wait())

    def column(g):
        s, t, c, head, active = place.me()
        return 0, jnp.minimum(head, H - 1)

    columns = pl.BlockSpec((width, VW), column)
    return pl.pallas_call(
        kernel,
        grid=(1,),
        out_shape=[
            jax.ShapeDtypeStruct((n,) + rows.shape, rows.dtype),
            jax.ShapeDtypeStruct((n,) + run_pos.shape, run_pos.dtype),
            jax.ShapeDtypeStruct((n, count, 3 * VW), bf16),
        ],
        in_specs=[ANY] * 2 + [VMEM] + [columns] * 3,
        out_specs=[ANY] * 2 + [VMEM],
        scratch_shapes=[
            pltpu.VMEM((n,) + rows.shape, rows.dtype),
            pltpu.SemaphoreType.DMA((n,)),
        ]
        + [pltpu.SemaphoreType.DMA((k,)) for k in tell.sems + sems],
        compiler_params=pltpu.CompilerParams(
            collective_id=ident, has_side_effects=True, vmem_limit_bytes=vmem_cap
        ),
        cost_estimate=busy(50),
    )(rows, run_pos, gain, *weights)


def gather_all_plain(place, rows, run_pos, gain, weights):
    axes = ("seq", "tp")
    rows_all = lax.all_gather(rows, axes, axis=0, tiled=False)
    pos = lax.all_gather(run_pos, axes, axis=0, tiled=False)
    x = rows_all.astype(f32)
    x = (x * rms_scale(x) * gain).astype(bf16)
    s, t, c, head, active = place.me()
    column = jnp.minimum(head, H - 1) * VW
    qkv = [
        dot(x, lax.dynamic_slice_in_dim(w, column, VW, 1)).astype(bf16) for w in weights
    ]
    return rows_all, pos, jnp.concatenate(qkv, axis=2)


def feed_forward(place, mixed, rows_all, cotangent_all, gain, w_out, w_gate, w_up, w_down, ident):
    n, tp, half = place.n, place.tp, mixed.shape[1]
    count, width = rows_all.shape[1:]
    hid = w_gate.shape[1]
    chunk = 256

    def into(o, t, h, c):
        return o.at[
            t,
            pl.ds(pl.multiple_of(half * c, half), half),
            pl.ds(pl.multiple_of(VW * h, VW), VW),
        ]

    back = Collect(place, into)

    def kernel(*refs):
        mixed, rows_all, cot, gain, wo_in, wg_in, wu_in, wd_in, *refs = refs
        parts, mixed_out, hidden, middle, middle_grad, branch, mixed_grad, gain_part, *refs = refs
        mixed_v, x_v, rows_v, gate_v, up_v, send_v, recv_v, own_part, held, *refs = refs
        wo, wg, wu, wd, *sems = refs
        share_send, share_recv, part_send, part_recv, w_sem, x_sem, out_sem, mixed_sem = sems[3:]
        s, t = lax.axis_index("seq"), lax.axis_index("tp")
        greet(place)
        back.start(mixed, mixed_v, *sems[:3])

        def fetch(m):
            return pltpu.make_async_copy(rows_all.at[s * tp + m], x_v.at[m], x_sem.at[m])

        loads = [
            pltpu.make_async_copy(a, b, w_sem.at[i])
            for i, (a, b) in enumerate(((wo_in, wo), (wg_in, wg), (wu_in, wu), (wd_in, wd)))
        ]
        loop(tp, lambda m: fetch(m).start())
        for load in loads:
            load.start()

        def share(k, c, slot):
            other = lax.rem(t + k, tp)
            at = slot(other)
            return remote(
                mixed_v.at[t, half * c : half * c + half, :],
                mixed_v.at[at, half * c : half * c + half, :],
                share_send.at[2 * other + c],
                share_recv.at[2 * at + c],
                (s, other),
            )

        def give(k, slot):
            other = lax.rem(t + k, tp)
            at = slot(other)
            return remote(
                send_v.at[other], recv_v.at[at], part_send.at[other], part_recv.at[at], (s, other)
            )

        for c in range(2):
            loop(H, lambda h: back.got(2 * h + c, mixed, mixed_v, *sems[:3]))
            for k in range(1, tp):
                share(k, c, lambda other: t).start()
        loop(tp, lambda m: fetch(m).wait())
        for load in loads:
            load.wait()

        def member(k):
            m = lax.rem(t + k, tp)

            @pl.when(k > 0)
            def _():
                for c in range(2):
                    share(k, c, lambda other: other).wait_recv()

            x = x_v[m].astype(f32) + dot(mixed_v[m], wo[...])
            rows = (x * rms_scale(x) * gain[...]).astype(bf16)
            rows_v[m] = rows
            gate = dot(rows, wg[...])
            up = dot(rows, wu[...])
            sig = jax.nn.sigmoid(gate)
            act = gate * sig
            hidden[m] = (act * up).astype(bf16)
            grad = dot_nt(cot[m], wd[...])
            gate_rows = (grad * up * sig * (1.0 + gate * (1.0 - sig))).astype(bf16)
            up_rows = (grad * act).astype(bf16)
            gate_v[m] = gate_rows
            up_v[m] = up_rows
            part = dot_nt(gate_rows, wg[...]) + dot_nt(up_rows, wu[...])

            @pl.when(k == 0)
            def _():
                own_part[...] = part
                middle[...] = x

            @pl.when(k > 0)
            def _():
                send_v[m] = part.astype(bf16)
                give(k, lambda other: t).start()

        loop(tp, member)
        keep = pltpu.make_async_copy(mixed_v, mixed_out, mixed_sem.at[0])
        keep.start()

        def copy(i):
            at = pl.ds(pl.multiple_of(chunk * i, chunk), chunk)
            return pltpu.make_async_copy(held.at[at], parts.at[at], out_sem.at[i])

        def weight_rows(i):
            at = pl.ds(pl.multiple_of(chunk * i, chunk), chunk)
            for k, (left, right) in enumerate(((cot, hidden), (rows_v, gate_v), (rows_v, up_v))):
                held[at, k * hid : (k + 1) * hid] = dot_tn(
                    left[:, :, at].reshape(tp * count, chunk), right[...].reshape(tp * count, hid)
                ).astype(bf16)
            copy(i).start()

        loop(width // chunk, weight_rows)
        total = own_part[...]
        for k in range(1, tp):
            give(k, lambda other: other).wait_recv()
            total = total + recv_v[lax.rem(t + k, tp)].astype(f32)
        mid = middle[...]
        scale = rms_scale(mid)
        gain_part[...] = jnp.sum(total * mid * scale, axis=0, keepdims=True)
        grad = cot[t].astype(f32) + rms_back(mid, scale, gain[...], total)
        middle_grad[...] = grad
        branch[...] = grad.astype(bf16)
        mixed_grad[...] = dot_nt(grad.astype(bf16), wo[...]).astype(bf16)
        loop(width // chunk, lambda i: copy(i).wait())
        keep.wait()
        for k in range(1, tp):
            give(k, lambda other: other).wait_send()
            for c in range(2):
                share(k, c, lambda other: other).wait_send()
        back.sent(mixed, mixed_v, *sems[:3])

    struct = jax.ShapeDtypeStruct
    group = (tp, count, width)
    return pl.pallas_call(
        kernel,
        out_shape=[
            struct((width, 3 * hid), bf16),
            struct(group, bf16),
            struct((tp, count, hid), bf16),
            struct((count, width), f32),
            struct((count, width), f32),
            struct((count, width), bf16),
            struct((count, width), bf16),
            struct((1, width), f32),
        ],
        in_specs=[ANY, ANY, VMEM, VMEM] + [ANY] * 4,
        out_specs=[ANY, ANY] + [VMEM] * 6,
        scratch_shapes=[
            pltpu.VMEM(group, bf16),
            pltpu.VMEM(group, bf16),
            pltpu.VMEM(group, bf16),
            pltpu.VMEM((tp, count, hid), bf16),
            pltpu.VMEM((tp, count, hid), bf16),
            pltpu.VMEM(group, bf16),
            pltpu.VMEM(group, bf16),
            pltpu.VMEM((count, width), f32),
            pltpu.VMEM((width, 3 * hid), bf16),
            pltpu.VMEM(w_out.shape, bf16),
            pltpu.VMEM(w_gate.shape, bf16),
            pltpu.VMEM(w_up.shape, bf16),
            pltpu.VMEM(w_down.shape, bf16),
        ]
        + [
            pltpu.SemaphoreType.DMA((k,))
            for k in back.sems + [2 * tp, 2 * tp, tp, tp, 4, tp, width // chunk, 1]
        ],
        compiler_params=pltpu.CompilerParams(
            collective_id=ident, has_side_effects=True, vmem_limit_bytes=vmem_cap
        ),
        cost_estimate=busy(60),
    )(mixed, rows_all, cotangent_all, gain, w_out, w_gate, w_up, w_down)


def finish_heads(
    place, dq, dkv, dkv_sib, rows_all, gain, weights, branch_grad, ident
):
    n, half = place.n, dq.shape[1]
    width = rows_all.shape[2]
    part, chunk, lot = width // n, 256, 8

    def into(o, t, h, c):
        return o.at[
            pl.ds(pl.multiple_of(half * c, half), half),
            pl.ds(pl.multiple_of(3 * VW * h, 3 * VW), 3 * VW),
        ]

    back, share = Collect(place, into), Group(place, True)

    def kernel(*refs):
        dq, dkv, dkv_sib, rows_all, gain, *refs = refs
        weights, refs = refs[:3], refs[3:]
        branch, normed_grad, weight_half, branch_all, *refs = refs
        other_dkv, grads, rows_back, raw, held, away, other, w_all, *sems = refs
        s, t = lax.axis_index("seq"), lax.axis_index("tp")
        c = lax.rem(s, 2)
        send, recv, raw_sem, w_sem = sems[6:]
        sibling = (s + 1 - 2 * c, t)
        greet(place)
        swap = remote(dkv_sib, other_dkv, send.at[0], recv.at[0], sibling)
        swap.start()

        def fetch(i):
            return pltpu.make_async_copy(
                rows_all.at[
                    pl.ds(lot * i, lot), pl.ds(pl.multiple_of(half * c, half), half), :
                ],
                raw.at[lax.rem(i, 2)],
                raw_sem.at[lax.rem(i, 2)],
            )

        fetch(0).start()
        loads = [
            pltpu.make_async_copy(w, w_all.at[i], w_sem.at[i]) for i, w in enumerate(weights)
        ]
        for load in loads:
            load.start()
        swap.wait_recv()

        def join(i):
            grads[i, :, :VW] = dq[i]
            grads[i, :, VW:] = (dkv[i] + other_dkv[i].astype(f32)).astype(bf16)

        loop(n, join)
        back.start(grads, rows_back, *sems[:3])
        share.start(branch, branch_all, *sems[3:6])
        held[...] = jnp.zeros_like(held)

        def rows(i):
            @pl.when(i + 1 < n // lot)
            def _():
                fetch(i + 1).start()

            fetch(i).wait()
            x = raw[lax.rem(i, 2)].reshape(lot * half, width).astype(f32)
            x = (x * rms_scale(x) * gain[...]).astype(bf16)
            g = grads[pl.ds(lot * i, lot)].reshape(lot * half, 3 * VW)
            for k in range(width // chunk):
                held[k * chunk : (k + 1) * chunk, :] += dot_tn(
                    x[:, k * chunk : (k + 1) * chunk], g
                )

        loop(n // lot, rows)
        low = pl.multiple_of(c * (width // 2), width // 2)
        high = pl.multiple_of((1 - c) * (width // 2), width // 2)
        away[...] = held[pl.ds(high, width // 2), :].astype(bf16)
        cross = remote(away, other, send.at[1], recv.at[1], sibling)
        cross.start()
        back.finish(grads, rows_back, *sems[:3])
        for load in loads:
            load.wait()
        total = None
        for h in range(0, H, 2):
            for i in range(3):
                at = (3 * h + i) * VW
                x = jnp.concatenate(
                    [rows_back[:, at : at + VW], rows_back[:, at + 3 * VW : at + 4 * VW]], axis=1
                )
                new = dot_nt(x, w_all[i, :, h * VW : (h + 2) * VW])
                total = new if total is None else total + new
        normed_grad[...] = total
        cross.wait_recv()
        weight_half[...] = (held[pl.ds(low, width // 2), :] + other[...].astype(f32)).astype(bf16)
        share.finish(branch, branch_all, *sems[3:6])
        swap.wait_send()
        cross.wait_send()

    return pl.pallas_call(
        kernel,
        out_shape=[
            jax.ShapeDtypeStruct((2 * half, width), f32),
            jax.ShapeDtypeStruct((width // 2, 3 * VW), bf16),
            jax.ShapeDtypeStruct((place.tp,) + branch_grad.shape, bf16),
        ],
        in_specs=[VMEM, VMEM, ANY, ANY, VMEM] + [ANY] * 4,
        out_specs=[VMEM, VMEM, ANY],
        scratch_shapes=[
            pltpu.VMEM((n, half, 2 * VW), bf16),
            pltpu.VMEM((n, half, 3 * VW), bf16),
            pltpu.VMEM((2 * half, 3 * HW), bf16),
            pltpu.VMEM((2, lot, half, width), bf16),
            pltpu.VMEM((width, 3 * VW), f32),
            pltpu.VMEM((width // 2, 3 * VW), bf16),
            pltpu.VMEM((width // 2, 3 * VW), bf16),
            pltpu.VMEM((3,) + weights[0].shape, bf16),
        ]
        + [pltpu.SemaphoreType.DMA((k,)) for k in back.sems + share.sems + [2, 2, 2, 3]],
        compiler_params=pltpu.CompilerParams(
            collective_id=ident, has_side_effects=True, vmem_limit_bytes=vmem_cap
        ),
        cost_estimate=busy(40),
    )(dq, dkv, dkv_sib, rows_all, gain, *weights, branch_grad)


def spans(n, count, step):
    if n <= 32:
        for j in range(count):
            step(j)
    else:
        loop(count, step)


def fold(n, count, step, carry):
    if n <= 32:
        for k in range(count):
            carry = step(k, carry)
        return carry
    return lax.fori_loop(0, count, step, carry)


def aligned(value, unit):
    return value if isinstance(value, int) else pl.multiple_of(value, unit)


def query_rows(n):
    return 256 if n <= 64 else 128


def two_maps(rows):
    lane = lax.broadcasted_iota(jnp.int32, rows.shape, 1)
    zero = jnp.zeros_like(rows)
    return jnp.concatenate(
        [jnp.where(lane < HALF, rows, zero), jnp.where(lane < HALF, zero, rows)], axis=0
    )


def fwd_kernel(n, pos, lam, qkv, gain, mixed, mix, lse, qs, ks, vs, order, score):
    qb = query_rows(n)
    kb_rows = 2 * qb
    c = lax.rem(lax.axis_index("seq"), 2)

    def place_run(run):
        order[pos[run // 2, lax.rem(run, 2) * 64] // 64] = run

    loop(2 * n, place_run)
    lambda_value = lam[0]

    def sort(p):
        run = order[p]
        i, b = run // 2, pl.multiple_of(32 * lax.rem(run, 2), 32)
        for h in range(2):
            at = pl.ds(pl.multiple_of(64 * p + 32 * h, 32), 32)
            rows = pl.ds(pl.multiple_of(64 * h + b, 32), 32)
            ks[at, :] = qkv[i, rows, VW : 2 * VW]
            vs[at, :] = qkv[i, rows, 2 * VW :]
        mine = qkv[i, pl.ds(pl.multiple_of(64 * c + b, 32), 32), :VW]
        qs[pl.ds(pl.multiple_of(32 * p, 32), 32), :] = mine * jnp.asarray(0.125, bf16)

    loop(2 * n, sort)

    def block(j):
        at = pl.ds(aligned(qb * j, qb), qb)
        q2 = two_maps(qs[at, :])

        def scores(kb):
            return dot_nt(q2, ks[pl.ds(aligned(kb_rows * kb, kb_rows), kb_rows), :])

        def lanes(top, s):
            for i in range(kb_rows // 128):
                top = jnp.maximum(top, s[:, 128 * i : 128 * i + 128])
            return top

        def first(kb, top):
            s = scores(kb)
            score[:, pl.ds(aligned(kb_rows * kb, kb_rows), kb_rows)] = s
            return lanes(top, s)

        top = fold(n, j, first, jnp.full((2 * qb, 128), masked_score, f32))
        s = scores(j)
        row = lax.broadcasted_iota(jnp.int32, s.shape, 0)
        row = lax.rem(row, qb)
        allowed = (
            lax.broadcasted_iota(jnp.int32, s.shape, 1)
            <= 64 * (row // 32) + lax.rem(row, 32) + 32 * c
        )
        s = jnp.where(allowed, s, masked_score)
        score[:, pl.ds(aligned(kb_rows * j, kb_rows), kb_rows)] = s
        high = jnp.max(lanes(top, s), axis=1, keepdims=True)
        ones = jnp.ones((kb_rows, VW), bf16)

        def second(kb, acc):
            here = pl.ds(aligned(kb_rows * kb, kb_rows), kb_rows)
            weights = jnp.exp(score[:, here] - high).astype(bf16)
            return acc + dot(weights, jnp.concatenate([vs[here, :], ones], axis=1))

        acc = fold(n, j + 1, second, jnp.zeros((2 * qb, 2 * VW), f32))
        total = acc[:, VW:]
        mixes = acc[:, :VW] / total
        lse[j] = jnp.transpose(high + jnp.log(total))[:8, :]
        mix[0, at, :] = mixes[:qb]
        mix[1, at, :] = mixes[qb:]
        out = mixes[:qb] - lambda_value * mixes[qb:]
        out = (out * rms_scale(out) * gain[...]).astype(bf16)
        for i in range(qb // 32):
            run = order[j * (qb // 32) + i]
            b = pl.multiple_of(32 * lax.rem(run, 2), 32)
            mixed[run // 2, pl.ds(b, 32), :] = out[32 * i : 32 * i + 32]

    spans(n, n * 64 // qb, block)


def attend(place, pos, lam, qkv, gain):
    n = place.n
    rows = 64 * n
    qb = query_rows(n)
    return pl.pallas_call(
        functools.partial(fwd_kernel, n),
        out_shape=[
            jax.ShapeDtypeStruct((n, 64, VW), bf16),
            jax.ShapeDtypeStruct((2, rows, VW), f32),
            jax.ShapeDtypeStruct((rows // qb, 8, 2 * qb), f32),
            jax.ShapeDtypeStruct((rows, VW), bf16),
            jax.ShapeDtypeStruct((2 * rows, VW), bf16),
            jax.ShapeDtypeStruct((2 * rows, VW), bf16),
            jax.ShapeDtypeStruct((2 * n,), jnp.int32),
        ],
        in_specs=[SMEM, SMEM, VMEM, VMEM],
        out_specs=[VMEM] * 6 + [SMEM],
        scratch_shapes=[pltpu.VMEM((2 * qb, 2 * rows), f32)],
        compiler_params=pltpu.CompilerParams(vmem_limit_bytes=vmem_cap),
        cost_estimate=busy(20),
    )(pos, lam, qkv, gain)


def bwd_kernel(
    n,
    lam,
    grad,
    mix,
    lse,
    qs,
    ks,
    vs,
    order,
    gain,
    dq,
    dkv,
    dkv_sib,
    sums,
    dk,
    dv,
):
    qb = query_rows(n)
    kb_rows = 2 * qb
    c = lax.rem(lax.axis_index("seq"), 2)
    lambda_value = lam[0]
    dk[...] = jnp.zeros_like(dk)
    dv[...] = jnp.zeros_like(dv)
    sums[...] = jnp.zeros_like(sums)

    def block(j):
        at = pl.ds(aligned(qb * j, qb), qb)
        pieces = []
        for i in range(qb // 32):
            run = order[j * (qb // 32) + i]
            b = pl.multiple_of(32 * lax.rem(run, 2), 32)
            pieces.append(grad[run // 2, pl.ds(b, 32), :])
        mixed_grad = jnp.concatenate(pieces, axis=0).astype(f32)
        mix_1, mix_2 = mix[0, at, :], mix[1, at, :]
        out = mix_1 - lambda_value * mix_2
        scale = rms_scale(out)
        sums[0:1, :] += jnp.sum(mixed_grad * out * scale, axis=0, keepdims=True) * (
            1.0 - lambda_init
        )
        heads_grad = rms_back(out, scale, gain[...], mixed_grad).astype(bf16)
        grad_f = heads_grad.astype(f32)
        dot_2 = grad_f * mix_2
        sums[1:2, :] += -jnp.sum(dot_2, axis=0, keepdims=True)
        delta_1 = jnp.sum(jnp.transpose(grad_f * mix_1), axis=0, keepdims=True)
        delta_2 = -lambda_value * jnp.sum(jnp.transpose(dot_2), axis=0, keepdims=True)
        q2 = two_maps(qs[at, :])
        lse_now = lse[j][0:1, :]
        q2_t = jnp.transpose(q2)
        grad_t = jnp.transpose(heads_grad)

        def piece(kb, acc, diagonal):
            here = pl.ds(aligned(kb_rows * kb, kb_rows), kb_rows)
            keys = ks[here, :]
            s = dot(keys, q2_t) - lse_now
            if diagonal:
                col = lax.rem(lax.broadcasted_iota(jnp.int32, s.shape, 1), qb)
                allowed = (
                    lax.broadcasted_iota(jnp.int32, s.shape, 0)
                    <= 64 * (col // 32) + lax.rem(col, 32) + 32 * c
                )
                s = jnp.where(allowed, s, masked_score)
            prob = jnp.exp(s)
            prob_1, prob_2 = prob[:, :qb], prob[:, qb:]
            value_dot = dot(vs[here, :], grad_t)
            grads = jnp.concatenate(
                [
                    (prob_1 * (value_dot - delta_1)).astype(bf16),
                    (prob_2 * (-lambda_value * value_dot - delta_2)).astype(bf16),
                ],
                axis=1,
            )
            dv[here, :] += dot((prob_1 - lambda_value * prob_2).astype(bf16), heads_grad)
            dk[here, :] += dot(grads, q2)
            return acc + dot_tn(keys, grads)

        acc = fold(
            n, j, lambda kb, a: piece(kb, a, False), jnp.zeros((VW, 2 * qb), f32)
        )
        acc = jnp.transpose(piece(j, acc, True))
        lane = lax.broadcasted_iota(jnp.int32, (qb, VW), 1)
        done = (jnp.where(lane < HALF, acc[:qb], acc[qb:]) * 0.125).astype(bf16)
        for i in range(qb // 32):
            run = order[j * (qb // 32) + i]
            b = pl.multiple_of(32 * lax.rem(run, 2), 32)
            dq[run // 2, pl.ds(b, 32), :] = done[32 * i : 32 * i + 32]

    spans(n, n * 64 // qb, block)

    def unsort(p):
        run = order[p]
        b = pl.multiple_of(32 * lax.rem(run, 2), 32)
        low = pl.multiple_of(64 * p + 32 * c, 32)
        high = pl.multiple_of(64 * p + 32 * (1 - c), 32)
        dkv[run // 2, pl.ds(b, 32), :VW] = dk[pl.ds(low, 32), :]
        dkv[run // 2, pl.ds(b, 32), VW:] = dv[pl.ds(low, 32), :]
        dkv_sib[run // 2, pl.ds(b, 32), :VW] = dk[pl.ds(high, 32), :].astype(bf16)
        dkv_sib[run // 2, pl.ds(b, 32), VW:] = dv[pl.ds(high, 32), :].astype(bf16)

    loop(2 * n, unsort)


def attend_back(place, lam, grad, saved, gain):
    n = place.n
    rows = 64 * n
    qb = query_rows(n)
    return pl.pallas_call(
        functools.partial(bwd_kernel, n),
        out_shape=[
            jax.ShapeDtypeStruct((n, 64, VW), bf16),
            jax.ShapeDtypeStruct((n, 64, 2 * VW), f32),
            jax.ShapeDtypeStruct((n, 64, 2 * VW), bf16),
            jax.ShapeDtypeStruct((8, VW), f32),
        ],
        in_specs=[SMEM] + [VMEM] * 6 + [SMEM, VMEM],
        out_specs=[VMEM] * 4,
        scratch_shapes=[pltpu.VMEM((2 * rows, VW), f32)] * 2,
        compiler_params=pltpu.CompilerParams(vmem_limit_bytes=vmem_cap),
        cost_estimate=busy(35),
    )(lam, grad, *saved, gain)


def swap_halves(rows):
    count, width = rows.shape
    return rows.reshape(2, 2, count // 4, width).transpose(1, 0, 2, 3).reshape(count, width)


def body(
    place,
    inputs,
    positions,
    attn_gain,
    w_query,
    w_key,
    w_value,
    w_out,
    lambda_params,
    sub_gain,
    ffn_gain,
    w_gate,
    w_up,
    w_down,
    cotangent,
):
    n, tp, seq = place.n, place.tp, place.seq
    s, t, core, head, active = place.me()
    inputs, cotangent = swap_halves(inputs), swap_halves(cotangent)
    row_count, width = inputs.shape
    half = row_count // 2
    part = width // n
    inputs_f = inputs.astype(f32)
    attn_scale = rms_scale(inputs_f)
    first_exp = jnp.exp(jnp.sum(lambda_params[0] * lambda_params[1]))
    second_exp = jnp.exp(jnp.sum(lambda_params[2] * lambda_params[3]))
    lambda_value = first_exp - second_exp + lambda_init
    lam = lambda_value.reshape(1)

    weights = (w_query, w_key, w_value)
    gain_row = attn_gain.reshape(1, width)
    if tp == 4:
        rows_all, pos, qkv = gather_all(
            place, inputs, positions.reshape(1, row_count), gain_row, weights, 1
        )
    else:
        rows_all, pos, qkv = gather_all_plain(
            place, inputs, positions.reshape(1, row_count), gain_row, weights
        )
    cotangent_late, pos = lax.optimization_barrier((cotangent, pos))
    cotangent_all = lax.all_gather(cotangent_late, "tp", axis=0, tiled=True)
    head_gain = (sub_gain * (1.0 - lambda_init)).reshape(1, VW)
    mixed, *saved = attend(place, pos.reshape(n, row_count), lam, qkv, head_gain)
    parts, mixed_all, hidden, middle, middle_grad, branch_grad, mixed_grad, ffn_gain_part = (
        feed_forward(
            place,
            mixed,
            rows_all,
            cotangent_all.reshape(tp, row_count, width),
            ffn_gain.reshape(1, width),
            w_out,
            w_gate,
            w_up,
            w_down,
            2,
        )
    )
    mixed_all = mixed_all.reshape(tp * row_count, HW)
    hidden_width = hidden.shape[2]

    def scatter_rows(array):
        return lax.psum_scatter(array, "seq", scatter_dimension=0, tiled=True)

    ffn_grads = scatter_rows(parts)

    def head_block(x, h, c):
        return x.at[
            pl.ds(pl.multiple_of(half * c, half), half), pl.ds(pl.multiple_of(VW * h, VW), VW)
        ]

    def ffn_result(given, made, rest):
        hid, weight = given
        (out,) = made
        for i in range(tp):
            out[i] = dot(hid[i], weight[...]).astype(bf16)

    grad_heads, ffn_out = moves(
        place,
        [Dispatch(place, head_block)],
        [mixed_grad],
        [(n, half, VW)],
        4,
        20,
        work=ffn_result,
        operands=[(hidden, VMEM), (w_down, VMEM)],
        results=[(jax.ShapeDtypeStruct((tp, row_count, width), bf16), VMEM)],
    )
    dq, dkv, dkv_sib, sums = attend_back(place, lam, grad_heads, saved, head_gain)
    normed_grad, weight_half, branch_all = finish_heads(
        place,
        dq,
        dkv,
        dkv_sib,
        rows_all,
        gain_row,
        weights,
        branch_grad,
        5,
    )
    out_part = dot_tn(mixed_all, branch_all.reshape(tp * row_count, width)).astype(bf16)
    out_part = lax.dynamic_index_in_dim(
        out_part.reshape(seq, tp, part, width), t, 1, keepdims=False
    ).reshape(seq * part, width)
    out_part, ffn_grads = lax.optimization_barrier((out_part, ffn_grads))

    attn_gain_part = jnp.sum(normed_grad * inputs_f * attn_scale, axis=0)
    input_grad = middle_grad + rms_back(inputs_f, attn_scale, attn_gain, normed_grad)

    sums = jnp.where(active, sums, 0.0)
    pad = ((0, 0), (0, 128 - part))
    small = jnp.stack(
        [
            jnp.pad(attn_gain_part.reshape(n, part), pad),
            jnp.pad(ffn_gain_part.reshape(n, part), pad),
            jnp.broadcast_to(sums[0], (n, VW)),
            jnp.broadcast_to(sums[1], (n, VW)),
        ]
        + [jnp.zeros((n, VW), f32)] * 4,
        axis=1,
    )
    small, out_part = lax.optimization_barrier((small, out_part))
    weight_rows, small_all, out_parts = moves(
        place,
        [
            Collect(place, lambda o, t, h, c: o.at[h], True),
            Everyone(place, False),
            Group(place, False),
        ],
        [weight_half.reshape(n // 2, part, 3 * VW), small, ffn_out],
        [(H, part, 3 * VW), (n, 8, VW), (tp, row_count, width)],
        6,
        20,
    )
    output = (middle + jnp.sum(out_parts.astype(f32), axis=0)).astype(bf16)
    out_grad = scatter_rows(out_part).astype(f32)
    ffn_grads = ffn_grads.astype(f32)
    down_grad = ffn_grads[:, :hidden_width].T
    gate_grad = ffn_grads[:, hidden_width : 2 * hidden_width]
    up_grad = ffn_grads[:, 2 * hidden_width :]
    weight_rows = weight_rows.astype(f32).reshape(H, part, 3, VW).transpose(2, 1, 0, 3)
    weight_rows = weight_rows.reshape(3, part, HW)
    small_sum = jnp.sum(small_all, axis=0)
    lambda_total = jnp.sum(small_sum[3])
    lambda_grads = jnp.stack(
        [
            lambda_total * first_exp * lambda_params[1],
            lambda_total * first_exp * lambda_params[0],
            -lambda_total * second_exp * lambda_params[3],
            -lambda_total * second_exp * lambda_params[2],
        ]
    )
    lambda_norm = jnp.sqrt(jnp.sum(lambda_grads * lambda_grads))
    output, input_grad = swap_halves(output), swap_halves(input_grad)
    return (
        output,
        input_grad,
        small_sum[0, :part],
        weight_rows[0],
        weight_rows[1],
        weight_rows[2],
        out_grad,
        lambda_grads,
        small_sum[2],
        small_sum[1, :part],
        gate_grad,
        up_grad,
        down_grad,
        lambda_total,
        lambda_norm,
    )


def solution(mesh):
    place = Place(mesh.shape["seq"], mesh.shape["tp"])
    both = ("seq", "tp")
    placed = (
        P(both, None),
        P(both),
        P(),
        P(),
        P(),
        P(),
        P(),
        P(),
        P(),
        P(),
        P(None, "tp"),
        P(None, "tp"),
        P("tp", None),
        P(both, None),
    )
    return jax.shard_map(
        functools.partial(body, place),
        mesh=mesh,
        in_specs=placed,
        out_specs=(
            P(both, None),
            P(both, None),
            P(both),
            P(both, None),
            P(both, None),
            P(both, None),
            P(both, None),
            P(),
            P(),
            P(both),
            P("seq", "tp"),
            P("seq", "tp"),
            P("tp", "seq"),
            P(),
            P(),
        ),
        check_vma=False,
    )
```

```python
import functools
import math

import jax
import jax.numpy as jnp
from jax import lax
from jax.experimental import pallas as pl
from jax.experimental.pallas import tpu as pltpu
from jax.sharding import PartitionSpec as P

H = 12
HALF = 64
VW = 128
HW = 1536

eps = 1e-05
lambda_init = 0.8 - 0.6 * math.exp(-3.3)
masked_score = -1e30
MESH = pl.DeviceIdType.MESH
ANY = pl.BlockSpec(memory_space=pl.ANY)
VMEM = pl.BlockSpec(memory_space=pltpu.VMEM)
SMEM = pl.BlockSpec(memory_space=pltpu.SMEM)
bf16 = jnp.bfloat16
f32 = jnp.float32
vmem_cap = 60 * 1024 * 1024


def dot(left, right):
    return jnp.dot(left, right, preferred_element_type=f32)


def dot_tn(left, right):
    return lax.dot_general(left, right, (((0,), (0,)), ((), ())), preferred_element_type=f32)


def dot_nt(left, right):
    return lax.dot_general(left, right, (((1,), (1,)), ((), ())), preferred_element_type=f32)


def rms_scale(values):
    return lax.rsqrt(jnp.mean(values * values, axis=-1, keepdims=True) + eps)


def rms_back(values, inv_rms, gain_vec, upstream):
    weighted = upstream * gain_vec
    inner_mean = jnp.mean(weighted * values, axis=-1, keepdims=True)
    return inv_rms * weighted - values * (inv_rms * inv_rms * inv_rms) * inner_mean


class Place:
    def __init__(self, seq, tp):
        self.seq, self.tp, self.n = seq, tp, seq * tp
        self.per = -(-H // (seq // 2))
        assert self.per <= tp and seq % 2 == 0

    def me(self):
        s, t = lax.axis_index("seq"), lax.axis_index("tp")
        head = (s // 2) * self.per + t
        active = jnp.logical_and(t < self.per, head < H)
        return s, t, lax.rem(s, 2), head, active

    def head_device(self, index):
        head, core = index // 2, lax.rem(index, 2)
        return 2 * (head // self.per) + core, lax.rem(head, self.per)

    def device(self, linear):
        return linear // self.tp, lax.rem(linear, self.tp)


def busy(microseconds):
    return pl.CostEstimate(
        flops=int(microseconds * 1e9), bytes_accessed=int(microseconds * 3e6), transcendentals=0
    )


def remote(src, dst, send, recv, where):
    return pltpu.make_async_remote_copy(
        src_ref=src, dst_ref=dst, send_sem=send, recv_sem=recv, device_id=where, device_id_type=MESH
    )


def loop(count, step):
    def one(k, carry):
        step(k)
        return carry

    lax.fori_loop(0, count, one, 0)


class Dispatch:
    def __init__(self, place, cut):
        self.p, self.cut = place, cut
        self.sems = [2 * H, place.n, 1]

    def start_one(self, index, x, o, send, recv, here):
        p = self.p
        s, t, c, head, active = p.me()
        lin = s * p.tp + t
        ds, dt = p.head_device(index)
        mine = jnp.logical_and(ds == s, dt == t)
        source = self.cut(x, index // 2, lax.rem(index, 2))

        @pl.when(jnp.logical_not(mine))
        def _():
            remote(source, o.at[lin], send.at[index], recv.at[lin], (ds, dt)).start()

        @pl.when(mine)
        def _():
            pltpu.make_async_copy(source, o.at[lin], here.at[0]).start()

    def start(self, *refs):
        p = self.p
        lin = lax.axis_index("seq") * p.tp + lax.axis_index("tp")
        loop(2 * H, lambda k: self.start_one(lax.rem(k + lin, 2 * H), *refs))

    def finish(self, x, o, send, recv, here, arrived=None):
        p = self.p
        s, t, c, head, active = p.me()
        lin = s * p.tp + t

        @pl.when(active)
        def _():
            pltpu.make_async_copy(self.cut(x, head, c), o.at[lin], here.at[0]).wait()
            if arrived is not None:
                arrived(lin)

            def got(k):
                other = lax.rem(lin + 1 + k, p.n)
                remote(o.at[other], o.at[other], send.at[0], recv.at[other], (s, t)).wait_recv()
                if arrived is not None:
                    arrived(other)

            loop(p.n - 1, got)

        def sent(k):
            ds, dt = p.head_device(k)

            @pl.when(jnp.logical_not(jnp.logical_and(ds == s, dt == t)))
            def _():
                remote(
                    self.cut(x, k // 2, lax.rem(k, 2)), o.at[0], send.at[k], recv.at[0], (ds, dt)
                ).wait_send()

        loop(2 * H, sent)


class Collect:
    def __init__(self, place, into, halves=False):
        self.p, self.into, self.halves = place, into, halves
        self.sems = [place.n, 2 * H, 1]

    def start(self, x, o, send, recv, here):
        p = self.p
        s, t, c, head, active = p.me()
        lin = s * p.tp + t
        count = p.n // 2 if self.halves else p.n

        @pl.when(active)
        def _():
            def step(k):
                slot = lax.rem(k + lin, count)
                other = slot + c * count if self.halves else slot
                into = self.into(o, lax.rem(other, p.tp), head, c)

                @pl.when(other != lin)
                def _():
                    remote(
                        x.at[slot], into, send.at[slot], recv.at[head * 2 + c], p.device(other)
                    ).start()

                @pl.when(other == lin)
                def _():
                    pltpu.make_async_copy(x.at[slot], into, here.at[0]).start()

            loop(count, step)

    def got(self, index, x, o, send, recv, here):
        p = self.p
        s, t = lax.axis_index("seq"), lax.axis_index("tp")
        into = self.into(o, t, index // 2, lax.rem(index, 2))
        ds, dt = p.head_device(index)
        mine = jnp.logical_and(ds == s, dt == t)

        @pl.when(jnp.logical_not(mine))
        def _():
            remote(into, into, send.at[0], recv.at[index], (s, t)).wait_recv()

        @pl.when(mine)
        def _():
            pltpu.make_async_copy(x.at[0], into, here.at[0]).wait()

    def sent(self, x, o, send, recv, here):
        p = self.p
        s, t, c, head, active = p.me()
        lin = s * p.tp + t
        count = p.n // 2 if self.halves else p.n

        @pl.when(active)
        def _():
            def one(k):
                other = k + c * count if self.halves else k

                @pl.when(other != lin)
                def _():
                    remote(
                        x.at[k], x.at[k], send.at[k], recv.at[0], p.device(other)
                    ).wait_send()

            loop(count, one)

    def finish(self, *refs):
        p = self.p
        if self.halves:
            lin = lax.axis_index("seq") * p.tp + lax.axis_index("tp")
            half = lin // (p.n // 2)
            loop(H, lambda k: self.got(2 * k + half, *refs))
        else:
            loop(2 * H, lambda k: self.got(k, *refs))
        self.sent(*refs)


class Everyone:
    def __init__(self, place, whole):
        self.p, self.whole = place, whole
        self.sems = [place.n, place.n, 1]

    def start(self, x, o, send, recv, here):
        p = self.p
        s, t = lax.axis_index("seq"), lax.axis_index("tp")
        lin = s * p.tp + t
        pltpu.make_async_copy(x if self.whole else x.at[lin], o.at[lin], here.at[0]).start()

        def step(k):
            other = lax.rem(lin + 1 + k, p.n)
            remote(
                x if self.whole else x.at[other],
                o.at[lin],
                send.at[other],
                recv.at[lin],
                p.device(other),
            ).start()

        loop(p.n - 1, step)

    def finish(self, x, o, send, recv, here):
        p = self.p
        s, t = lax.axis_index("seq"), lax.axis_index("tp")
        lin = s * p.tp + t
        pltpu.make_async_copy(x if self.whole else x.at[lin], o.at[lin], here.at[0]).wait()

        def done(k):
            other = lax.rem(lin + 1 + k, p.n)
            both = remote(
                x if self.whole else x.at[other],
                o.at[other],
                send.at[other],
                recv.at[other],
                p.device(other),
            )
            both.wait_recv()
            both.wait_send()

        loop(p.n - 1, done)


class Group:
    def __init__(self, place, whole):
        self.p, self.whole = place, whole
        self.sems = [place.tp, place.tp, 1]

    def start(self, x, o, send, recv, here):
        p = self.p
        s, t = lax.axis_index("seq"), lax.axis_index("tp")
        pltpu.make_async_copy(x if self.whole else x.at[t], o.at[t], here.at[0]).start()
        for k in range(1, p.tp):
            other = lax.rem(t + k, p.tp)
            remote(
                x if self.whole else x.at[other], o.at[t], send.at[other], recv.at[t], (s, other)
            ).start()

    def finish(self, x, o, send, recv, here):
        p = self.p
        s, t = lax.axis_index("seq"), lax.axis_index("tp")
        pltpu.make_async_copy(x if self.whole else x.at[t], o.at[t], here.at[0]).wait()
        for k in range(1, p.tp):
            other = lax.rem(t + k, p.tp)
            both = remote(
                x if self.whole else x.at[other],
                o.at[other],
                send.at[other],
                recv.at[other],
                (s, other),
            )
            both.wait_recv()
            both.wait_send()


class Along:
    def __init__(self, place):
        self.depth = place.seq // 2
        self.sems = [self.depth, self.depth, 1]

    def start(self, x, o, send, recv, here):
        s, t = lax.axis_index("seq"), lax.axis_index("tp")
        z, c = s // 2, lax.rem(s, 2)
        pltpu.make_async_copy(x.at[z], o.at[z], here.at[0]).start()

        def step(k):
            other = lax.rem(z + 1 + k, self.depth)
            remote(x.at[other], o.at[z], send.at[other], recv.at[z], (2 * other + c, t)).start()

        loop(self.depth - 1, step)

    def finish(self, x, o, send, recv, here):
        s, t = lax.axis_index("seq"), lax.axis_index("tp")
        z, c = s // 2, lax.rem(s, 2)
        pltpu.make_async_copy(x.at[z], o.at[z], here.at[0]).wait()

        def done(k):
            other = lax.rem(z + 1 + k, self.depth)
            both = remote(
                x.at[other], o.at[other], send.at[other], recv.at[other], (2 * other + c, t)
            )
            both.wait_recv()
            both.wait_send()

        loop(self.depth - 1, done)


def greet(place):
    s, t = lax.axis_index("seq"), lax.axis_index("tp")
    lin = s * place.tp + t
    barrier = pltpu.get_barrier_semaphore()

    def hello(k):
        pl.semaphore_signal(
            barrier,
            inc=1,
            device_id=place.device(lax.rem(lin + 1 + k, place.n)),
            device_id_type=MESH,
        )

    loop(place.n - 1, hello)
    pl.semaphore_wait(barrier, place.n - 1)


def moves(place, parts, arrays, outs, ident, cost, work=None, operands=(), results=(), scratch=()):
    count, extra = len(parts), len(operands)

    def kernel(*refs):
        ins, given = refs[:count], refs[count : count + extra]
        refs = refs[count + extra :]
        into, made = refs[:count], refs[count : count + len(results)]
        refs = refs[count + len(results) :]
        sems, rest = refs[: 3 * count], refs[3 * count :]
        greet(place)
        for i, part in enumerate(parts):
            part.start(ins[i], into[i], *sems[3 * i : 3 * i + 3])
        if work is not None:
            work(given, made, rest)
        for i, part in enumerate(parts):
            part.finish(ins[i], into[i], *sems[3 * i : 3 * i + 3])

    return pl.pallas_call(
        kernel,
        out_shape=[jax.ShapeDtypeStruct(s, a.dtype) for s, a in zip(outs, arrays)]
        + [shape for shape, spec in results],
        in_specs=[ANY] * count + [spec for array, spec in operands],
        out_specs=[ANY] * count + [spec for shape, spec in results],
        scratch_shapes=[pltpu.SemaphoreType.DMA((k,)) for part in parts for k in part.sems]
        + list(scratch),
        compiler_params=pltpu.CompilerParams(
            collective_id=ident, has_side_effects=True, vmem_limit_bytes=vmem_cap
        ),
        cost_estimate=busy(cost),
    )(*arrays, *[array for array, spec in operands])


def gather_all(place, rows, run_pos, gain, weights, ident):
    n, tp, depth = place.n, place.tp, place.seq // 2
    count, width = rows.shape
    half = count // 2
    tell = Everyone(place, True)

    def relay(first, use, x, o, full, halves, z_up, z_down, by_x, by_y, half_x, half_y, across, here):
        s, t = lax.axis_index("seq"), lax.axis_index("tp")
        z, c = s // 2, lax.rem(s, 2)
        t_x = t + 1 - 2 * lax.rem(t, 2)
        t_y = lax.rem(t + 2, 4)
        t_d = t_x + 2 - 4 * (t_x // 2)

        def slot(zs, core, ts):
            return (2 * zs + core) * tp + ts

        def line(zs, source, step):
            at = slot(zs, c, t)
            sem = z_up if step > 0 else z_down
            return remote(source, o.at[at], sem.at[zs], full.at[at], (s + 2 * step, t))

        def side(zs, source, sem, ts):
            at = slot(zs, c, t)
            return remote(source, o.at[at], sem.at[zs], full.at[at], (s, ts))

        def other_core(zs, ts, source):
            at = slot(zs, c, ts)
            return remote(
                source, o.at[at], across.at[zs * tp + ts], full.at[at], (s + 1 - 2 * c, t)
            )

        def corner(zs, ts, low, sem, to):
            at = slot(zs, c, ts)
            part = o.at[at, low : low + half]
            return remote(
                part, part, sem.at[zs], halves.at[2 * at + low // half], (s, to)
            )

        def arrived(at):
            remote(o.at[at], o.at[at], here.at[0], full.at[at], (s, t)).wait_recv()

        def push(zs, source):
            @pl.when(jnp.logical_and(zs <= z, z < depth - 1))
            def _():
                line(zs, source, 1).start()

            @pl.when(jnp.logical_and(zs >= z, z > 0))
            def _():
                line(zs, source, -1).start()

            side(zs, source, by_x, t_x).start()
            side(zs, source, by_y, t_y).start()
            other_core(zs, t, source).start()

        def each(k, act):
            def one(sign):
                zs = z + (2 * sign - 1) * k
                valid = jnp.logical_and(zs >= 0, zs < depth)
                valid = jnp.logical_and(valid, jnp.logical_and(k >= 0, k + 1 > sign))

                @pl.when(valid)
                def _():
                    act(zs)

            loop(2, one)

        def from_line(zs):
            arrived(slot(zs, c, t))
            push(zs, o.at[slot(zs, c, t)])

        def from_sides(zs):
            arrived(slot(zs, c, t_x))
            corner(zs, t_x, 0, half_y, t_y).start()
            other_core(zs, t_x, o.at[slot(zs, c, t_x)]).start()
            arrived(slot(zs, c, t_y))
            corner(zs, t_y, half, half_x, t_x).start()
            other_core(zs, t_y, o.at[slot(zs, c, t_y)]).start()

        def from_corner(zs):
            at = slot(zs, c, t_d)
            for low in (0, half):
                part = o.at[at, low : low + half]
                remote(
                    part, part, here.at[0], halves.at[2 * at + low // half], (s, t)
                ).wait_recv()
            other_core(zs, t_d, o.at[at]).start()

        keep = pltpu.make_async_copy(x, o.at[slot(z, c, t)], here.at[0])
        keep.start()
        push(z, x)
        first()
        keep.wait()

        def use_block(k):
            def one(i):
                other, v = i // 4, lax.rem(i, 4)
                m_x, m_y = lax.rem(v, 2), v // 2
                x_bit, y_bit = lax.rem(t, 2), t // 2
                ts = 2 * (y_bit + m_y - 2 * y_bit * m_y) + x_bit + m_x - 2 * x_bit * m_x
                core = c + other - 2 * c * other

                def act(zs):
                    at = slot(zs, core, ts)

                    @pl.when(other > 0)
                    def _():
                        arrived(at)

                    use(at)

                each(k - m_x - m_y - other, act)

            loop(8, one)

        def wave(k):
            @pl.when(k > 0)
            def _():
                each(k, from_line)
                each(k - 1, from_sides)
                each(k - 2, from_corner)

            use_block(k)

        loop(depth + 3, wave)

        def sent(k):
            zs = k
            at = slot(zs, c, t)

            @pl.when(jnp.logical_and(zs <= z, z < depth - 1))
            def _():
                line(zs, o.at[at], 1).wait_send()

            @pl.when(jnp.logical_and(zs >= z, z > 0))
            def _():
                line(zs, o.at[at], -1).wait_send()

            side(zs, o.at[at], by_x, t_x).wait_send()
            side(zs, o.at[at], by_y, t_y).wait_send()
            corner(zs, t_x, 0, half_y, t_y).wait_send()
            corner(zs, t_y, half, half_x, t_x).wait_send()
            for ts in range(tp):
                other_core(zs, ts, o.at[at]).wait_send()

        loop(depth, sent)

    sems = [n, 2 * n] + [depth] * 6 + [depth * tp, 1]

    def kernel(x, r, gain, wq, wk, wv, out, pos, qkv, o, out_sem, *refs):
        greet(place)

        def save(at):
            return pltpu.make_async_copy(o.at[at], out.at[at], out_sem.at[at])

        def use(at):
            save(at).start()
            x = o[at].astype(f32)
            x = (x * rms_scale(x) * gain[...]).astype(bf16)
            for i, w in enumerate((wq, wk, wv)):
                qkv[at, :, i * VW : (i + 1) * VW] = dot(x, w[...]).astype(bf16)

        relay(lambda: tell.start(r, pos, *refs[:3]), use, x, o, *refs[3:])
        tell.finish(r, pos, *refs[:3])
        loop(n, lambda k: save(k).wait())

    def column(g):
        s, t, c, head, active = place.me()
        return 0, jnp.minimum(head, H - 1)

    columns = pl.BlockSpec((width, VW), column)
    return pl.pallas_call(
        kernel,
        grid=(1,),
        out_shape=[
            jax.ShapeDtypeStruct((n,) + rows.shape, rows.dtype),
            jax.ShapeDtypeStruct((n,) + run_pos.shape, run_pos.dtype),
            jax.ShapeDtypeStruct((n, count, 3 * VW), bf16),
        ],
        in_specs=[ANY] * 2 + [VMEM] + [columns] * 3,
        out_specs=[ANY] * 2 + [VMEM],
        scratch_shapes=[
            pltpu.VMEM((n,) + rows.shape, rows.dtype),
            pltpu.SemaphoreType.DMA((n,)),
        ]
        + [pltpu.SemaphoreType.DMA((k,)) for k in tell.sems + sems],
        compiler_params=pltpu.CompilerParams(
            collective_id=ident, has_side_effects=True, vmem_limit_bytes=vmem_cap
        ),
        cost_estimate=busy(50),
    )(rows, run_pos, gain, *weights)


def gather_all_plain(place, rows, run_pos, gain, weights):
    axes = ("seq", "tp")
    rows_all = lax.all_gather(rows, axes, axis=0, tiled=False)
    pos = lax.all_gather(run_pos, axes, axis=0, tiled=False)
    x = rows_all.astype(f32)
    x = (x * rms_scale(x) * gain).astype(bf16)
    s, t, c, head, active = place.me()
    column = jnp.minimum(head, H - 1) * VW
    qkv = [
        dot(x, lax.dynamic_slice_in_dim(w, column, VW, 1)).astype(bf16) for w in weights
    ]
    return rows_all, pos, jnp.concatenate(qkv, axis=2)


def feed_forward(place, mixed, rows_all, cotangent_all, gain, w_out, w_gate, w_up, w_down, ident):
    n, tp, half = place.n, place.tp, mixed.shape[1]
    count, width = rows_all.shape[1:]
    hid = w_gate.shape[1]
    chunk = 256

    def into(o, t, h, c):
        return o.at[
            t,
            pl.ds(pl.multiple_of(half * c, half), half),
            pl.ds(pl.multiple_of(VW * h, VW), VW),
        ]

    back = Collect(place, into)

    def kernel(*refs):
        mixed, rows_all, cot, gain, wo_in, wg_in, wu_in, wd_in, *refs = refs
        parts, mixed_out, hidden, middle, middle_grad, branch, mixed_grad, gain_part, *refs = refs
        mixed_v, x_v, rows_v, gate_v, up_v, send_v, recv_v, own_part, held, *refs = refs
        wo, wg, wu, wd, *sems = refs
        share_send, share_recv, part_send, part_recv, w_sem, x_sem, out_sem, mixed_sem = sems[3:]
        s, t = lax.axis_index("seq"), lax.axis_index("tp")
        greet(place)
        back.start(mixed, mixed_v, *sems[:3])

        def fetch(m):
            return pltpu.make_async_copy(rows_all.at[s * tp + m], x_v.at[m], x_sem.at[m])

        loads = [
            pltpu.make_async_copy(a, b, w_sem.at[i])
            for i, (a, b) in enumerate(((wo_in, wo), (wg_in, wg), (wu_in, wu), (wd_in, wd)))
        ]
        loop(tp, lambda m: fetch(m).start())
        for load in loads:
            load.start()

        def share(k, c, slot):
            other = lax.rem(t + k, tp)
            at = slot(other)
            return remote(
                mixed_v.at[t, half * c : half * c + half, :],
                mixed_v.at[at, half * c : half * c + half, :],
                share_send.at[2 * other + c],
                share_recv.at[2 * at + c],
                (s, other),
            )

        def give(k, slot):
            other = lax.rem(t + k, tp)
            at = slot(other)
            return remote(
                send_v.at[other], recv_v.at[at], part_send.at[other], part_recv.at[at], (s, other)
            )

        for c in range(2):
            loop(H, lambda h: back.got(2 * h + c, mixed, mixed_v, *sems[:3]))
            for k in range(1, tp):
                share(k, c, lambda other: t).start()
        loop(tp, lambda m: fetch(m).wait())
        for load in loads:
            load.wait()

        def member(k):
            m = lax.rem(t + k, tp)

            @pl.when(k > 0)
            def _():
                for c in range(2):
                    share(k, c, lambda other: other).wait_recv()

            x = x_v[m].astype(f32) + dot(mixed_v[m], wo[...])
            rows = (x * rms_scale(x) * gain[...]).astype(bf16)
            rows_v[m] = rows
            gate = dot(rows, wg[...])
            up = dot(rows, wu[...])
            sig = jax.nn.sigmoid(gate)
            act = gate * sig
            hidden[m] = (act * up).astype(bf16)
            grad = dot_nt(cot[m], wd[...])
            gate_rows = (grad * up * sig * (1.0 + gate * (1.0 - sig))).astype(bf16)
            up_rows = (grad * act).astype(bf16)
            gate_v[m] = gate_rows
            up_v[m] = up_rows
            part = dot_nt(gate_rows, wg[...]) + dot_nt(up_rows, wu[...])

            @pl.when(k == 0)
            def _():
                own_part[...] = part
                middle[...] = x

            @pl.when(k > 0)
            def _():
                send_v[m] = part.astype(bf16)
                give(k, lambda other: t).start()

        loop(tp, member)
        keep = pltpu.make_async_copy(mixed_v, mixed_out, mixed_sem.at[0])
        keep.start()

        def copy(i):
            at = pl.ds(pl.multiple_of(chunk * i, chunk), chunk)
            return pltpu.make_async_copy(held.at[at], parts.at[at], out_sem.at[i])

        def weight_rows(i):
            at = pl.ds(pl.multiple_of(chunk * i, chunk), chunk)
            for k, (left, right) in enumerate(((cot, hidden), (rows_v, gate_v), (rows_v, up_v))):
                held[at, k * hid : (k + 1) * hid] = dot_tn(
                    left[:, :, at].reshape(tp * count, chunk), right[...].reshape(tp * count, hid)
                ).astype(bf16)
            copy(i).start()

        loop(width // chunk, weight_rows)
        total = own_part[...]
        for k in range(1, tp):
            give(k, lambda other: other).wait_recv()
            total = total + recv_v[lax.rem(t + k, tp)].astype(f32)
        mid = middle[...]
        scale = rms_scale(mid)
        gain_part[...] = jnp.sum(total * mid * scale, axis=0, keepdims=True)
        grad = cot[t].astype(f32) + rms_back(mid, scale, gain[...], total)
        middle_grad[...] = grad
        branch[...] = grad.astype(bf16)
        mixed_grad[...] = dot_nt(grad.astype(bf16), wo[...]).astype(bf16)
        loop(width // chunk, lambda i: copy(i).wait())
        keep.wait()
        for k in range(1, tp):
            give(k, lambda other: other).wait_send()
            for c in range(2):
                share(k, c, lambda other: other).wait_send()
        back.sent(mixed, mixed_v, *sems[:3])

    struct = jax.ShapeDtypeStruct
    group = (tp, count, width)
    return pl.pallas_call(
        kernel,
        out_shape=[
            struct((width, 3 * hid), bf16),
            struct(group, bf16),
            struct((tp, count, hid), bf16),
            struct((count, width), f32),
            struct((count, width), f32),
            struct((count, width), bf16),
            struct((count, width), bf16),
            struct((1, width), f32),
        ],
        in_specs=[ANY, ANY, VMEM, VMEM] + [ANY] * 4,
        out_specs=[ANY, ANY] + [VMEM] * 6,
        scratch_shapes=[
            pltpu.VMEM(group, bf16),
            pltpu.VMEM(group, bf16),
            pltpu.VMEM(group, bf16),
            pltpu.VMEM((tp, count, hid), bf16),
            pltpu.VMEM((tp, count, hid), bf16),
            pltpu.VMEM(group, bf16),
            pltpu.VMEM(group, bf16),
            pltpu.VMEM((count, width), f32),
            pltpu.VMEM((width, 3 * hid), bf16),
            pltpu.VMEM(w_out.shape, bf16),
            pltpu.VMEM(w_gate.shape, bf16),
            pltpu.VMEM(w_up.shape, bf16),
            pltpu.VMEM(w_down.shape, bf16),
        ]
        + [
            pltpu.SemaphoreType.DMA((k,))
            for k in back.sems + [2 * tp, 2 * tp, tp, tp, 4, tp, width // chunk, 1]
        ],
        compiler_params=pltpu.CompilerParams(
            collective_id=ident, has_side_effects=True, vmem_limit_bytes=vmem_cap
        ),
        cost_estimate=busy(60),
    )(mixed, rows_all, cotangent_all, gain, w_out, w_gate, w_up, w_down)


def finish_heads(
    place,
    dq,
    dkv,
    dkv_sib,
    rows_all,
    gain,
    weights,
    branch_grad,
    mixed_all,
    inputs,
    middle_grad,
    ident,
):
    n, half = place.n, dq.shape[1]
    width = rows_all.shape[2]
    part, chunk, depth = width // n, 256, place.seq // 2
    lot = 8 if n <= 64 else 2
    out_type = bf16 if part % 16 == 0 else f32

    def into(o, t, h, c):
        return o.at[
            pl.ds(pl.multiple_of(half * c, half), half),
            pl.ds(pl.multiple_of(3 * VW * h, 3 * VW), 3 * VW),
        ]

    back, share = Collect(place, into), Group(place, True)

    def kernel(*refs):
        dq, dkv, dkv_sib, rows_all, gain, *refs = refs
        weights, refs = refs[:3], refs[3:]
        branch, mixed_in, inputs, middle_grad, *refs = refs
        input_grad, gain_part, weight_half, out_own, *refs = refs
        other_dkv, grads, rows_back, raw, held, away, other, w_all, branch_all, mixed, *refs = refs
        out_part, out_away, out_other, *sems = refs
        s, t = lax.axis_index("seq"), lax.axis_index("tp")
        c = lax.rem(s, 2)
        send, recv, raw_sem, w_sem, mixed_sem = sems[6:]
        sibling = (s + 1 - 2 * c, t)
        greet(place)
        swap = remote(dkv_sib, other_dkv, send.at[0], recv.at[0], sibling)
        swap.start()

        def fetch(i):
            return pltpu.make_async_copy(
                rows_all.at[
                    pl.ds(lot * i, lot), pl.ds(pl.multiple_of(half * c, half), half), :
                ],
                raw.at[lax.rem(i, 2)],
                raw_sem.at[lax.rem(i, 2)],
            )

        fetch(0).start()
        loads = [
            pltpu.make_async_copy(w, w_all.at[i], w_sem.at[i]) for i, w in enumerate(weights)
        ]
        for load in loads:
            load.start()
        mixed_load = pltpu.make_async_copy(mixed_in, mixed, mixed_sem.at[0])
        mixed_load.start()
        swap.wait_recv()

        def join(i):
            grads[i, :, :VW] = dq[i]
            grads[i, :, VW:] = (dkv[i] + other_dkv[i].astype(f32)).astype(bf16)

        loop(n, join)
        back.start(grads, rows_back, *sems[:3])
        share.start(branch, branch_all, *sems[3:6])
        held[...] = jnp.zeros_like(held)

        def rows(i):
            @pl.when(i + 1 < n // lot)
            def _():
                fetch(i + 1).start()

            fetch(i).wait()
            x = raw[lax.rem(i, 2)].reshape(lot * half, width).astype(f32)
            x = (x * rms_scale(x) * gain[...]).astype(bf16)
            g = grads[pl.ds(lot * i, lot)].reshape(lot * half, 3 * VW)
            for k in range(width // chunk):
                held[k * chunk : (k + 1) * chunk, :] += dot_tn(
                    x[:, k * chunk : (k + 1) * chunk], g
                )

        loop(n // lot, rows)
        low = pl.multiple_of(c * (width // 2), width // 2)
        high = pl.multiple_of((1 - c) * (width // 2), width // 2)
        away[...] = held[pl.ds(high, width // 2), :].astype(bf16)
        cross = remote(away, other, send.at[1], recv.at[1], sibling)
        cross.start()
        mixed_load.wait()
        share.finish(branch, branch_all, *sems[3:6])

        def out_rows(i):
            at = pl.ds(pl.multiple_of(chunk * i, chunk), chunk)
            out_part[at, :] = dot_tn(
                mixed[:, :, at].reshape(-1, chunk), branch_all[...].reshape(-1, width)
            ).astype(out_type)

        loop(HW // chunk, out_rows)

        def out_picked(z, core):
            picked = jnp.zeros((part, width), f32)
            for k in range(2 * place.tp):
                low = part * (2 * place.tp * z + k)
                here = k == core * place.tp + t
                picked = picked + jnp.where(here, out_part[low : low + part, :], 0.0)
            return picked.astype(bf16)

        def out_block(z, core):
            if part % 16:
                return out_picked(z, core)
            base = part * (place.tp * (2 * z + core) + t)
            return out_part[pl.ds(pl.multiple_of(base, part), part), :].astype(bf16)

        for z in range(depth):
            out_away[z] = out_block(z, 1 - c)
        out_cross = remote(out_away, out_other, send.at[2], recv.at[2], sibling)
        out_cross.start()
        back.finish(grads, rows_back, *sems[:3])
        for load in loads:
            load.wait()
        total = None
        for h in range(0, H, 2):
            for i in range(3):
                at = (3 * h + i) * VW
                x = jnp.concatenate(
                    [rows_back[:, at : at + VW], rows_back[:, at + 3 * VW : at + 4 * VW]], axis=1
                )
                new = dot_nt(x, w_all[i, :, h * VW : (h + 2) * VW])
                total = new if total is None else total + new
        x = inputs[...].astype(f32)
        scale = rms_scale(x)
        gain_part[...] = jnp.sum(total * x * scale, axis=0, keepdims=True)
        done = middle_grad[...] + rms_back(x, scale, gain[...], total)
        quarter = half // 2
        for b in range(2):
            for h in range(2):
                to, from_ = (2 * b + h) * quarter, (2 * h + b) * quarter
                input_grad[to : to + quarter, :] = done[from_ : from_ + quarter]
        cross.wait_recv()
        weight_half[...] = (held[pl.ds(low, width // 2), :] + other[...].astype(f32)).astype(bf16)
        out_cross.wait_recv()
        for z in range(depth):
            out_own[z] = (out_block(z, c).astype(f32) + out_other[z].astype(f32)).astype(bf16)
        swap.wait_send()
        cross.wait_send()
        out_cross.wait_send()

    return pl.pallas_call(
        kernel,
        out_shape=[
            jax.ShapeDtypeStruct((2 * half, width), f32),
            jax.ShapeDtypeStruct((1, width), f32),
            jax.ShapeDtypeStruct((width // 2, 3 * VW), bf16),
            jax.ShapeDtypeStruct((depth, part, width), bf16),
        ],
        in_specs=[VMEM, VMEM, ANY, ANY, VMEM] + [ANY] * 5 + [VMEM] * 2,
        out_specs=[VMEM] * 4,
        scratch_shapes=[
            pltpu.VMEM((n, half, 2 * VW), bf16),
            pltpu.VMEM((n, half, 3 * VW), bf16),
            pltpu.VMEM((2 * half, 3 * HW), bf16),
            pltpu.VMEM((2, lot, half, width), bf16),
            pltpu.VMEM((width, 3 * VW), f32),
            pltpu.VMEM((width // 2, 3 * VW), bf16),
            pltpu.VMEM((width // 2, 3 * VW), bf16),
            pltpu.VMEM((3,) + weights[0].shape, bf16),
            pltpu.VMEM((place.tp,) + branch_grad.shape, bf16),
            pltpu.VMEM(mixed_all.shape, bf16),
            pltpu.VMEM((HW, width), out_type),
            pltpu.VMEM((depth, part, width), bf16),
            pltpu.VMEM((depth, part, width), bf16),
        ]
        + [pltpu.SemaphoreType.DMA((k,)) for k in back.sems + share.sems + [3, 3, 2, 3, 1]],
        compiler_params=pltpu.CompilerParams(
            collective_id=ident, has_side_effects=True, vmem_limit_bytes=vmem_cap
        ),
        cost_estimate=busy(40),
    )(
        dq,
        dkv,
        dkv_sib,
        rows_all,
        gain,
        *weights,
        branch_grad,
        mixed_all,
        inputs,
        middle_grad,
    )


def last_moves(place, weight_half, small, ffn_out, out_part, middle, ident):
    n, tp, seq = place.n, place.tp, place.seq
    count, width = middle.shape
    part = width // n
    kinds = [
        Collect(place, lambda o, t, h, c: o.at[h], True),
        Everyone(place, False),
        Group(place, False),
        Along(place),
    ]
    arrays = [weight_half, small, ffn_out, out_part]
    landing = [
        pltpu.VMEM((H, part, 3 * VW), bf16),
        pltpu.VMEM(small.shape, f32),
        pltpu.VMEM(ffn_out.shape, bf16),
        pltpu.VMEM(out_part.shape, bf16),
    ]

    def kernel(*refs):
        ins, middle, refs = refs[:4], refs[4], refs[5:]
        output, query_grad, key_grad, value_grad, out_grad, sums, *refs = refs
        lands, sems = refs[:4], refs[4:]
        greet(place)
        every = list(zip(kinds, ins, lands, [sems[3 * i : 3 * i + 3] for i in range(4)]))
        for kind, source, land, sem in every:
            kind.start(source, land, *sem)

        def finish(i):
            kind, source, land, sem = every[i]
            kind.finish(source, land, *sem)

        finish(1)
        sums[...] = jnp.sum(lands[1][...], axis=0)
        finish(2)
        total = middle[...]
        for m in range(tp):
            total = total + lands[2][m].astype(f32)
        total = total.astype(bf16)
        quarter = count // 4
        for b in range(2):
            for h in range(2):
                low, from_ = (2 * b + h) * quarter, (2 * h + b) * quarter
                output[low : low + quarter, :] = total[from_ : from_ + quarter]
        finish(0)
        for h in range(H):
            for i, grad in enumerate((query_grad, key_grad, value_grad)):
                grad[:, h * VW : (h + 1) * VW] = lands[0][h, :, i * VW : (i + 1) * VW].astype(f32)
        finish(3)
        total = lands[3][0].astype(f32)
        for m in range(1, seq // 2):
            total = total + lands[3][m].astype(f32)
        out_grad[...] = total

    struct = jax.ShapeDtypeStruct
    return pl.pallas_call(
        kernel,
        out_shape=[struct((count, width), bf16)]
        + [struct((part, HW), f32)] * 4
        + [struct((8, VW), f32)],
        in_specs=[ANY] * 4 + [VMEM],
        out_specs=[VMEM] * 6,
        scratch_shapes=landing
        + [pltpu.SemaphoreType.DMA((k,)) for kind in kinds for k in kind.sems],
        compiler_params=pltpu.CompilerParams(
            collective_id=ident, has_side_effects=True, vmem_limit_bytes=vmem_cap
        ),
        cost_estimate=busy(35),
    )(*arrays, middle)


def spans(n, count, step):
    if n <= 32:
        for j in range(count):
            step(j)
    else:
        loop(count, step)


def fold(n, count, step, carry):
    if n <= 32:
        for k in range(count):
            carry = step(k, carry)
        return carry
    return lax.fori_loop(0, count, step, carry)


def aligned(value, unit):
    return value if isinstance(value, int) else pl.multiple_of(value, unit)


def query_rows(n):
    return 256 if n <= 64 else 128


def two_maps(rows):
    lane = lax.broadcasted_iota(jnp.int32, rows.shape, 1)
    zero = jnp.zeros_like(rows)
    return jnp.concatenate(
        [jnp.where(lane < HALF, rows, zero), jnp.where(lane < HALF, zero, rows)], axis=0
    )


def fwd_kernel(n, pos, lam, qkv, gain, mixed, mix, lse, qs, ks, vs, order, score):
    qb = query_rows(n)
    kb_rows = 2 * qb
    c = lax.rem(lax.axis_index("seq"), 2)

    def place_run(run):
        order[pos[run // 2, lax.rem(run, 2) * 64] // 64] = run

    loop(2 * n, place_run)
    lambda_value = lam[0]

    def sort(p):
        run = order[p]
        i, b = run // 2, pl.multiple_of(32 * lax.rem(run, 2), 32)
        for h in range(2):
            at = pl.ds(pl.multiple_of(64 * p + 32 * h, 32), 32)
            rows = pl.ds(pl.multiple_of(64 * h + b, 32), 32)
            ks[at, :] = qkv[i, rows, VW : 2 * VW]
            vs[at, :] = qkv[i, rows, 2 * VW :]
        mine = qkv[i, pl.ds(pl.multiple_of(64 * c + b, 32), 32), :VW]
        qs[pl.ds(pl.multiple_of(32 * p, 32), 32), :] = mine * jnp.asarray(0.125, bf16)

    loop(2 * n, sort)

    def block(j):
        at = pl.ds(aligned(qb * j, qb), qb)
        q2 = two_maps(qs[at, :])

        def scores(kb):
            return dot_nt(q2, ks[pl.ds(aligned(kb_rows * kb, kb_rows), kb_rows), :])

        def lanes(top, s):
            for i in range(kb_rows // 128):
                top = jnp.maximum(top, s[:, 128 * i : 128 * i + 128])
            return top

        def first(kb, top):
            s = scores(kb)
            score[:, pl.ds(aligned(kb_rows * kb, kb_rows), kb_rows)] = s
            return lanes(top, s)

        top = fold(n, j, first, jnp.full((2 * qb, 128), masked_score, f32))
        s = scores(j)
        row = lax.broadcasted_iota(jnp.int32, s.shape, 0)
        row = lax.rem(row, qb)
        allowed = (
            lax.broadcasted_iota(jnp.int32, s.shape, 1)
            <= 64 * (row // 32) + lax.rem(row, 32) + 32 * c
        )
        s = jnp.where(allowed, s, masked_score)
        score[:, pl.ds(aligned(kb_rows * j, kb_rows), kb_rows)] = s
        high = jnp.max(lanes(top, s), axis=1, keepdims=True)
        ones = jnp.ones((kb_rows, VW), bf16)

        def second(kb, acc):
            here = pl.ds(aligned(kb_rows * kb, kb_rows), kb_rows)
            weights = jnp.exp(score[:, here] - high).astype(bf16)
            return acc + dot(weights, jnp.concatenate([vs[here, :], ones], axis=1))

        acc = fold(n, j + 1, second, jnp.zeros((2 * qb, 2 * VW), f32))
        total = acc[:, VW:]
        mixes = acc[:, :VW] / total
        lse[j] = jnp.transpose(high + jnp.log(total))[:8, :]
        mix[0, at, :] = mixes[:qb]
        mix[1, at, :] = mixes[qb:]
        out = mixes[:qb] - lambda_value * mixes[qb:]
        out = (out * rms_scale(out) * gain[...]).astype(bf16)
        for i in range(qb // 32):
            run = order[j * (qb // 32) + i]
            b = pl.multiple_of(32 * lax.rem(run, 2), 32)
            mixed[run // 2, pl.ds(b, 32), :] = out[32 * i : 32 * i + 32]

    spans(n, n * 64 // qb, block)


def attend(place, pos, lam, qkv, gain):
    n = place.n
    rows = 64 * n
    qb = query_rows(n)
    return pl.pallas_call(
        functools.partial(fwd_kernel, n),
        out_shape=[
            jax.ShapeDtypeStruct((n, 64, VW), bf16),
            jax.ShapeDtypeStruct((2, rows, VW), f32),
            jax.ShapeDtypeStruct((rows // qb, 8, 2 * qb), f32),
            jax.ShapeDtypeStruct((rows, VW), bf16),
            jax.ShapeDtypeStruct((2 * rows, VW), bf16),
            jax.ShapeDtypeStruct((2 * rows, VW), bf16),
            jax.ShapeDtypeStruct((2 * n,), jnp.int32),
        ],
        in_specs=[SMEM, SMEM, VMEM, VMEM],
        out_specs=[VMEM] * 6 + [SMEM],
        scratch_shapes=[pltpu.VMEM((2 * qb, 2 * rows), f32)],
        compiler_params=pltpu.CompilerParams(vmem_limit_bytes=vmem_cap),
        cost_estimate=busy(20),
    )(pos, lam, qkv, gain)


def bwd_kernel(
    n,
    lam,
    grad,
    mix,
    lse,
    qs,
    ks,
    vs,
    order,
    gain,
    dq,
    dkv,
    dkv_sib,
    sums,
    dk,
    dv,
):
    qb = query_rows(n)
    kb_rows = 2 * qb
    c = lax.rem(lax.axis_index("seq"), 2)
    lambda_value = lam[0]
    dk[...] = jnp.zeros_like(dk)
    dv[...] = jnp.zeros_like(dv)
    sums[...] = jnp.zeros_like(sums)

    def block(j):
        at = pl.ds(aligned(qb * j, qb), qb)
        pieces = []
        for i in range(qb // 32):
            run = order[j * (qb // 32) + i]
            b = pl.multiple_of(32 * lax.rem(run, 2), 32)
            pieces.append(grad[run // 2, pl.ds(b, 32), :])
        mixed_grad = jnp.concatenate(pieces, axis=0).astype(f32)
        mix_1, mix_2 = mix[0, at, :], mix[1, at, :]
        out = mix_1 - lambda_value * mix_2
        scale = rms_scale(out)
        sums[0:1, :] += jnp.sum(mixed_grad * out * scale, axis=0, keepdims=True) * (
            1.0 - lambda_init
        )
        heads_grad = rms_back(out, scale, gain[...], mixed_grad).astype(bf16)
        grad_f = heads_grad.astype(f32)
        dot_2 = grad_f * mix_2
        sums[1:2, :] += -jnp.sum(dot_2, axis=0, keepdims=True)
        delta_1 = jnp.sum(jnp.transpose(grad_f * mix_1), axis=0, keepdims=True)
        delta_2 = -lambda_value * jnp.sum(jnp.transpose(dot_2), axis=0, keepdims=True)
        q2 = two_maps(qs[at, :])
        lse_now = lse[j][0:1, :]
        q2_t = jnp.transpose(q2)
        grad_t = jnp.transpose(heads_grad)

        def piece(kb, acc, diagonal):
            here = pl.ds(aligned(kb_rows * kb, kb_rows), kb_rows)
            keys = ks[here, :]
            s = dot(keys, q2_t) - lse_now
            if diagonal:
                col = lax.rem(lax.broadcasted_iota(jnp.int32, s.shape, 1), qb)
                allowed = (
                    lax.broadcasted_iota(jnp.int32, s.shape, 0)
                    <= 64 * (col // 32) + lax.rem(col, 32) + 32 * c
                )
                s = jnp.where(allowed, s, masked_score)
            prob = jnp.exp(s)
            prob_1, prob_2 = prob[:, :qb], prob[:, qb:]
            value_dot = dot(vs[here, :], grad_t)
            grads = jnp.concatenate(
                [
                    (prob_1 * (value_dot - delta_1)).astype(bf16),
                    (prob_2 * (-lambda_value * value_dot - delta_2)).astype(bf16),
                ],
                axis=1,
            )
            dv[here, :] += dot((prob_1 - lambda_value * prob_2).astype(bf16), heads_grad)
            dk[here, :] += dot(grads, q2)
            return acc + dot_tn(keys, grads)

        acc = fold(
            n, j, lambda kb, a: piece(kb, a, False), jnp.zeros((VW, 2 * qb), f32)
        )
        acc = jnp.transpose(piece(j, acc, True))
        lane = lax.broadcasted_iota(jnp.int32, (qb, VW), 1)
        done = (jnp.where(lane < HALF, acc[:qb], acc[qb:]) * 0.125).astype(bf16)
        for i in range(qb // 32):
            run = order[j * (qb // 32) + i]
            b = pl.multiple_of(32 * lax.rem(run, 2), 32)
            dq[run // 2, pl.ds(b, 32), :] = done[32 * i : 32 * i + 32]

    spans(n, n * 64 // qb, block)

    def unsort(p):
        run = order[p]
        b = pl.multiple_of(32 * lax.rem(run, 2), 32)
        low = pl.multiple_of(64 * p + 32 * c, 32)
        high = pl.multiple_of(64 * p + 32 * (1 - c), 32)
        dkv[run // 2, pl.ds(b, 32), :VW] = dk[pl.ds(low, 32), :]
        dkv[run // 2, pl.ds(b, 32), VW:] = dv[pl.ds(low, 32), :]
        dkv_sib[run // 2, pl.ds(b, 32), :VW] = dk[pl.ds(high, 32), :].astype(bf16)
        dkv_sib[run // 2, pl.ds(b, 32), VW:] = dv[pl.ds(high, 32), :].astype(bf16)

    loop(2 * n, unsort)


def attend_back(place, lam, grad, saved, gain):
    n = place.n
    rows = 64 * n
    qb = query_rows(n)
    return pl.pallas_call(
        functools.partial(bwd_kernel, n),
        out_shape=[
            jax.ShapeDtypeStruct((n, 64, VW), bf16),
            jax.ShapeDtypeStruct((n, 64, 2 * VW), f32),
            jax.ShapeDtypeStruct((n, 64, 2 * VW), bf16),
            jax.ShapeDtypeStruct((8, VW), f32),
        ],
        in_specs=[SMEM] + [VMEM] * 6 + [SMEM, VMEM],
        out_specs=[VMEM] * 4,
        scratch_shapes=[pltpu.VMEM((2 * rows, VW), f32)] * 2,
        compiler_params=pltpu.CompilerParams(vmem_limit_bytes=vmem_cap),
        cost_estimate=busy(35),
    )(lam, grad, *saved, gain)


def swap_halves(rows):
    count, width = rows.shape
    return rows.reshape(2, 2, count // 4, width).transpose(1, 0, 2, 3).reshape(count, width)


def body(
    place,
    inputs,
    positions,
    attn_gain,
    w_query,
    w_key,
    w_value,
    w_out,
    lambda_params,
    sub_gain,
    ffn_gain,
    w_gate,
    w_up,
    w_down,
    cotangent,
):
    n, tp, seq = place.n, place.tp, place.seq
    s, t, core, head, active = place.me()
    inputs, cotangent = swap_halves(inputs), swap_halves(cotangent)
    row_count, width = inputs.shape
    half = row_count // 2
    part = width // n
    inputs_f = inputs.astype(f32)
    attn_scale = rms_scale(inputs_f)
    first_exp = jnp.exp(jnp.sum(lambda_params[0] * lambda_params[1]))
    second_exp = jnp.exp(jnp.sum(lambda_params[2] * lambda_params[3]))
    lambda_value = first_exp - second_exp + lambda_init
    lam = lambda_value.reshape(1)

    weights = (w_query, w_key, w_value)
    gain_row = attn_gain.reshape(1, width)
    if tp == 4:
        rows_all, pos, qkv = gather_all(
            place, inputs, positions.reshape(1, row_count), gain_row, weights, 1
        )
    else:
        rows_all, pos, qkv = gather_all_plain(
            place, inputs, positions.reshape(1, row_count), gain_row, weights
        )
    cotangent_late, pos = lax.optimization_barrier((cotangent, pos))
    cotangent_all = lax.all_gather(cotangent_late, "tp", axis=0, tiled=True)
    head_gain = (sub_gain * (1.0 - lambda_init)).reshape(1, VW)
    mixed, *saved = attend(place, pos.reshape(n, row_count), lam, qkv, head_gain)
    parts, mixed_all, hidden, middle, middle_grad, branch_grad, mixed_grad, ffn_gain_part = (
        feed_forward(
            place,
            mixed,
            rows_all,
            cotangent_all.reshape(tp, row_count, width),
            ffn_gain.reshape(1, width),
            w_out,
            w_gate,
            w_up,
            w_down,
            2,
        )
    )
    hidden_width = hidden.shape[2]

    def scatter_rows(array):
        return lax.psum_scatter(array, "seq", scatter_dimension=0, tiled=True)

    ffn_grads = scatter_rows(parts)

    def head_block(x, h, c):
        return x.at[
            pl.ds(pl.multiple_of(half * c, half), half), pl.ds(pl.multiple_of(VW * h, VW), VW)
        ]

    def ffn_result(given, made, rest):
        hid, weight = given
        (out,) = made
        for i in range(tp):
            out[i] = dot(hid[i], weight[...]).astype(bf16)

    grad_heads, ffn_out = moves(
        place,
        [Dispatch(place, head_block)],
        [mixed_grad],
        [(n, half, VW)],
        4,
        20,
        work=ffn_result,
        operands=[(hidden, VMEM), (w_down, VMEM)],
        results=[(jax.ShapeDtypeStruct((tp, row_count, width), bf16), VMEM)],
    )
    dq, dkv, dkv_sib, sums = attend_back(place, lam, grad_heads, saved, head_gain)
    input_grad, attn_gain_part, weight_half, out_part = finish_heads(
        place,
        dq,
        dkv,
        dkv_sib,
        rows_all,
        gain_row,
        weights,
        branch_grad,
        mixed_all,
        inputs,
        middle_grad,
        5,
    )
    sums = jnp.where(active, sums, 0.0)
    pad = ((0, 0), (0, 128 - part))
    small = jnp.stack(
        [
            jnp.pad(attn_gain_part.reshape(n, part), pad),
            jnp.pad(ffn_gain_part.reshape(n, part), pad),
            jnp.broadcast_to(sums[0], (n, VW)),
            jnp.broadcast_to(sums[1], (n, VW)),
        ]
        + [jnp.zeros((n, VW), f32)] * 4,
        axis=1,
    )
    output, query_grad, key_grad, value_grad, out_grad, small_sum = last_moves(
        place,
        weight_half.reshape(n // 2, part, 3 * VW),
        small,
        ffn_out,
        out_part,
        middle,
        6,
    )
    ffn_grads = ffn_grads.astype(f32)
    down_grad = ffn_grads[:, :hidden_width].T
    gate_grad = ffn_grads[:, hidden_width : 2 * hidden_width]
    up_grad = ffn_grads[:, 2 * hidden_width :]
    lambda_total = jnp.sum(small_sum[3])
    lambda_grads = jnp.stack(
        [
            lambda_total * first_exp * lambda_params[1],
            lambda_total * first_exp * lambda_params[0],
            -lambda_total * second_exp * lambda_params[3],
            -lambda_total * second_exp * lambda_params[2],
        ]
    )
    lambda_norm = jnp.sqrt(jnp.sum(lambda_grads * lambda_grads))
    return (
        output,
        input_grad,
        small_sum[0, :part],
        query_grad,
        key_grad,
        value_grad,
        out_grad,
        lambda_grads,
        small_sum[2],
        small_sum[1, :part],
        gate_grad,
        up_grad,
        down_grad,
        lambda_total,
        lambda_norm,
    )


def solution(mesh):
    place = Place(mesh.shape["seq"], mesh.shape["tp"])
    both = ("seq", "tp")
    placed = (
        P(both, None),
        P(both),
        P(),
        P(),
        P(),
        P(),
        P(),
        P(),
        P(),
        P(),
        P(None, "tp"),
        P(None, "tp"),
        P("tp", None),
        P(both, None),
    )
    return jax.shard_map(
        functools.partial(body, place),
        mesh=mesh,
        in_specs=placed,
        out_specs=(
            P(both, None),
            P(both, None),
            P(both),
            P(both, None),
            P(both, None),
            P(both, None),
            P(both, None),
            P(),
            P(),
            P(both),
            P("seq", "tp"),
            P("seq", "tp"),
            P("tp", "seq"),
            P(),
            P(),
        ),
        check_vma=False,
    )
```

```python
import functools
import math

import jax
import jax.numpy as jnp
from jax import lax
from jax.experimental import pallas as pl
from jax.experimental.pallas import tpu as pltpu
from jax.sharding import PartitionSpec as P

H = 12
HALF = 64
VW = 128
HW = 1536

eps = 1e-05
lambda_init = 0.8 - 0.6 * math.exp(-3.3)
masked_score = -1e30
MESH = pl.DeviceIdType.MESH
ANY = pl.BlockSpec(memory_space=pl.ANY)
VMEM = pl.BlockSpec(memory_space=pltpu.VMEM)
SMEM = pl.BlockSpec(memory_space=pltpu.SMEM)
bf16 = jnp.bfloat16
f32 = jnp.float32
vmem_cap = 60 * 1024 * 1024


def dot(left, right):
    return jnp.dot(left, right, preferred_element_type=f32)


def dot_tn(left, right):
    return lax.dot_general(left, right, (((0,), (0,)), ((), ())), preferred_element_type=f32)


def dot_nt(left, right):
    return lax.dot_general(left, right, (((1,), (1,)), ((), ())), preferred_element_type=f32)


def rms_scale(values):
    return lax.rsqrt(jnp.mean(values * values, axis=-1, keepdims=True) + eps)


def rms_back(values, inv_rms, gain_vec, upstream):
    weighted = upstream * gain_vec
    inner_mean = jnp.mean(weighted * values, axis=-1, keepdims=True)
    return inv_rms * weighted - values * (inv_rms * inv_rms * inv_rms) * inner_mean


class Place:
    def __init__(self, seq, tp):
        self.seq, self.tp, self.n = seq, tp, seq * tp
        self.per = -(-H // (seq // 2))
        assert self.per <= tp and seq % 2 == 0

    def me(self):
        s, t = lax.axis_index("seq"), lax.axis_index("tp")
        head = (s // 2) * self.per + t
        active = jnp.logical_and(t < self.per, head < H)
        return s, t, lax.rem(s, 2), head, active

    def head_device(self, index):
        head, core = index // 2, lax.rem(index, 2)
        return 2 * (head // self.per) + core, lax.rem(head, self.per)

    def device(self, linear):
        return linear // self.tp, lax.rem(linear, self.tp)


def busy(microseconds):
    return pl.CostEstimate(
        flops=int(microseconds * 1e9), bytes_accessed=int(microseconds * 3e6), transcendentals=0
    )


def remote(src, dst, send, recv, where):
    return pltpu.make_async_remote_copy(
        src_ref=src, dst_ref=dst, send_sem=send, recv_sem=recv, device_id=where, device_id_type=MESH
    )


def loop(count, step):
    def one(k, carry):
        step(k)
        return carry

    lax.fori_loop(0, count, one, 0)


class Dispatch:
    def __init__(self, place, cut):
        self.p, self.cut = place, cut
        self.sems = [2 * H, place.n, 1]

    def start_one(self, index, x, o, send, recv, here):
        p = self.p
        s, t, c, head, active = p.me()
        lin = s * p.tp + t
        ds, dt = p.head_device(index)
        mine = jnp.logical_and(ds == s, dt == t)
        source = self.cut(x, index // 2, lax.rem(index, 2))

        @pl.when(jnp.logical_not(mine))
        def _():
            remote(source, o.at[lin], send.at[index], recv.at[lin], (ds, dt)).start()

        @pl.when(mine)
        def _():
            pltpu.make_async_copy(source, o.at[lin], here.at[0]).start()

    def start(self, *refs):
        p = self.p
        lin = lax.axis_index("seq") * p.tp + lax.axis_index("tp")
        loop(2 * H, lambda k: self.start_one(lax.rem(k + lin, 2 * H), *refs))

    def finish(self, x, o, send, recv, here, arrived=None):
        p = self.p
        s, t, c, head, active = p.me()
        lin = s * p.tp + t

        @pl.when(active)
        def _():
            pltpu.make_async_copy(self.cut(x, head, c), o.at[lin], here.at[0]).wait()
            if arrived is not None:
                arrived(lin)

            def got(k):
                other = lax.rem(lin + 1 + k, p.n)
                remote(o.at[other], o.at[other], send.at[0], recv.at[other], (s, t)).wait_recv()
                if arrived is not None:
                    arrived(other)

            loop(p.n - 1, got)

        def sent(k):
            ds, dt = p.head_device(k)

            @pl.when(jnp.logical_not(jnp.logical_and(ds == s, dt == t)))
            def _():
                remote(
                    self.cut(x, k // 2, lax.rem(k, 2)), o.at[0], send.at[k], recv.at[0], (ds, dt)
                ).wait_send()

        loop(2 * H, sent)


class Collect:
    def __init__(self, place, into, halves=False):
        self.p, self.into, self.halves = place, into, halves
        self.sems = [place.n, 2 * H, 1]

    def start(self, x, o, send, recv, here):
        p = self.p
        s, t, c, head, active = p.me()
        lin = s * p.tp + t
        count = p.n // 2 if self.halves else p.n

        @pl.when(active)
        def _():
            def step(k):
                slot = lax.rem(k + lin, count)
                other = slot + c * count if self.halves else slot
                into = self.into(o, lax.rem(other, p.tp), head, c)

                @pl.when(other != lin)
                def _():
                    remote(
                        x.at[slot], into, send.at[slot], recv.at[head * 2 + c], p.device(other)
                    ).start()

                @pl.when(other == lin)
                def _():
                    pltpu.make_async_copy(x.at[slot], into, here.at[0]).start()

            loop(count, step)

    def got(self, index, x, o, send, recv, here):
        p = self.p
        s, t = lax.axis_index("seq"), lax.axis_index("tp")
        into = self.into(o, t, index // 2, lax.rem(index, 2))
        ds, dt = p.head_device(index)
        mine = jnp.logical_and(ds == s, dt == t)

        @pl.when(jnp.logical_not(mine))
        def _():
            remote(into, into, send.at[0], recv.at[index], (s, t)).wait_recv()

        @pl.when(mine)
        def _():
            pltpu.make_async_copy(x.at[0], into, here.at[0]).wait()

    def sent(self, x, o, send, recv, here):
        p = self.p
        s, t, c, head, active = p.me()
        lin = s * p.tp + t
        count = p.n // 2 if self.halves else p.n

        @pl.when(active)
        def _():
            def one(k):
                other = k + c * count if self.halves else k

                @pl.when(other != lin)
                def _():
                    remote(
                        x.at[k], x.at[k], send.at[k], recv.at[0], p.device(other)
                    ).wait_send()

            loop(count, one)

    def finish(self, *refs):
        p = self.p
        if self.halves:
            lin = lax.axis_index("seq") * p.tp + lax.axis_index("tp")
            half = lin // (p.n // 2)
            loop(H, lambda k: self.got(2 * k + half, *refs))
        else:
            loop(2 * H, lambda k: self.got(k, *refs))
        self.sent(*refs)


class Everyone:
    def __init__(self, place, whole):
        self.p, self.whole = place, whole
        self.sems = [place.n, place.n, 1]

    def start(self, x, o, send, recv, here):
        p = self.p
        s, t = lax.axis_index("seq"), lax.axis_index("tp")
        lin = s * p.tp + t
        pltpu.make_async_copy(x if self.whole else x.at[lin], o.at[lin], here.at[0]).start()

        def step(k):
            other = lax.rem(lin + 1 + k, p.n)
            remote(
                x if self.whole else x.at[other],
                o.at[lin],
                send.at[other],
                recv.at[lin],
                p.device(other),
            ).start()

        loop(p.n - 1, step)

    def finish(self, x, o, send, recv, here):
        p = self.p
        s, t = lax.axis_index("seq"), lax.axis_index("tp")
        lin = s * p.tp + t
        pltpu.make_async_copy(x if self.whole else x.at[lin], o.at[lin], here.at[0]).wait()

        def done(k):
            other = lax.rem(lin + 1 + k, p.n)
            both = remote(
                x if self.whole else x.at[other],
                o.at[other],
                send.at[other],
                recv.at[other],
                p.device(other),
            )
            both.wait_recv()
            both.wait_send()

        loop(p.n - 1, done)


class Group:
    def __init__(self, place, whole):
        self.p, self.whole = place, whole
        self.sems = [place.tp, place.tp, 1]

    def start(self, x, o, send, recv, here):
        p = self.p
        s, t = lax.axis_index("seq"), lax.axis_index("tp")
        pltpu.make_async_copy(x if self.whole else x.at[t], o.at[t], here.at[0]).start()
        for k in range(1, p.tp):
            other = lax.rem(t + k, p.tp)
            remote(
                x if self.whole else x.at[other], o.at[t], send.at[other], recv.at[t], (s, other)
            ).start()

    def finish(self, x, o, send, recv, here):
        p = self.p
        s, t = lax.axis_index("seq"), lax.axis_index("tp")
        pltpu.make_async_copy(x if self.whole else x.at[t], o.at[t], here.at[0]).wait()
        for k in range(1, p.tp):
            other = lax.rem(t + k, p.tp)
            both = remote(
                x if self.whole else x.at[other],
                o.at[other],
                send.at[other],
                recv.at[other],
                (s, other),
            )
            both.wait_recv()
            both.wait_send()


class Along:
    def __init__(self, place):
        self.depth = place.seq // 2
        self.sems = [self.depth, self.depth, 1]

    def start(self, x, o, send, recv, here):
        s, t = lax.axis_index("seq"), lax.axis_index("tp")
        z, c = s // 2, lax.rem(s, 2)
        pltpu.make_async_copy(x.at[z], o.at[z], here.at[0]).start()

        def step(k):
            other = lax.rem(z + 1 + k, self.depth)
            remote(x.at[other], o.at[z], send.at[other], recv.at[z], (2 * other + c, t)).start()

        loop(self.depth - 1, step)

    def finish(self, x, o, send, recv, here):
        s, t = lax.axis_index("seq"), lax.axis_index("tp")
        z, c = s // 2, lax.rem(s, 2)
        pltpu.make_async_copy(x.at[z], o.at[z], here.at[0]).wait()

        def done(k):
            other = lax.rem(z + 1 + k, self.depth)
            both = remote(
                x.at[other], o.at[other], send.at[other], recv.at[other], (2 * other + c, t)
            )
            both.wait_recv()
            both.wait_send()

        loop(self.depth - 1, done)


def greet(place):
    s, t = lax.axis_index("seq"), lax.axis_index("tp")
    lin = s * place.tp + t
    barrier = pltpu.get_barrier_semaphore()

    def hello(k):
        pl.semaphore_signal(
            barrier,
            inc=1,
            device_id=place.device(lax.rem(lin + 1 + k, place.n)),
            device_id_type=MESH,
        )

    loop(place.n - 1, hello)
    pl.semaphore_wait(barrier, place.n - 1)


def moves(place, parts, arrays, outs, ident, cost, work=None, operands=(), results=(), scratch=()):
    count, extra = len(parts), len(operands)

    def kernel(*refs):
        ins, given = refs[:count], refs[count : count + extra]
        refs = refs[count + extra :]
        into, made = refs[:count], refs[count : count + len(results)]
        refs = refs[count + len(results) :]
        sems, rest = refs[: 3 * count], refs[3 * count :]
        greet(place)
        for i, part in enumerate(parts):
            part.start(ins[i], into[i], *sems[3 * i : 3 * i + 3])
        if work is not None:
            work(given, made, rest)
        for i, part in enumerate(parts):
            part.finish(ins[i], into[i], *sems[3 * i : 3 * i + 3])

    return pl.pallas_call(
        kernel,
        out_shape=[jax.ShapeDtypeStruct(s, a.dtype) for s, a in zip(outs, arrays)]
        + [shape for shape, spec in results],
        in_specs=[ANY] * count + [spec for array, spec in operands],
        out_specs=[ANY] * count + [spec for shape, spec in results],
        scratch_shapes=[pltpu.SemaphoreType.DMA((k,)) for part in parts for k in part.sems]
        + list(scratch),
        compiler_params=pltpu.CompilerParams(
            collective_id=ident, has_side_effects=True, vmem_limit_bytes=vmem_cap
        ),
        cost_estimate=busy(cost),
    )(*arrays, *[array for array, spec in operands])


def gather_all(place, rows, run_pos, gain, weights, ident):
    n, tp, depth = place.n, place.tp, place.seq // 2
    count, width = rows.shape
    half = count // 2
    tell = Everyone(place, True)

    def relay(first, known, use, x, o, full, halves, z_up, z_down, by_x, by_y, half_x, half_y, across, here):
        s, t = lax.axis_index("seq"), lax.axis_index("tp")
        z, c = s // 2, lax.rem(s, 2)
        t_x = t + 1 - 2 * lax.rem(t, 2)
        t_y = lax.rem(t + 2, 4)
        t_d = t_x + 2 - 4 * (t_x // 2)

        def slot(zs, core, ts):
            return (2 * zs + core) * tp + ts

        def line(zs, source, step):
            at = slot(zs, c, t)
            sem = z_up if step > 0 else z_down
            return remote(source, o.at[at], sem.at[zs], full.at[at], (s + 2 * step, t))

        def side(zs, source, sem, ts):
            at = slot(zs, c, t)
            return remote(source, o.at[at], sem.at[zs], full.at[at], (s, ts))

        def other_core(zs, ts, source):
            at = slot(zs, c, ts)
            return remote(
                source, o.at[at], across.at[zs * tp + ts], full.at[at], (s + 1 - 2 * c, t)
            )

        def corner(zs, ts, low, sem, to):
            at = slot(zs, c, ts)
            part = o.at[at, low : low + half]
            return remote(
                part, part, sem.at[zs], halves.at[2 * at + low // half], (s, to)
            )

        def arrived(at):
            remote(o.at[at], o.at[at], here.at[0], full.at[at], (s, t)).wait_recv()

        def push(zs, source):
            @pl.when(jnp.logical_and(zs <= z, z < depth - 1))
            def _():
                line(zs, source, 1).start()

            @pl.when(jnp.logical_and(zs >= z, z > 0))
            def _():
                line(zs, source, -1).start()

            side(zs, source, by_x, t_x).start()
            side(zs, source, by_y, t_y).start()
            other_core(zs, t, source).start()

        def each(k, act):
            def one(sign):
                zs = z + (2 * sign - 1) * k
                valid = jnp.logical_and(zs >= 0, zs < depth)
                valid = jnp.logical_and(valid, jnp.logical_and(k >= 0, k + 1 > sign))

                @pl.when(valid)
                def _():
                    act(zs)

            loop(2, one)

        def from_line(zs):
            arrived(slot(zs, c, t))
            push(zs, o.at[slot(zs, c, t)])

        def from_sides(zs):
            arrived(slot(zs, c, t_x))
            corner(zs, t_x, 0, half_y, t_y).start()
            other_core(zs, t_x, o.at[slot(zs, c, t_x)]).start()
            arrived(slot(zs, c, t_y))
            corner(zs, t_y, half, half_x, t_x).start()
            other_core(zs, t_y, o.at[slot(zs, c, t_y)]).start()

        def from_corner(zs):
            at = slot(zs, c, t_d)
            for low in (0, half):
                part = o.at[at, low : low + half]
                remote(
                    part, part, here.at[0], halves.at[2 * at + low // half], (s, t)
                ).wait_recv()
            other_core(zs, t_d, o.at[at]).start()

        keep = pltpu.make_async_copy(x, o.at[slot(z, c, t)], here.at[0])
        keep.start()
        push(z, x)
        first()
        keep.wait()

        def use_block(k):
            def one(i):
                other, v = i // 4, lax.rem(i, 4)
                m_x, m_y = lax.rem(v, 2), v // 2
                x_bit, y_bit = lax.rem(t, 2), t // 2
                ts = 2 * (y_bit + m_y - 2 * y_bit * m_y) + x_bit + m_x - 2 * x_bit * m_x
                core = c + other - 2 * c * other

                def act(zs):
                    at = slot(zs, core, ts)

                    @pl.when(other > 0)
                    def _():
                        arrived(at)

                    use(at)

                each(k - m_x - m_y - other, act)

            loop(8, one)

        def wave(k):
            @pl.when(k > 0)
            def _():
                each(k, from_line)
                each(k - 1, from_sides)
                each(k - 2, from_corner)

            use_block(k)

            @pl.when(k == depth)
            def _():
                known()

        loop(depth + 3, wave)

        def sent(k):
            zs = k
            at = slot(zs, c, t)

            @pl.when(jnp.logical_and(zs <= z, z < depth - 1))
            def _():
                line(zs, o.at[at], 1).wait_send()

            @pl.when(jnp.logical_and(zs >= z, z > 0))
            def _():
                line(zs, o.at[at], -1).wait_send()

            side(zs, o.at[at], by_x, t_x).wait_send()
            side(zs, o.at[at], by_y, t_y).wait_send()
            corner(zs, t_x, 0, half_y, t_y).wait_send()
            corner(zs, t_y, half, half_x, t_x).wait_send()
            for ts in range(tp):
                other_core(zs, ts, o.at[at]).wait_send()

        loop(depth, sent)

    sems = [n, 2 * n] + [depth] * 6 + [depth * tp, 1]

    def kernel(x, r, gain, wq, wk, wv, out, pos, qkv, o, wide, out_sem, *refs):
        greet(place)

        def save(at):
            return pltpu.make_async_copy(o.at[at], out.at[at], out_sem.at[at])

        def use(at):
            save(at).start()
            x = o[at].astype(f32)
            x = (x * rms_scale(x) * gain[...]).astype(bf16)
            qkv[at] = dot(x, wide[...]).astype(bf16)

        def first():
            tell.start(r, pos, *refs[:3])
            for i, w in enumerate((wq, wk, wv)):
                wide[:, i * VW : (i + 1) * VW] = w[...]

        relay(first, lambda: tell.finish(r, pos, *refs[:3]), use, x, o, *refs[3:])
        loop(n, lambda k: save(k).wait())

    def column(g):
        s, t, c, head, active = place.me()
        return 0, jnp.minimum(head, H - 1)

    columns = pl.BlockSpec((width, VW), column)
    return pl.pallas_call(
        kernel,
        grid=(1,),
        out_shape=[
            jax.ShapeDtypeStruct((n,) + rows.shape, rows.dtype),
            jax.ShapeDtypeStruct((n,) + run_pos.shape, run_pos.dtype),
            jax.ShapeDtypeStruct((n, count, 3 * VW), bf16),
        ],
        in_specs=[ANY] * 2 + [VMEM] + [columns] * 3,
        out_specs=[ANY] * 2 + [VMEM],
        scratch_shapes=[
            pltpu.VMEM((n,) + rows.shape, rows.dtype),
            pltpu.VMEM((width, 3 * VW), bf16),
            pltpu.SemaphoreType.DMA((n,)),
        ]
        + [pltpu.SemaphoreType.DMA((k,)) for k in tell.sems + sems],
        compiler_params=pltpu.CompilerParams(
            collective_id=ident, has_side_effects=True, vmem_limit_bytes=vmem_cap
        ),
        cost_estimate=busy(50),
    )(rows, run_pos, gain, *weights)


def gather_all_plain(place, rows, run_pos, gain, weights):
    axes = ("seq", "tp")
    rows_all = lax.all_gather(rows, axes, axis=0, tiled=False)
    pos = lax.all_gather(run_pos, axes, axis=0, tiled=False)
    x = rows_all.astype(f32)
    x = (x * rms_scale(x) * gain).astype(bf16)
    s, t, c, head, active = place.me()
    column = jnp.minimum(head, H - 1) * VW
    qkv = [
        dot(x, lax.dynamic_slice_in_dim(w, column, VW, 1)).astype(bf16) for w in weights
    ]
    return rows_all, pos, jnp.concatenate(qkv, axis=2)


def feed_forward(place, mixed, rows_all, cotangent_all, gain, w_out, w_gate, w_up, w_down, ident):
    n, tp, half = place.n, place.tp, mixed.shape[1]
    count, width = rows_all.shape[1:]
    hid = w_gate.shape[1]
    chunk = 256

    def into(o, t, h, c):
        return o.at[
            t,
            pl.ds(pl.multiple_of(half * c, half), half),
            pl.ds(pl.multiple_of(VW * h, VW), VW),
        ]

    back = Collect(place, into)

    def kernel(*refs):
        mixed, rows_all, cot, gain, wo_in, wg_in, wu_in, wd_in, *refs = refs
        parts, mixed_out, hidden, middle, middle_grad, branch, mixed_grad, gain_part, *refs = refs
        mixed_v, x_v, rows_v, both_v, send_v, recv_v, own_part, held, *refs = refs
        wo, wg, wu, wd, *sems = refs
        share_send, share_recv, part_send, part_recv, w_sem, x_sem, out_sem, mixed_sem = sems[3:]
        s, t = lax.axis_index("seq"), lax.axis_index("tp")
        greet(place)
        back.start(mixed, mixed_v, *sems[:3])

        def fetch(m):
            return pltpu.make_async_copy(rows_all.at[s * tp + m], x_v.at[m], x_sem.at[m])

        loads = [
            pltpu.make_async_copy(a, b, w_sem.at[i])
            for i, (a, b) in enumerate(((wo_in, wo), (wg_in, wg), (wu_in, wu), (wd_in, wd)))
        ]
        loop(tp, lambda m: fetch(m).start())
        for load in loads:
            load.start()

        def share(k, c, slot):
            other = lax.rem(t + k, tp)
            at = slot(other)
            return remote(
                mixed_v.at[t, half * c : half * c + half, :],
                mixed_v.at[at, half * c : half * c + half, :],
                share_send.at[2 * other + c],
                share_recv.at[2 * at + c],
                (s, other),
            )

        def give(k, slot):
            other = lax.rem(t + k, tp)
            at = slot(other)
            return remote(
                send_v.at[other], recv_v.at[at], part_send.at[other], part_recv.at[at], (s, other)
            )

        for c in range(2):
            loop(H, lambda h: back.got(2 * h + c, mixed, mixed_v, *sems[:3]))
            for k in range(1, tp):
                share(k, c, lambda other: t).start()
        loop(tp, lambda m: fetch(m).wait())
        for load in loads:
            load.wait()

        def member(k):
            m = lax.rem(t + k, tp)

            @pl.when(k > 0)
            def _():
                for c in range(2):
                    share(k, c, lambda other: other).wait_recv()

            x = x_v[m].astype(f32) + dot(mixed_v[m], wo[...])
            rows = (x * rms_scale(x) * gain[...]).astype(bf16)
            rows_v[m] = rows
            gate = dot(rows, wg[...])
            up = dot(rows, wu[...])
            sig = jax.nn.sigmoid(gate)
            act = gate * sig
            hidden[m] = (act * up).astype(bf16)
            grad = dot_nt(cot[m], wd[...])
            gate_rows = (grad * up * sig * (1.0 + gate * (1.0 - sig))).astype(bf16)
            up_rows = (grad * act).astype(bf16)
            both_v[m, :, :hid] = gate_rows
            both_v[m, :, hid:] = up_rows
            part = dot_nt(gate_rows, wg[...]) + dot_nt(up_rows, wu[...])

            @pl.when(k == 0)
            def _():
                own_part[...] = part
                middle[...] = x

            @pl.when(k > 0)
            def _():
                send_v[m] = part.astype(bf16)
                give(k, lambda other: t).start()

        loop(tp, member)
        keep = pltpu.make_async_copy(mixed_v, mixed_out, mixed_sem.at[0])
        keep.start()

        def copy(i):
            at = pl.ds(pl.multiple_of(chunk * i, chunk), chunk)
            return pltpu.make_async_copy(held.at[at], parts.at[at], out_sem.at[i])

        def weight_rows(i):
            at = pl.ds(pl.multiple_of(chunk * i, chunk), chunk)
            held[at, :hid] = dot_tn(
                cot[:, :, at].reshape(tp * count, chunk), hidden[...].reshape(tp * count, hid)
            ).astype(bf16)
            held[at, hid:] = dot_tn(
                rows_v[:, :, at].reshape(tp * count, chunk),
                both_v[...].reshape(tp * count, 2 * hid),
            ).astype(bf16)
            copy(i).start()

        loop(width // chunk, weight_rows)
        total = own_part[...]
        for k in range(1, tp):
            give(k, lambda other: other).wait_recv()
            total = total + recv_v[lax.rem(t + k, tp)].astype(f32)
        mid = middle[...]
        scale = rms_scale(mid)
        gain_part[...] = jnp.sum(total * mid * scale, axis=0, keepdims=True)
        grad = cot[t].astype(f32) + rms_back(mid, scale, gain[...], total)
        middle_grad[...] = grad
        branch[...] = grad.astype(bf16)
        mixed_grad[...] = dot_nt(grad.astype(bf16), wo[...]).astype(bf16)
        loop(width // chunk, lambda i: copy(i).wait())
        keep.wait()
        for k in range(1, tp):
            give(k, lambda other: other).wait_send()
            for c in range(2):
                share(k, c, lambda other: other).wait_send()
        back.sent(mixed, mixed_v, *sems[:3])

    struct = jax.ShapeDtypeStruct
    group = (tp, count, width)
    return pl.pallas_call(
        kernel,
        out_shape=[
            struct((width, 3 * hid), bf16),
            struct(group, bf16),
            struct((tp, count, hid), bf16),
            struct((count, width), f32),
            struct((count, width), f32),
            struct((count, width), bf16),
            struct((count, width), bf16),
            struct((1, width), f32),
        ],
        in_specs=[ANY, ANY, VMEM, VMEM] + [ANY] * 4,
        out_specs=[ANY, ANY] + [VMEM] * 6,
        scratch_shapes=[
            pltpu.VMEM(group, bf16),
            pltpu.VMEM(group, bf16),
            pltpu.VMEM(group, bf16),
            pltpu.VMEM((tp, count, 2 * hid), bf16),
            pltpu.VMEM(group, bf16),
            pltpu.VMEM(group, bf16),
            pltpu.VMEM((count, width), f32),
            pltpu.VMEM((width, 3 * hid), bf16),
            pltpu.VMEM(w_out.shape, bf16),
            pltpu.VMEM(w_gate.shape, bf16),
            pltpu.VMEM(w_up.shape, bf16),
            pltpu.VMEM(w_down.shape, bf16),
        ]
        + [
            pltpu.SemaphoreType.DMA((k,))
            for k in back.sems + [2 * tp, 2 * tp, tp, tp, 4, tp, width // chunk, 1]
        ],
        compiler_params=pltpu.CompilerParams(
            collective_id=ident, has_side_effects=True, vmem_limit_bytes=vmem_cap
        ),
        cost_estimate=busy(60),
    )(mixed, rows_all, cotangent_all, gain, w_out, w_gate, w_up, w_down)


def finish_heads(
    place,
    dq,
    dkv,
    dkv_sib,
    rows_all,
    gain,
    weights,
    branch_grad,
    mixed_all,
    inputs,
    middle_grad,
    ident,
):
    n, half = place.n, dq.shape[1]
    width = rows_all.shape[2]
    part, chunk, depth = width // n, 256, place.seq // 2
    lot = 8 if n <= 64 else 2
    out_type = bf16 if part % 16 == 0 else f32

    def into(o, t, h, c):
        return o.at[
            pl.ds(pl.multiple_of(half * c, half), half),
            pl.ds(pl.multiple_of(3 * VW * h, 3 * VW), 3 * VW),
        ]

    back, share = Collect(place, into), Group(place, True)

    def kernel(*refs):
        dq, dkv, dkv_sib, rows_all, gain, *refs = refs
        weights, refs = refs[:3], refs[3:]
        branch, mixed_in, inputs, middle_grad, *refs = refs
        input_grad, gain_part, weight_half, out_own, *refs = refs
        other_dkv, grads, rows_back, raw, held, away, other, w_all, branch_all, mixed, *refs = refs
        out_part, out_away, out_other, *sems = refs
        s, t = lax.axis_index("seq"), lax.axis_index("tp")
        c = lax.rem(s, 2)
        send, recv, raw_sem, w_sem, mixed_sem = sems[6:]
        sibling = (s + 1 - 2 * c, t)
        greet(place)
        swap = remote(dkv_sib, other_dkv, send.at[0], recv.at[0], sibling)
        swap.start()

        def fetch(i):
            return pltpu.make_async_copy(
                rows_all.at[
                    pl.ds(lot * i, lot), pl.ds(pl.multiple_of(half * c, half), half), :
                ],
                raw.at[lax.rem(i, 2)],
                raw_sem.at[lax.rem(i, 2)],
            )

        fetch(0).start()
        loads = [
            pltpu.make_async_copy(w, w_all.at[i], w_sem.at[i]) for i, w in enumerate(weights)
        ]
        for load in loads:
            load.start()
        mixed_load = pltpu.make_async_copy(mixed_in, mixed, mixed_sem.at[0])
        mixed_load.start()
        swap.wait_recv()

        def join(i):
            grads[i, :, :VW] = dq[i]
            grads[i, :, VW:] = (dkv[i] + other_dkv[i].astype(f32)).astype(bf16)

        loop(n, join)
        back.start(grads, rows_back, *sems[:3])
        share.start(branch, branch_all, *sems[3:6])
        held[...] = jnp.zeros_like(held)

        def rows(i):
            @pl.when(i + 1 < n // lot)
            def _():
                fetch(i + 1).start()

            fetch(i).wait()
            x = raw[lax.rem(i, 2)].reshape(lot * half, width).astype(f32)
            x = (x * rms_scale(x) * gain[...]).astype(bf16)
            g = grads[pl.ds(lot * i, lot)].reshape(lot * half, 3 * VW)
            for k in range(width // chunk):
                held[k * chunk : (k + 1) * chunk, :] += dot_tn(
                    x[:, k * chunk : (k + 1) * chunk], g
                )

        loop(n // lot, rows)
        low = pl.multiple_of(c * (width // 2), width // 2)
        high = pl.multiple_of((1 - c) * (width // 2), width // 2)
        away[...] = held[pl.ds(high, width // 2), :].astype(bf16)
        cross = remote(away, other, send.at[1], recv.at[1], sibling)
        cross.start()
        mixed_load.wait()
        share.finish(branch, branch_all, *sems[3:6])

        def out_rows(i):
            at = pl.ds(pl.multiple_of(chunk * i, chunk), chunk)
            out_part[at, :] = dot_tn(
                mixed[:, :, at].reshape(-1, chunk), branch_all[...].reshape(-1, width)
            ).astype(out_type)

        loop(HW // chunk, out_rows)

        def out_picked(z, core):
            picked = jnp.zeros((part, width), f32)
            for k in range(2 * place.tp):
                low = part * (2 * place.tp * z + k)
                here = k == core * place.tp + t
                picked = picked + jnp.where(here, out_part[low : low + part, :], 0.0)
            return picked.astype(bf16)

        def out_block(z, core):
            if part % 16:
                return out_picked(z, core)
            base = part * (place.tp * (2 * z + core) + t)
            return out_part[pl.ds(pl.multiple_of(base, part), part), :].astype(bf16)

        for z in range(depth):
            out_away[z] = out_block(z, 1 - c)
        out_cross = remote(out_away, out_other, send.at[2], recv.at[2], sibling)
        out_cross.start()
        back.finish(grads, rows_back, *sems[:3])
        for load in loads:
            load.wait()
        total = None
        for h in range(0, H, 2):
            for i in range(3):
                at = (3 * h + i) * VW
                x = jnp.concatenate(
                    [rows_back[:, at : at + VW], rows_back[:, at + 3 * VW : at + 4 * VW]], axis=1
                )
                new = dot_nt(x, w_all[i, :, h * VW : (h + 2) * VW])
                total = new if total is None else total + new
        x = inputs[...].astype(f32)
        scale = rms_scale(x)
        gain_part[...] = jnp.sum(total * x * scale, axis=0, keepdims=True)
        done = middle_grad[...] + rms_back(x, scale, gain[...], total)
        quarter = half // 2
        for b in range(2):
            for h in range(2):
                to, from_ = (2 * b + h) * quarter, (2 * h + b) * quarter
                input_grad[to : to + quarter, :] = done[from_ : from_ + quarter]
        cross.wait_recv()
        weight_half[...] = (held[pl.ds(low, width // 2), :] + other[...].astype(f32)).astype(bf16)
        out_cross.wait_recv()
        for z in range(depth):
            out_own[z] = (out_block(z, c).astype(f32) + out_other[z].astype(f32)).astype(bf16)
        swap.wait_send()
        cross.wait_send()
        out_cross.wait_send()

    return pl.pallas_call(
        kernel,
        out_shape=[
            jax.ShapeDtypeStruct((2 * half, width), f32),
            jax.ShapeDtypeStruct((1, width), f32),
            jax.ShapeDtypeStruct((width // 2, 3 * VW), bf16),
            jax.ShapeDtypeStruct((depth, part, width), bf16),
        ],
        in_specs=[VMEM, VMEM, ANY, ANY, VMEM] + [ANY] * 5 + [VMEM] * 2,
        out_specs=[VMEM] * 4,
        scratch_shapes=[
            pltpu.VMEM((n, half, 2 * VW), bf16),
            pltpu.VMEM((n, half, 3 * VW), bf16),
            pltpu.VMEM((2 * half, 3 * HW), bf16),
            pltpu.VMEM((2, lot, half, width), bf16),
            pltpu.VMEM((width, 3 * VW), f32),
            pltpu.VMEM((width // 2, 3 * VW), bf16),
            pltpu.VMEM((width // 2, 3 * VW), bf16),
            pltpu.VMEM((3,) + weights[0].shape, bf16),
            pltpu.VMEM((place.tp,) + branch_grad.shape, bf16),
            pltpu.VMEM(mixed_all.shape, bf16),
            pltpu.VMEM((HW, width), out_type),
            pltpu.VMEM((depth, part, width), bf16),
            pltpu.VMEM((depth, part, width), bf16),
        ]
        + [pltpu.SemaphoreType.DMA((k,)) for k in back.sems + share.sems + [3, 3, 2, 3, 1]],
        compiler_params=pltpu.CompilerParams(
            collective_id=ident, has_side_effects=True, vmem_limit_bytes=vmem_cap
        ),
        cost_estimate=busy(40),
    )(
        dq,
        dkv,
        dkv_sib,
        rows_all,
        gain,
        *weights,
        branch_grad,
        mixed_all,
        inputs,
        middle_grad,
    )


def last_moves(place, weight_half, small, ffn_out, out_part, middle, lambda_params, ident):
    n, tp, seq = place.n, place.tp, place.seq
    count, width = middle.shape
    part = width // n
    kinds = [
        Collect(place, lambda o, t, h, c: o.at[h], True),
        Everyone(place, False),
        Group(place, False),
        Along(place),
    ]
    arrays = [weight_half, small, ffn_out, out_part]
    landing = [
        pltpu.VMEM((H, part, 3 * VW), bf16),
        pltpu.VMEM(small.shape, f32),
        pltpu.VMEM(ffn_out.shape, bf16),
        pltpu.VMEM(out_part.shape, bf16),
    ]

    def kernel(*refs):
        ins, middle, params, refs = refs[:4], refs[4], refs[5], refs[6:]
        output, query_grad, key_grad, value_grad, out_grad, sums, *refs = refs
        lambda_grads, lambda_total, lambda_norm, *refs = refs
        lands, sems = refs[:4], refs[4:]
        greet(place)
        every = list(zip(kinds, ins, lands, [sems[3 * i : 3 * i + 3] for i in range(4)]))
        for kind, source, land, sem in every:
            kind.start(source, land, *sem)

        def finish(i):
            kind, source, land, sem = every[i]
            kind.finish(source, land, *sem)

        finish(1)
        sums[...] = jnp.sum(lands[1][...], axis=0)
        lambda_sum = jnp.sum(sums[3:4, :], axis=1, keepdims=True)
        squares = jnp.zeros((1, 1), f32)
        for i, sign in ((0, 1.0), (2, -1.0)):
            left, right = params[i : i + 1, :], params[i + 1 : i + 2, :]
            factor = sign * lambda_sum * jnp.exp(jnp.sum(left * right, axis=1, keepdims=True))
            for row, vector in ((i, right), (i + 1, left)):
                grad = factor * vector
                lambda_grads[row : row + 1, :] = grad
                squares = squares + jnp.sum(grad * grad, axis=1, keepdims=True)
        lambda_total[...] = lambda_sum
        lambda_norm[...] = jnp.sqrt(squares)
        finish(2)
        total = middle[...]
        for m in range(tp):
            total = total + lands[2][m].astype(f32)
        total = total.astype(bf16)
        quarter = count // 4
        for b in range(2):
            for h in range(2):
                low, from_ = (2 * b + h) * quarter, (2 * h + b) * quarter
                output[low : low + quarter, :] = total[from_ : from_ + quarter]
        finish(0)
        for h in range(H):
            for i, grad in enumerate((query_grad, key_grad, value_grad)):
                grad[:, h * VW : (h + 1) * VW] = lands[0][h, :, i * VW : (i + 1) * VW].astype(f32)
        finish(3)
        total = lands[3][0].astype(f32)
        for m in range(1, seq // 2):
            total = total + lands[3][m].astype(f32)
        out_grad[...] = total

    struct = jax.ShapeDtypeStruct
    return pl.pallas_call(
        kernel,
        out_shape=[struct((count, width), bf16)]
        + [struct((part, HW), f32)] * 4
        + [struct((8, VW), f32), struct(lambda_params.shape, f32)]
        + [struct((1, 1), f32)] * 2,
        in_specs=[ANY] * 4 + [VMEM] * 2,
        out_specs=[VMEM] * 9,
        scratch_shapes=landing
        + [pltpu.SemaphoreType.DMA((k,)) for kind in kinds for k in kind.sems],
        compiler_params=pltpu.CompilerParams(
            collective_id=ident, has_side_effects=True, vmem_limit_bytes=vmem_cap
        ),
        cost_estimate=busy(35),
    )(*arrays, middle, lambda_params)


def spans(n, count, step):
    if n <= 32:
        for j in range(count):
            step(j)
    else:
        loop(count, step)


def fold(n, count, step, carry):
    if n <= 32:
        for k in range(count):
            carry = step(k, carry)
        return carry
    return lax.fori_loop(0, count, step, carry)


def aligned(value, unit):
    return value if isinstance(value, int) else pl.multiple_of(value, unit)


def query_rows(n):
    return 256 if n <= 64 else 128


def two_maps(rows):
    lane = lax.broadcasted_iota(jnp.int32, rows.shape, 1)
    zero = jnp.zeros_like(rows)
    return jnp.concatenate(
        [jnp.where(lane < HALF, rows, zero), jnp.where(lane < HALF, zero, rows)], axis=0
    )


def fwd_kernel(n, pos, lam, qkv, gain, mixed, mix, lse, qs, ks, vs, order, score):
    qb = query_rows(n)
    kb_rows = 2 * qb
    c = lax.rem(lax.axis_index("seq"), 2)

    def place_run(run):
        order[pos[run // 2, lax.rem(run, 2) * 64] // 64] = run

    loop(2 * n, place_run)
    lambda_value = lam[0]

    def sort(p):
        run = order[p]
        i, b = run // 2, pl.multiple_of(32 * lax.rem(run, 2), 32)
        for h in range(2):
            at = pl.ds(pl.multiple_of(64 * p + 32 * h, 32), 32)
            rows = pl.ds(pl.multiple_of(64 * h + b, 32), 32)
            ks[at, :] = qkv[i, rows, VW : 2 * VW]
            vs[at, :] = qkv[i, rows, 2 * VW :]
        mine = qkv[i, pl.ds(pl.multiple_of(64 * c + b, 32), 32), :VW]
        qs[pl.ds(pl.multiple_of(32 * p, 32), 32), :] = mine * jnp.asarray(0.125, bf16)

    loop(2 * n, sort)

    def block(j):
        at = pl.ds(aligned(qb * j, qb), qb)
        q2 = two_maps(qs[at, :])

        def scores(kb):
            return dot_nt(q2, ks[pl.ds(aligned(kb_rows * kb, kb_rows), kb_rows), :])

        def lanes(top, s):
            for i in range(kb_rows // 128):
                top = jnp.maximum(top, s[:, 128 * i : 128 * i + 128])
            return top

        def first(kb, top):
            s = scores(kb)
            score[:, pl.ds(aligned(kb_rows * kb, kb_rows), kb_rows)] = s
            return lanes(top, s)

        top = fold(n, j, first, jnp.full((2 * qb, 128), masked_score, f32))
        s = scores(j)
        row = lax.broadcasted_iota(jnp.int32, s.shape, 0)
        row = lax.rem(row, qb)
        allowed = (
            lax.broadcasted_iota(jnp.int32, s.shape, 1)
            <= 64 * (row // 32) + lax.rem(row, 32) + 32 * c
        )
        s = jnp.where(allowed, s, masked_score)
        score[:, pl.ds(aligned(kb_rows * j, kb_rows), kb_rows)] = s
        high = jnp.max(lanes(top, s), axis=1, keepdims=True)
        ones = jnp.ones((kb_rows, VW), bf16)

        def second(kb, acc):
            here = pl.ds(aligned(kb_rows * kb, kb_rows), kb_rows)
            weights = jnp.exp(score[:, here] - high).astype(bf16)
            return acc + dot(weights, jnp.concatenate([vs[here, :], ones], axis=1))

        acc = fold(n, j + 1, second, jnp.zeros((2 * qb, 2 * VW), f32))
        total = acc[:, VW:]
        mixes = acc[:, :VW] / total
        lse[j] = jnp.transpose(high + jnp.log(total))[:8, :]
        mix[0, at, :] = mixes[:qb]
        mix[1, at, :] = mixes[qb:]
        out = mixes[:qb] - lambda_value * mixes[qb:]
        out = (out * rms_scale(out) * gain[...]).astype(bf16)
        for i in range(qb // 32):
            run = order[j * (qb // 32) + i]
            b = pl.multiple_of(32 * lax.rem(run, 2), 32)
            mixed[run // 2, pl.ds(b, 32), :] = out[32 * i : 32 * i + 32]

    spans(n, n * 64 // qb, block)


def attend(place, pos, lam, qkv, gain):
    n = place.n
    rows = 64 * n
    qb = query_rows(n)
    return pl.pallas_call(
        functools.partial(fwd_kernel, n),
        out_shape=[
            jax.ShapeDtypeStruct((n, 64, VW), bf16),
            jax.ShapeDtypeStruct((2, rows, VW), f32),
            jax.ShapeDtypeStruct((rows // qb, 8, 2 * qb), f32),
            jax.ShapeDtypeStruct((rows, VW), bf16),
            jax.ShapeDtypeStruct((2 * rows, VW), bf16),
            jax.ShapeDtypeStruct((2 * rows, VW), bf16),
            jax.ShapeDtypeStruct((2 * n,), jnp.int32),
        ],
        in_specs=[SMEM, SMEM, VMEM, VMEM],
        out_specs=[VMEM] * 6 + [SMEM],
        scratch_shapes=[pltpu.VMEM((2 * qb, 2 * rows), f32)],
        compiler_params=pltpu.CompilerParams(vmem_limit_bytes=vmem_cap),
        cost_estimate=busy(20),
    )(pos, lam, qkv, gain)


def bwd_kernel(
    n,
    lam,
    grad,
    mix,
    lse,
    qs,
    ks,
    vs,
    order,
    gain,
    dq,
    dkv,
    dkv_sib,
    sums,
    dk,
    dv,
):
    qb = query_rows(n)
    kb_rows = 2 * qb
    c = lax.rem(lax.axis_index("seq"), 2)
    lambda_value = lam[0]
    dk[...] = jnp.zeros_like(dk)
    dv[...] = jnp.zeros_like(dv)
    sums[...] = jnp.zeros_like(sums)

    def block(j):
        at = pl.ds(aligned(qb * j, qb), qb)
        pieces = []
        for i in range(qb // 32):
            run = order[j * (qb // 32) + i]
            b = pl.multiple_of(32 * lax.rem(run, 2), 32)
            pieces.append(grad[run // 2, pl.ds(b, 32), :])
        mixed_grad = jnp.concatenate(pieces, axis=0).astype(f32)
        mix_1, mix_2 = mix[0, at, :], mix[1, at, :]
        out = mix_1 - lambda_value * mix_2
        scale = rms_scale(out)
        sums[0:1, :] += jnp.sum(mixed_grad * out * scale, axis=0, keepdims=True) * (
            1.0 - lambda_init
        )
        heads_grad = rms_back(out, scale, gain[...], mixed_grad).astype(bf16)
        grad_f = heads_grad.astype(f32)
        dot_2 = grad_f * mix_2
        sums[1:2, :] += -jnp.sum(dot_2, axis=0, keepdims=True)
        delta_1 = jnp.sum(jnp.transpose(grad_f * mix_1), axis=0, keepdims=True)
        delta_2 = -lambda_value * jnp.sum(jnp.transpose(dot_2), axis=0, keepdims=True)
        q2 = two_maps(qs[at, :])
        lse_now = lse[j][0:1, :]
        q2_t = jnp.transpose(q2)
        grad_t = jnp.transpose(heads_grad)

        def piece(kb, acc, diagonal):
            here = pl.ds(aligned(kb_rows * kb, kb_rows), kb_rows)
            keys = ks[here, :]
            s = dot(keys, q2_t) - lse_now
            if diagonal:
                col = lax.rem(lax.broadcasted_iota(jnp.int32, s.shape, 1), qb)
                allowed = (
                    lax.broadcasted_iota(jnp.int32, s.shape, 0)
                    <= 64 * (col // 32) + lax.rem(col, 32) + 32 * c
                )
                s = jnp.where(allowed, s, masked_score)
            prob = jnp.exp(s)
            prob_1, prob_2 = prob[:, :qb], prob[:, qb:]
            value_dot = dot(vs[here, :], grad_t)
            grads = jnp.concatenate(
                [
                    (prob_1 * (value_dot - delta_1)).astype(bf16),
                    (prob_2 * (-lambda_value * value_dot - delta_2)).astype(bf16),
                ],
                axis=1,
            )
            dv[here, :] += dot((prob_1 - lambda_value * prob_2).astype(bf16), heads_grad)
            dk[here, :] += dot(grads, q2)
            return acc + dot_tn(keys, grads)

        acc = fold(
            n, j, lambda kb, a: piece(kb, a, False), jnp.zeros((VW, 2 * qb), f32)
        )
        acc = jnp.transpose(piece(j, acc, True))
        lane = lax.broadcasted_iota(jnp.int32, (qb, VW), 1)
        done = (jnp.where(lane < HALF, acc[:qb], acc[qb:]) * 0.125).astype(bf16)
        for i in range(qb // 32):
            run = order[j * (qb // 32) + i]
            b = pl.multiple_of(32 * lax.rem(run, 2), 32)
            dq[run // 2, pl.ds(b, 32), :] = done[32 * i : 32 * i + 32]

    spans(n, n * 64 // qb, block)

    def unsort(p):
        run = order[p]
        b = pl.multiple_of(32 * lax.rem(run, 2), 32)
        low = pl.multiple_of(64 * p + 32 * c, 32)
        high = pl.multiple_of(64 * p + 32 * (1 - c), 32)
        dkv[run // 2, pl.ds(b, 32), :VW] = dk[pl.ds(low, 32), :]
        dkv[run // 2, pl.ds(b, 32), VW:] = dv[pl.ds(low, 32), :]
        dkv_sib[run // 2, pl.ds(b, 32), :VW] = dk[pl.ds(high, 32), :].astype(bf16)
        dkv_sib[run // 2, pl.ds(b, 32), VW:] = dv[pl.ds(high, 32), :].astype(bf16)

    loop(2 * n, unsort)


def attend_back(place, lam, grad, saved, gain):
    n = place.n
    rows = 64 * n
    qb = query_rows(n)
    return pl.pallas_call(
        functools.partial(bwd_kernel, n),
        out_shape=[
            jax.ShapeDtypeStruct((n, 64, VW), bf16),
            jax.ShapeDtypeStruct((n, 64, 2 * VW), f32),
            jax.ShapeDtypeStruct((n, 64, 2 * VW), bf16),
            jax.ShapeDtypeStruct((8, VW), f32),
        ],
        in_specs=[SMEM] + [VMEM] * 6 + [SMEM, VMEM],
        out_specs=[VMEM] * 4,
        scratch_shapes=[pltpu.VMEM((2 * rows, VW), f32)] * 2,
        compiler_params=pltpu.CompilerParams(vmem_limit_bytes=vmem_cap),
        cost_estimate=busy(35),
    )(lam, grad, *saved, gain)


def swap_halves(rows):
    count, width = rows.shape
    return rows.reshape(2, 2, count // 4, width).transpose(1, 0, 2, 3).reshape(count, width)


def body(
    place,
    inputs,
    positions,
    attn_gain,
    w_query,
    w_key,
    w_value,
    w_out,
    lambda_params,
    sub_gain,
    ffn_gain,
    w_gate,
    w_up,
    w_down,
    cotangent,
):
    n, tp, seq = place.n, place.tp, place.seq
    s, t, core, head, active = place.me()
    inputs, cotangent = swap_halves(inputs), swap_halves(cotangent)
    row_count, width = inputs.shape
    half = row_count // 2
    part = width // n
    inputs_f = inputs.astype(f32)
    attn_scale = rms_scale(inputs_f)
    first_exp = jnp.exp(jnp.sum(lambda_params[0] * lambda_params[1]))
    second_exp = jnp.exp(jnp.sum(lambda_params[2] * lambda_params[3]))
    lambda_value = first_exp - second_exp + lambda_init
    lam = lambda_value.reshape(1)

    weights = (w_query, w_key, w_value)
    gain_row = attn_gain.reshape(1, width)
    if tp == 4:
        rows_all, pos, qkv = gather_all(
            place, inputs, positions.reshape(1, row_count), gain_row, weights, 1
        )
    else:
        rows_all, pos, qkv = gather_all_plain(
            place, inputs, positions.reshape(1, row_count), gain_row, weights
        )
    cotangent_late, pos = lax.optimization_barrier((cotangent, pos))
    cotangent_all = lax.all_gather(cotangent_late, "tp", axis=0, tiled=True)
    head_gain = (sub_gain * (1.0 - lambda_init)).reshape(1, VW)
    mixed, *saved = attend(place, pos.reshape(n, row_count), lam, qkv, head_gain)
    parts, mixed_all, hidden, middle, middle_grad, branch_grad, mixed_grad, ffn_gain_part = (
        feed_forward(
            place,
            mixed,
            rows_all,
            cotangent_all.reshape(tp, row_count, width),
            ffn_gain.reshape(1, width),
            w_out,
            w_gate,
            w_up,
            w_down,
            2,
        )
    )
    hidden_width = hidden.shape[2]

    def scatter_rows(array):
        return lax.psum_scatter(array, "seq", scatter_dimension=0, tiled=True)

    ffn_grads = scatter_rows(parts)

    def head_block(x, h, c):
        return x.at[
            pl.ds(pl.multiple_of(half * c, half), half), pl.ds(pl.multiple_of(VW * h, VW), VW)
        ]

    def ffn_result(given, made, rest):
        hid, weight = given
        (out,) = made
        for i in range(tp):
            out[i] = dot(hid[i], weight[...]).astype(bf16)

    grad_heads, ffn_out = moves(
        place,
        [Dispatch(place, head_block)],
        [mixed_grad],
        [(n, half, VW)],
        4,
        20,
        work=ffn_result,
        operands=[(hidden, VMEM), (w_down, VMEM)],
        results=[(jax.ShapeDtypeStruct((tp, row_count, width), bf16), VMEM)],
    )
    dq, dkv, dkv_sib, sums = attend_back(place, lam, grad_heads, saved, head_gain)
    input_grad, attn_gain_part, weight_half, out_part = finish_heads(
        place,
        dq,
        dkv,
        dkv_sib,
        rows_all,
        gain_row,
        weights,
        branch_grad,
        mixed_all,
        inputs,
        middle_grad,
        5,
    )
    sums = jnp.where(active, sums, 0.0)
    pad = ((0, 0), (0, 128 - part))
    small = jnp.stack(
        [
            jnp.pad(attn_gain_part.reshape(n, part), pad),
            jnp.pad(ffn_gain_part.reshape(n, part), pad),
            jnp.broadcast_to(sums[0], (n, VW)),
            jnp.broadcast_to(sums[1], (n, VW)),
        ]
        + [jnp.zeros((n, VW), f32)] * 4,
        axis=1,
    )
    (
        output,
        query_grad,
        key_grad,
        value_grad,
        out_grad,
        small_sum,
        lambda_grads,
        lambda_total,
        lambda_norm,
    ) = last_moves(
        place,
        weight_half.reshape(n // 2, part, 3 * VW),
        small,
        ffn_out,
        out_part,
        middle,
        lambda_params,
        6,
    )
    lambda_total, lambda_norm = lambda_total.reshape(()), lambda_norm.reshape(())
    ffn_grads = ffn_grads.astype(f32)
    down_grad = ffn_grads[:, :hidden_width].T
    gate_grad = ffn_grads[:, hidden_width : 2 * hidden_width]
    up_grad = ffn_grads[:, 2 * hidden_width :]
    return (
        output,
        input_grad,
        small_sum[0, :part],
        query_grad,
        key_grad,
        value_grad,
        out_grad,
        lambda_grads,
        small_sum[2],
        small_sum[1, :part],
        gate_grad,
        up_grad,
        down_grad,
        lambda_total,
        lambda_norm,
    )


def solution(mesh):
    place = Place(mesh.shape["seq"], mesh.shape["tp"])
    both = ("seq", "tp")
    placed = (
        P(both, None),
        P(both),
        P(),
        P(),
        P(),
        P(),
        P(),
        P(),
        P(),
        P(),
        P(None, "tp"),
        P(None, "tp"),
        P("tp", None),
        P(both, None),
    )
    return jax.shard_map(
        functools.partial(body, place),
        mesh=mesh,
        in_specs=placed,
        out_specs=(
            P(both, None),
            P(both, None),
            P(both),
            P(both, None),
            P(both, None),
            P(both, None),
            P(both, None),
            P(),
            P(),
            P(both),
            P("seq", "tp"),
            P("seq", "tp"),
            P("tp", "seq"),
            P(),
            P(),
        ),
        check_vma=False,
    )
```

```python
import functools
import math

import jax
import jax.numpy as jnp
from jax import lax
from jax.experimental import pallas as pl
from jax.experimental.pallas import tpu as pltpu
from jax.sharding import PartitionSpec as P

H = 12
HALF = 64
VW = 128
HW = 1536

eps = 1e-05
lambda_init = 0.8 - 0.6 * math.exp(-3.3)
masked_score = -1e30
MESH = pl.DeviceIdType.MESH
ANY = pl.BlockSpec(memory_space=pl.ANY)
VMEM = pl.BlockSpec(memory_space=pltpu.VMEM)
SMEM = pl.BlockSpec(memory_space=pltpu.SMEM)
bf16 = jnp.bfloat16
f32 = jnp.float32
vmem_cap = 60 * 1024 * 1024


def dot(left, right):
    return jnp.dot(left, right, preferred_element_type=f32)


def dot_tn(left, right):
    return lax.dot_general(left, right, (((0,), (0,)), ((), ())), preferred_element_type=f32)


def dot_nt(left, right):
    return lax.dot_general(left, right, (((1,), (1,)), ((), ())), preferred_element_type=f32)


def rms_scale(values):
    return lax.rsqrt(jnp.mean(values * values, axis=-1, keepdims=True) + eps)


def rms_back(values, inv_rms, gain_vec, upstream):
    weighted = upstream * gain_vec
    inner_mean = jnp.mean(weighted * values, axis=-1, keepdims=True)
    return inv_rms * weighted - values * (inv_rms * inv_rms * inv_rms) * inner_mean


class Place:
    def __init__(self, seq, tp):
        self.seq, self.tp, self.n = seq, tp, seq * tp
        self.per = -(-H // (seq // 2))
        assert self.per <= tp and seq % 2 == 0

    def me(self):
        s, t = lax.axis_index("seq"), lax.axis_index("tp")
        head = (s // 2) * self.per + t
        active = jnp.logical_and(t < self.per, head < H)
        return s, t, lax.rem(s, 2), head, active

    def head_device(self, index):
        head, core = index // 2, lax.rem(index, 2)
        return 2 * (head // self.per) + core, lax.rem(head, self.per)

    def device(self, linear):
        return linear // self.tp, lax.rem(linear, self.tp)


def busy(microseconds):
    return pl.CostEstimate(
        flops=int(microseconds * 1e9), bytes_accessed=int(microseconds * 3e6), transcendentals=0
    )


def remote(src, dst, send, recv, where):
    return pltpu.make_async_remote_copy(
        src_ref=src, dst_ref=dst, send_sem=send, recv_sem=recv, device_id=where, device_id_type=MESH
    )


def loop(count, step):
    def one(k, carry):
        step(k)
        return carry

    lax.fori_loop(0, count, one, 0)


class Dispatch:
    def __init__(self, place, cut):
        self.p, self.cut = place, cut
        self.sems = [2 * H, place.n, 1]

    def start_one(self, index, x, o, send, recv, here):
        p = self.p
        s, t, c, head, active = p.me()
        lin = s * p.tp + t
        ds, dt = p.head_device(index)
        mine = jnp.logical_and(ds == s, dt == t)
        source = self.cut(x, index // 2, lax.rem(index, 2))

        @pl.when(jnp.logical_not(mine))
        def _():
            remote(source, o.at[lin], send.at[index], recv.at[lin], (ds, dt)).start()

        @pl.when(mine)
        def _():
            pltpu.make_async_copy(source, o.at[lin], here.at[0]).start()

    def start(self, *refs):
        p = self.p
        lin = lax.axis_index("seq") * p.tp + lax.axis_index("tp")
        loop(2 * H, lambda k: self.start_one(lax.rem(k + lin, 2 * H), *refs))

    def finish(self, x, o, send, recv, here, arrived=None):
        p = self.p
        s, t, c, head, active = p.me()
        lin = s * p.tp + t

        @pl.when(active)
        def _():
            pltpu.make_async_copy(self.cut(x, head, c), o.at[lin], here.at[0]).wait()
            if arrived is not None:
                arrived(lin)

            def got(k):
                other = lax.rem(lin + 1 + k, p.n)
                remote(o.at[other], o.at[other], send.at[0], recv.at[other], (s, t)).wait_recv()
                if arrived is not None:
                    arrived(other)

            loop(p.n - 1, got)

        def sent(k):
            ds, dt = p.head_device(k)

            @pl.when(jnp.logical_not(jnp.logical_and(ds == s, dt == t)))
            def _():
                remote(
                    self.cut(x, k // 2, lax.rem(k, 2)), o.at[0], send.at[k], recv.at[0], (ds, dt)
                ).wait_send()

        loop(2 * H, sent)


class Collect:
    def __init__(self, place, into, halves=False):
        self.p, self.into, self.halves = place, into, halves
        self.sems = [place.n, 2 * H, 1]

    def start(self, x, o, send, recv, here):
        p = self.p
        s, t, c, head, active = p.me()
        lin = s * p.tp + t
        count = p.n // 2 if self.halves else p.n

        @pl.when(active)
        def _():
            def step(k):
                slot = lax.rem(k + lin, count)
                other = slot + c * count if self.halves else slot
                into = self.into(o, lax.rem(other, p.tp), head, c)

                @pl.when(other != lin)
                def _():
                    remote(
                        x.at[slot], into, send.at[slot], recv.at[head * 2 + c], p.device(other)
                    ).start()

                @pl.when(other == lin)
                def _():
                    pltpu.make_async_copy(x.at[slot], into, here.at[0]).start()

            loop(count, step)

    def got(self, index, x, o, send, recv, here):
        p = self.p
        s, t = lax.axis_index("seq"), lax.axis_index("tp")
        into = self.into(o, t, index // 2, lax.rem(index, 2))
        ds, dt = p.head_device(index)
        mine = jnp.logical_and(ds == s, dt == t)

        @pl.when(jnp.logical_not(mine))
        def _():
            remote(into, into, send.at[0], recv.at[index], (s, t)).wait_recv()

        @pl.when(mine)
        def _():
            pltpu.make_async_copy(x.at[0], into, here.at[0]).wait()

    def sent(self, x, o, send, recv, here):
        p = self.p
        s, t, c, head, active = p.me()
        lin = s * p.tp + t
        count = p.n // 2 if self.halves else p.n

        @pl.when(active)
        def _():
            def one(k):
                other = k + c * count if self.halves else k

                @pl.when(other != lin)
                def _():
                    remote(
                        x.at[k], x.at[k], send.at[k], recv.at[0], p.device(other)
                    ).wait_send()

            loop(count, one)

    def finish(self, *refs):
        p = self.p
        if self.halves:
            lin = lax.axis_index("seq") * p.tp + lax.axis_index("tp")
            half = lin // (p.n // 2)
            loop(H, lambda k: self.got(2 * k + half, *refs))
        else:
            loop(2 * H, lambda k: self.got(k, *refs))
        self.sent(*refs)


class Everyone:
    def __init__(self, place, whole):
        self.p, self.whole = place, whole
        self.sems = [place.n, place.n, 1]

    def start(self, x, o, send, recv, here):
        p = self.p
        s, t = lax.axis_index("seq"), lax.axis_index("tp")
        lin = s * p.tp + t
        pltpu.make_async_copy(x if self.whole else x.at[lin], o.at[lin], here.at[0]).start()

        def step(k):
            other = lax.rem(lin + 1 + k, p.n)
            remote(
                x if self.whole else x.at[other],
                o.at[lin],
                send.at[other],
                recv.at[lin],
                p.device(other),
            ).start()

        loop(p.n - 1, step)

    def finish(self, x, o, send, recv, here):
        p = self.p
        s, t = lax.axis_index("seq"), lax.axis_index("tp")
        lin = s * p.tp + t
        pltpu.make_async_copy(x if self.whole else x.at[lin], o.at[lin], here.at[0]).wait()

        def done(k):
            other = lax.rem(lin + 1 + k, p.n)
            both = remote(
                x if self.whole else x.at[other],
                o.at[other],
                send.at[other],
                recv.at[other],
                p.device(other),
            )
            both.wait_recv()
            both.wait_send()

        loop(p.n - 1, done)


class Group:
    def __init__(self, place, whole):
        self.p, self.whole = place, whole
        self.sems = [place.tp, place.tp, 1]

    def start(self, x, o, send, recv, here):
        p = self.p
        s, t = lax.axis_index("seq"), lax.axis_index("tp")
        pltpu.make_async_copy(x if self.whole else x.at[t], o.at[t], here.at[0]).start()
        for k in range(1, p.tp):
            other = lax.rem(t + k, p.tp)
            remote(
                x if self.whole else x.at[other], o.at[t], send.at[other], recv.at[t], (s, other)
            ).start()

    def finish(self, x, o, send, recv, here):
        p = self.p
        s, t = lax.axis_index("seq"), lax.axis_index("tp")
        pltpu.make_async_copy(x if self.whole else x.at[t], o.at[t], here.at[0]).wait()
        for k in range(1, p.tp):
            other = lax.rem(t + k, p.tp)
            both = remote(
                x if self.whole else x.at[other],
                o.at[other],
                send.at[other],
                recv.at[other],
                (s, other),
            )
            both.wait_recv()
            both.wait_send()


class Along:
    def __init__(self, place):
        self.depth = place.seq // 2
        self.sems = [self.depth, self.depth, 1]

    def start(self, x, o, send, recv, here):
        s, t = lax.axis_index("seq"), lax.axis_index("tp")
        z, c = s // 2, lax.rem(s, 2)
        pltpu.make_async_copy(x.at[z], o.at[z], here.at[0]).start()

        def step(k):
            other = lax.rem(z + 1 + k, self.depth)
            remote(x.at[other], o.at[z], send.at[other], recv.at[z], (2 * other + c, t)).start()

        loop(self.depth - 1, step)

    def finish(self, x, o, send, recv, here):
        s, t = lax.axis_index("seq"), lax.axis_index("tp")
        z, c = s // 2, lax.rem(s, 2)
        pltpu.make_async_copy(x.at[z], o.at[z], here.at[0]).wait()

        def done(k):
            other = lax.rem(z + 1 + k, self.depth)
            both = remote(
                x.at[other], o.at[other], send.at[other], recv.at[other], (2 * other + c, t)
            )
            both.wait_recv()
            both.wait_send()

        loop(self.depth - 1, done)


def greet(place):
    s, t = lax.axis_index("seq"), lax.axis_index("tp")
    lin = s * place.tp + t
    barrier = pltpu.get_barrier_semaphore()

    def hello(k):
        pl.semaphore_signal(
            barrier,
            inc=1,
            device_id=place.device(lax.rem(lin + 1 + k, place.n)),
            device_id_type=MESH,
        )

    loop(place.n - 1, hello)
    pl.semaphore_wait(barrier, place.n - 1)


def moves(place, parts, arrays, outs, ident, cost, work=None, operands=(), results=(), scratch=()):
    count, extra = len(parts), len(operands)

    def kernel(*refs):
        ins, given = refs[:count], refs[count : count + extra]
        refs = refs[count + extra :]
        into, made = refs[:count], refs[count : count + len(results)]
        refs = refs[count + len(results) :]
        sems, rest = refs[: 3 * count], refs[3 * count :]
        greet(place)
        for i, part in enumerate(parts):
            part.start(ins[i], into[i], *sems[3 * i : 3 * i + 3])
        if work is not None:
            work(given, made, rest)
        for i, part in enumerate(parts):
            part.finish(ins[i], into[i], *sems[3 * i : 3 * i + 3])

    return pl.pallas_call(
        kernel,
        out_shape=[jax.ShapeDtypeStruct(s, a.dtype) for s, a in zip(outs, arrays)]
        + [shape for shape, spec in results],
        in_specs=[ANY] * count + [spec for array, spec in operands],
        out_specs=[ANY] * count + [spec for shape, spec in results],
        scratch_shapes=[pltpu.SemaphoreType.DMA((k,)) for part in parts for k in part.sems]
        + list(scratch),
        compiler_params=pltpu.CompilerParams(
            collective_id=ident, has_side_effects=True, vmem_limit_bytes=vmem_cap
        ),
        cost_estimate=busy(cost),
    )(*arrays, *[array for array, spec in operands])


def gather_all(place, rows, run_pos, gain, weights, ident):
    n, tp, depth = place.n, place.tp, place.seq // 2
    count, width = rows.shape
    half = count // 2
    tell = Everyone(place, True)

    def relay(first, known, use, x, o, full, halves, z_up, z_down, by_x, by_y, half_x, half_y, across, here):
        s, t = lax.axis_index("seq"), lax.axis_index("tp")
        z, c = s // 2, lax.rem(s, 2)
        t_x = t + 1 - 2 * lax.rem(t, 2)
        t_y = lax.rem(t + 2, 4)
        t_d = t_x + 2 - 4 * (t_x // 2)

        def slot(zs, core, ts):
            return (2 * zs + core) * tp + ts

        def line(zs, source, step):
            at = slot(zs, c, t)
            sem = z_up if step > 0 else z_down
            return remote(source, o.at[at], sem.at[zs], full.at[at], (s + 2 * step, t))

        def side(zs, source, sem, ts):
            at = slot(zs, c, t)
            return remote(source, o.at[at], sem.at[zs], full.at[at], (s, ts))

        def other_core(zs, ts, source):
            at = slot(zs, c, ts)
            return remote(
                source, o.at[at], across.at[zs * tp + ts], full.at[at], (s + 1 - 2 * c, t)
            )

        def corner(zs, ts, low, sem, to):
            at = slot(zs, c, ts)
            part = o.at[at, low : low + half]
            return remote(
                part, part, sem.at[zs], halves.at[2 * at + low // half], (s, to)
            )

        def arrived(at):
            remote(o.at[at], o.at[at], here.at[0], full.at[at], (s, t)).wait_recv()

        def push(zs, source):
            @pl.when(jnp.logical_and(zs <= z, z < depth - 1))
            def _():
                line(zs, source, 1).start()

            @pl.when(jnp.logical_and(zs >= z, z > 0))
            def _():
                line(zs, source, -1).start()

            side(zs, source, by_x, t_x).start()
            side(zs, source, by_y, t_y).start()
            other_core(zs, t, source).start()

        def each(k, act):
            def one(sign):
                zs = z + (2 * sign - 1) * k
                valid = jnp.logical_and(zs >= 0, zs < depth)
                valid = jnp.logical_and(valid, jnp.logical_and(k >= 0, k + 1 > sign))

                @pl.when(valid)
                def _():
                    act(zs)

            loop(2, one)

        def from_line(zs):
            arrived(slot(zs, c, t))
            push(zs, o.at[slot(zs, c, t)])

        def from_sides(zs):
            arrived(slot(zs, c, t_x))
            corner(zs, t_x, 0, half_y, t_y).start()
            other_core(zs, t_x, o.at[slot(zs, c, t_x)]).start()
            arrived(slot(zs, c, t_y))
            corner(zs, t_y, half, half_x, t_x).start()
            other_core(zs, t_y, o.at[slot(zs, c, t_y)]).start()

        def from_corner(zs):
            at = slot(zs, c, t_d)
            for low in (0, half):
                part = o.at[at, low : low + half]
                remote(
                    part, part, here.at[0], halves.at[2 * at + low // half], (s, t)
                ).wait_recv()
            other_core(zs, t_d, o.at[at]).start()

        keep = pltpu.make_async_copy(x, o.at[slot(z, c, t)], here.at[0])
        keep.start()
        push(z, x)
        first()
        keep.wait()

        def use_block(k):
            def one(i):
                other, v = i // 4, lax.rem(i, 4)
                m_x, m_y = lax.rem(v, 2), v // 2
                x_bit, y_bit = lax.rem(t, 2), t // 2
                ts = 2 * (y_bit + m_y - 2 * y_bit * m_y) + x_bit + m_x - 2 * x_bit * m_x
                core = c + other - 2 * c * other

                def act(zs):
                    at = slot(zs, core, ts)

                    @pl.when(other > 0)
                    def _():
                        arrived(at)

                    use(at)

                each(k - m_x - m_y - other, act)

            loop(8, one)

        def wave(k):
            @pl.when(k > 0)
            def _():
                each(k, from_line)
                each(k - 1, from_sides)
                each(k - 2, from_corner)

            use_block(k)

            @pl.when(k == depth)
            def _():
                known()

        loop(depth + 3, wave)

        def sent(k):
            zs = k
            at = slot(zs, c, t)

            @pl.when(jnp.logical_and(zs <= z, z < depth - 1))
            def _():
                line(zs, o.at[at], 1).wait_send()

            @pl.when(jnp.logical_and(zs >= z, z > 0))
            def _():
                line(zs, o.at[at], -1).wait_send()

            side(zs, o.at[at], by_x, t_x).wait_send()
            side(zs, o.at[at], by_y, t_y).wait_send()
            corner(zs, t_x, 0, half_y, t_y).wait_send()
            corner(zs, t_y, half, half_x, t_x).wait_send()
            for ts in range(tp):
                other_core(zs, ts, o.at[at]).wait_send()

        loop(depth, sent)

    sems = [n, 2 * n] + [depth] * 6 + [depth * tp, 1]

    def kernel(x, r, gain, wq, wk, wv, out, pos, qkv, o, wide, out_sem, *refs):
        greet(place)

        def save(at):
            return pltpu.make_async_copy(o.at[at], out.at[at], out_sem.at[at])

        def use(at):
            save(at).start()
            x = o[at].astype(f32)
            x = (x * rms_scale(x) * gain[...]).astype(bf16)
            qkv[at] = dot(x, wide[...]).astype(bf16)

        def first():
            tell.start(r, pos, *refs[:3])
            for i, w in enumerate((wq, wk, wv)):
                wide[:, i * VW : (i + 1) * VW] = w[...]

        relay(first, lambda: tell.finish(r, pos, *refs[:3]), use, x, o, *refs[3:])
        loop(n, lambda k: save(k).wait())

    def column(g):
        s, t, c, head, active = place.me()
        return 0, jnp.minimum(head, H - 1)

    columns = pl.BlockSpec((width, VW), column)
    return pl.pallas_call(
        kernel,
        grid=(1,),
        out_shape=[
            jax.ShapeDtypeStruct((n,) + rows.shape, rows.dtype),
            jax.ShapeDtypeStruct((n,) + run_pos.shape, run_pos.dtype),
            jax.ShapeDtypeStruct((n, count, 3 * VW), bf16),
        ],
        in_specs=[ANY] * 2 + [VMEM] + [columns] * 3,
        out_specs=[ANY] * 2 + [VMEM],
        scratch_shapes=[
            pltpu.VMEM((n,) + rows.shape, rows.dtype),
            pltpu.VMEM((width, 3 * VW), bf16),
            pltpu.SemaphoreType.DMA((n,)),
        ]
        + [pltpu.SemaphoreType.DMA((k,)) for k in tell.sems + sems],
        compiler_params=pltpu.CompilerParams(
            collective_id=ident, has_side_effects=True, vmem_limit_bytes=vmem_cap
        ),
        cost_estimate=busy(50),
    )(rows, run_pos, gain, *weights)


def gather_all_plain(place, rows, run_pos, gain, weights):
    axes = ("seq", "tp")
    rows_all = lax.all_gather(rows, axes, axis=0, tiled=False)
    pos = lax.all_gather(run_pos, axes, axis=0, tiled=False)
    x = rows_all.astype(f32)
    x = (x * rms_scale(x) * gain).astype(bf16)
    s, t, c, head, active = place.me()
    column = jnp.minimum(head, H - 1) * VW
    qkv = [
        dot(x, lax.dynamic_slice_in_dim(w, column, VW, 1)).astype(bf16) for w in weights
    ]
    return rows_all, pos, jnp.concatenate(qkv, axis=2)


def feed_forward(place, mixed, rows_all, cotangent_all, gain, w_out, w_gate, w_up, w_down, ident):
    n, tp, half = place.n, place.tp, mixed.shape[1]
    count, width = rows_all.shape[1:]
    hid = w_gate.shape[1]
    chunk = 256

    def into(o, t, h, c):
        return o.at[
            t,
            pl.ds(pl.multiple_of(half * c, half), half),
            pl.ds(pl.multiple_of(VW * h, VW), VW),
        ]

    back = Collect(place, into)

    def kernel(*refs):
        mixed, rows_all, cot, gain, wo_in, wg_in, wu_in, wd_in, *refs = refs
        parts, mixed_out, hidden, middle, middle_grad, branch, mixed_grad, gain_part, *refs = refs
        mixed_v, x_v, rows_v, both_v, send_v, recv_v, own_part, held, *refs = refs
        wo, wg, wu, wd, *sems = refs
        share_send, share_recv, part_send, part_recv, w_sem, x_sem, out_sem, mixed_sem = sems[3:]
        s, t = lax.axis_index("seq"), lax.axis_index("tp")
        greet(place)
        back.start(mixed, mixed_v, *sems[:3])

        def fetch(m):
            return pltpu.make_async_copy(rows_all.at[s * tp + m], x_v.at[m], x_sem.at[m])

        loads = [
            pltpu.make_async_copy(a, b, w_sem.at[i])
            for i, (a, b) in enumerate(((wo_in, wo), (wg_in, wg), (wu_in, wu), (wd_in, wd)))
        ]
        loop(tp, lambda m: fetch(m).start())
        for load in loads:
            load.start()

        def share(k, c, slot):
            other = lax.rem(t + k, tp)
            at = slot(other)
            return remote(
                mixed_v.at[t, half * c : half * c + half, :],
                mixed_v.at[at, half * c : half * c + half, :],
                share_send.at[2 * other + c],
                share_recv.at[2 * at + c],
                (s, other),
            )

        def give(k, slot):
            other = lax.rem(t + k, tp)
            at = slot(other)
            return remote(
                send_v.at[other], recv_v.at[at], part_send.at[other], part_recv.at[at], (s, other)
            )

        for c in range(2):
            loop(H, lambda h: back.got(2 * h + c, mixed, mixed_v, *sems[:3]))
            for k in range(1, tp):
                share(k, c, lambda other: t).start()
        loop(tp, lambda m: fetch(m).wait())
        for load in loads:
            load.wait()

        def member(k):
            m = lax.rem(t + k, tp)

            @pl.when(k > 0)
            def _():
                for c in range(2):
                    share(k, c, lambda other: other).wait_recv()

            x = x_v[m].astype(f32) + dot(mixed_v[m], wo[...])
            rows = (x * rms_scale(x) * gain[...]).astype(bf16)
            rows_v[m] = rows
            gate = dot(rows, wg[...])
            up = dot(rows, wu[...])
            sig = jax.nn.sigmoid(gate)
            act = gate * sig
            hidden[m] = (act * up).astype(bf16)
            grad = dot_nt(cot[m], wd[...])
            gate_rows = (grad * up * sig * (1.0 + gate * (1.0 - sig))).astype(bf16)
            up_rows = (grad * act).astype(bf16)
            both_v[m, :, :hid] = gate_rows
            both_v[m, :, hid:] = up_rows
            part = dot_nt(gate_rows, wg[...]) + dot_nt(up_rows, wu[...])

            @pl.when(k == 0)
            def _():
                own_part[...] = part
                middle[...] = x

            @pl.when(k > 0)
            def _():
                send_v[m] = part.astype(bf16)
                give(k, lambda other: t).start()

        loop(tp, member)
        keep = pltpu.make_async_copy(mixed_v, mixed_out, mixed_sem.at[0])
        keep.start()

        def copy(i):
            at = pl.ds(pl.multiple_of(chunk * i, chunk), chunk)
            return pltpu.make_async_copy(held.at[at], parts.at[at], out_sem.at[i])

        def weight_rows(i):
            at = pl.ds(pl.multiple_of(chunk * i, chunk), chunk)
            held[at, :hid] = dot_tn(
                cot[:, :, at].reshape(tp * count, chunk), hidden[...].reshape(tp * count, hid)
            ).astype(bf16)
            held[at, hid:] = dot_tn(
                rows_v[:, :, at].reshape(tp * count, chunk),
                both_v[...].reshape(tp * count, 2 * hid),
            ).astype(bf16)
            copy(i).start()

        loop(width // chunk, weight_rows)
        total = own_part[...]
        for k in range(1, tp):
            give(k, lambda other: other).wait_recv()
            total = total + recv_v[lax.rem(t + k, tp)].astype(f32)
        mid = middle[...]
        scale = rms_scale(mid)
        gain_part[...] = jnp.sum(total * mid * scale, axis=0, keepdims=True)
        grad = cot[t].astype(f32) + rms_back(mid, scale, gain[...], total)
        middle_grad[...] = grad
        branch[...] = grad.astype(bf16)
        mixed_grad[...] = dot_nt(grad.astype(bf16), wo[...]).astype(bf16)
        loop(width // chunk, lambda i: copy(i).wait())
        keep.wait()
        for k in range(1, tp):
            give(k, lambda other: other).wait_send()
            for c in range(2):
                share(k, c, lambda other: other).wait_send()
        back.sent(mixed, mixed_v, *sems[:3])

    struct = jax.ShapeDtypeStruct
    group = (tp, count, width)
    return pl.pallas_call(
        kernel,
        out_shape=[
            struct((width, 3 * hid), bf16),
            struct(group, bf16),
            struct((tp, count, hid), bf16),
            struct((count, width), f32),
            struct((count, width), f32),
            struct((count, width), bf16),
            struct((count, width), bf16),
            struct((1, width), f32),
        ],
        in_specs=[ANY, ANY, VMEM, VMEM] + [ANY] * 4,
        out_specs=[ANY, ANY] + [VMEM] * 6,
        scratch_shapes=[
            pltpu.VMEM(group, bf16),
            pltpu.VMEM(group, bf16),
            pltpu.VMEM(group, bf16),
            pltpu.VMEM((tp, count, 2 * hid), bf16),
            pltpu.VMEM(group, bf16),
            pltpu.VMEM(group, bf16),
            pltpu.VMEM((count, width), f32),
            pltpu.VMEM((width, 3 * hid), bf16),
            pltpu.VMEM(w_out.shape, bf16),
            pltpu.VMEM(w_gate.shape, bf16),
            pltpu.VMEM(w_up.shape, bf16),
            pltpu.VMEM(w_down.shape, bf16),
        ]
        + [
            pltpu.SemaphoreType.DMA((k,))
            for k in back.sems + [2 * tp, 2 * tp, tp, tp, 4, tp, width // chunk, 1]
        ],
        compiler_params=pltpu.CompilerParams(
            collective_id=ident, has_side_effects=True, vmem_limit_bytes=vmem_cap
        ),
        cost_estimate=busy(60),
    )(mixed, rows_all, cotangent_all, gain, w_out, w_gate, w_up, w_down)


def finish_heads(
    place,
    dq,
    dkv,
    dkv_sib,
    rows_all,
    gain,
    weights,
    branch_grad,
    mixed_all,
    inputs,
    middle_grad,
    ident,
):
    n, half = place.n, dq.shape[1]
    width = rows_all.shape[2]
    part, chunk, depth = width // n, 256, place.seq // 2
    lot = 8 if n <= 64 else 2
    out_type = bf16 if part % 16 == 0 else f32

    def into(o, t, h, c):
        return o.at[
            pl.ds(pl.multiple_of(half * c, half), half),
            pl.ds(pl.multiple_of(3 * VW * h, 3 * VW), 3 * VW),
        ]

    back, share = Collect(place, into), Group(place, True)

    def kernel(*refs):
        dq, dkv, dkv_sib, rows_all, gain, *refs = refs
        weights, refs = refs[:3], refs[3:]
        branch, mixed_in, inputs, middle_grad, *refs = refs
        input_grad, gain_part, weight_half, out_own, *refs = refs
        other_dkv, grads, rows_back, raw, held, away, other, w_all, branch_all, mixed, *refs = refs
        out_part, out_away, out_other, *sems = refs
        s, t = lax.axis_index("seq"), lax.axis_index("tp")
        c = lax.rem(s, 2)
        send, recv, raw_sem, w_sem, mixed_sem = sems[6:]
        sibling = (s + 1 - 2 * c, t)
        greet(place)
        swap = remote(dkv_sib, other_dkv, send.at[0], recv.at[0], sibling)
        swap.start()
        share.start(branch, branch_all, *sems[3:6])

        def fetch(i):
            return pltpu.make_async_copy(
                rows_all.at[
                    pl.ds(lot * i, lot), pl.ds(pl.multiple_of(half * c, half), half), :
                ],
                raw.at[lax.rem(i, 2)],
                raw_sem.at[lax.rem(i, 2)],
            )

        fetch(0).start()
        loads = [
            pltpu.make_async_copy(w, w_all.at[i], w_sem.at[i]) for i, w in enumerate(weights)
        ]
        for load in loads:
            load.start()
        mixed_load = pltpu.make_async_copy(mixed_in, mixed, mixed_sem.at[0])
        mixed_load.start()
        swap.wait_recv()

        def join(i):
            grads[i, :, :VW] = dq[i]
            grads[i, :, VW:] = (dkv[i] + other_dkv[i].astype(f32)).astype(bf16)

        loop(n, join)
        back.start(grads, rows_back, *sems[:3])
        held[...] = jnp.zeros_like(held)

        def rows(i):
            @pl.when(i + 1 < n // lot)
            def _():
                fetch(i + 1).start()

            fetch(i).wait()
            x = raw[lax.rem(i, 2)].reshape(lot * half, width).astype(f32)
            x = (x * rms_scale(x) * gain[...]).astype(bf16)
            g = grads[pl.ds(lot * i, lot)].reshape(lot * half, 3 * VW)
            for k in range(width // chunk):
                held[k * chunk : (k + 1) * chunk, :] += dot_tn(
                    x[:, k * chunk : (k + 1) * chunk], g
                )

        loop(n // lot, rows)
        low = pl.multiple_of(c * (width // 2), width // 2)
        high = pl.multiple_of((1 - c) * (width // 2), width // 2)
        away[...] = held[pl.ds(high, width // 2), :].astype(bf16)
        cross = remote(away, other, send.at[1], recv.at[1], sibling)
        cross.start()
        mixed_load.wait()
        share.finish(branch, branch_all, *sems[3:6])

        def out_rows(i):
            at = pl.ds(pl.multiple_of(chunk * i, chunk), chunk)
            out_part[at, :] = dot_tn(
                mixed[:, :, at].reshape(-1, chunk), branch_all[...].reshape(-1, width)
            ).astype(out_type)

        loop(HW // chunk, out_rows)

        def out_picked(z, core):
            picked = jnp.zeros((part, width), f32)
            for k in range(2 * place.tp):
                low = part * (2 * place.tp * z + k)
                here = k == core * place.tp + t
                picked = picked + jnp.where(here, out_part[low : low + part, :], 0.0)
            return picked.astype(bf16)

        def out_block(z, core):
            if part % 16:
                return out_picked(z, core)
            base = part * (place.tp * (2 * z + core) + t)
            return out_part[pl.ds(pl.multiple_of(base, part), part), :].astype(bf16)

        for z in range(depth):
            out_away[z] = out_block(z, 1 - c)
        out_cross = remote(out_away, out_other, send.at[2], recv.at[2], sibling)
        out_cross.start()
        back.finish(grads, rows_back, *sems[:3])
        for load in loads:
            load.wait()
        total = None
        for h in range(0, H, 2):
            for i in range(3):
                at = (3 * h + i) * VW
                x = jnp.concatenate(
                    [rows_back[:, at : at + VW], rows_back[:, at + 3 * VW : at + 4 * VW]], axis=1
                )
                new = dot_nt(x, w_all[i, :, h * VW : (h + 2) * VW])
                total = new if total is None else total + new
        x = inputs[...].astype(f32)
        scale = rms_scale(x)
        gain_part[...] = jnp.sum(total * x * scale, axis=0, keepdims=True)
        done = middle_grad[...] + rms_back(x, scale, gain[...], total)
        quarter = half // 2
        for b in range(2):
            for h in range(2):
                to, from_ = (2 * b + h) * quarter, (2 * h + b) * quarter
                input_grad[to : to + quarter, :] = done[from_ : from_ + quarter]
        cross.wait_recv()
        weight_half[...] = (held[pl.ds(low, width // 2), :] + other[...].astype(f32)).astype(bf16)
        out_cross.wait_recv()
        for z in range(depth):
            out_own[z] = (out_block(z, c).astype(f32) + out_other[z].astype(f32)).astype(bf16)
        swap.wait_send()
        cross.wait_send()
        out_cross.wait_send()

    return pl.pallas_call(
        kernel,
        out_shape=[
            jax.ShapeDtypeStruct((2 * half, width), f32),
            jax.ShapeDtypeStruct((1, width), f32),
            jax.ShapeDtypeStruct((width // 2, 3 * VW), bf16),
            jax.ShapeDtypeStruct((depth, part, width), bf16),
        ],
        in_specs=[VMEM, VMEM, ANY, ANY, VMEM] + [ANY] * 5 + [VMEM] * 2,
        out_specs=[VMEM] * 4,
        scratch_shapes=[
            pltpu.VMEM((n, half, 2 * VW), bf16),
            pltpu.VMEM((n, half, 3 * VW), bf16),
            pltpu.VMEM((2 * half, 3 * HW), bf16),
            pltpu.VMEM((2, lot, half, width), bf16),
            pltpu.VMEM((width, 3 * VW), f32),
            pltpu.VMEM((width // 2, 3 * VW), bf16),
            pltpu.VMEM((width // 2, 3 * VW), bf16),
            pltpu.VMEM((3,) + weights[0].shape, bf16),
            pltpu.VMEM((place.tp,) + branch_grad.shape, bf16),
            pltpu.VMEM(mixed_all.shape, bf16),
            pltpu.VMEM((HW, width), out_type),
            pltpu.VMEM((depth, part, width), bf16),
            pltpu.VMEM((depth, part, width), bf16),
        ]
        + [pltpu.SemaphoreType.DMA((k,)) for k in back.sems + share.sems + [3, 3, 2, 3, 1]],
        compiler_params=pltpu.CompilerParams(
            collective_id=ident, has_side_effects=True, vmem_limit_bytes=vmem_cap
        ),
        cost_estimate=busy(40),
    )(
        dq,
        dkv,
        dkv_sib,
        rows_all,
        gain,
        *weights,
        branch_grad,
        mixed_all,
        inputs,
        middle_grad,
    )


def last_moves(place, weight_half, small, ffn_out, out_part, middle, lambda_params, ident):
    n, tp, seq = place.n, place.tp, place.seq
    count, width = middle.shape
    part = width // n
    kinds = [
        Collect(place, lambda o, t, h, c: o.at[h], True),
        Everyone(place, False),
        Group(place, False),
        Along(place),
    ]
    arrays = [weight_half, small, ffn_out, out_part]
    landing = [
        pltpu.VMEM((H, part, 3 * VW), bf16),
        pltpu.VMEM(small.shape, f32),
        pltpu.VMEM(ffn_out.shape, bf16),
        pltpu.VMEM(out_part.shape, bf16),
    ]

    def kernel(*refs):
        ins, middle, params, refs = refs[:4], refs[4], refs[5], refs[6:]
        output, query_grad, key_grad, value_grad, out_grad, sums, *refs = refs
        lambda_grads, lambda_total, lambda_norm, *refs = refs
        lands, sems = refs[:4], refs[4:]
        greet(place)
        every = list(zip(kinds, ins, lands, [sems[3 * i : 3 * i + 3] for i in range(4)]))
        for kind, source, land, sem in every:
            kind.start(source, land, *sem)

        def finish(i):
            kind, source, land, sem = every[i]
            kind.finish(source, land, *sem)

        finish(1)
        sums[...] = jnp.sum(lands[1][...], axis=0)
        lambda_sum = jnp.sum(sums[3:4, :], axis=1, keepdims=True)
        squares = jnp.zeros((1, 1), f32)
        for i, sign in ((0, 1.0), (2, -1.0)):
            left, right = params[i : i + 1, :], params[i + 1 : i + 2, :]
            factor = sign * lambda_sum * jnp.exp(jnp.sum(left * right, axis=1, keepdims=True))
            for row, vector in ((i, right), (i + 1, left)):
                grad = factor * vector
                lambda_grads[row : row + 1, :] = grad
                squares = squares + jnp.sum(grad * grad, axis=1, keepdims=True)
        lambda_total[...] = lambda_sum
        lambda_norm[...] = jnp.sqrt(squares)
        finish(2)
        total = middle[...]
        for m in range(tp):
            total = total + lands[2][m].astype(f32)
        total = total.astype(bf16)
        quarter = count // 4
        for b in range(2):
            for h in range(2):
                low, from_ = (2 * b + h) * quarter, (2 * h + b) * quarter
                output[low : low + quarter, :] = total[from_ : from_ + quarter]
        finish(0)
        for h in range(H):
            for i, grad in enumerate((query_grad, key_grad, value_grad)):
                grad[:, h * VW : (h + 1) * VW] = lands[0][h, :, i * VW : (i + 1) * VW].astype(f32)
        finish(3)
        total = lands[3][0].astype(f32)
        for m in range(1, seq // 2):
            total = total + lands[3][m].astype(f32)
        out_grad[...] = total

    struct = jax.ShapeDtypeStruct
    return pl.pallas_call(
        kernel,
        out_shape=[struct((count, width), bf16)]
        + [struct((part, HW), f32)] * 4
        + [struct((8, VW), f32), struct(lambda_params.shape, f32)]
        + [struct((1, 1), f32)] * 2,
        in_specs=[ANY] * 4 + [VMEM] * 2,
        out_specs=[VMEM] * 9,
        scratch_shapes=landing
        + [pltpu.SemaphoreType.DMA((k,)) for kind in kinds for k in kind.sems],
        compiler_params=pltpu.CompilerParams(
            collective_id=ident, has_side_effects=True, vmem_limit_bytes=vmem_cap
        ),
        cost_estimate=busy(35),
    )(*arrays, middle, lambda_params)


def spans(n, count, step):
    if n <= 32:
        for j in range(count):
            step(j)
    else:
        loop(count, step)


def fold(n, count, step, carry):
    if n <= 32:
        for k in range(count):
            carry = step(k, carry)
        return carry
    return lax.fori_loop(0, count, step, carry)


def aligned(value, unit):
    return value if isinstance(value, int) else pl.multiple_of(value, unit)


def query_rows(n):
    return 256 if n <= 64 else 128


def two_maps(rows):
    lane = lax.broadcasted_iota(jnp.int32, rows.shape, 1)
    zero = jnp.zeros_like(rows)
    return jnp.concatenate(
        [jnp.where(lane < HALF, rows, zero), jnp.where(lane < HALF, zero, rows)], axis=0
    )


def fwd_kernel(n, pos, lam, qkv, gain, mixed, mix, lse, qs, ks, vs, order, score):
    qb = query_rows(n)
    kb_rows = 2 * qb
    c = lax.rem(lax.axis_index("seq"), 2)

    def place_run(run):
        order[pos[run // 2, lax.rem(run, 2) * 64] // 64] = run

    loop(2 * n, place_run)
    lambda_value = lam[0]

    def sort(p):
        run = order[p]
        i, b = run // 2, pl.multiple_of(32 * lax.rem(run, 2), 32)
        for h in range(2):
            at = pl.ds(pl.multiple_of(64 * p + 32 * h, 32), 32)
            rows = pl.ds(pl.multiple_of(64 * h + b, 32), 32)
            ks[at, :] = qkv[i, rows, VW : 2 * VW]
            vs[at, :] = qkv[i, rows, 2 * VW :]
        mine = qkv[i, pl.ds(pl.multiple_of(64 * c + b, 32), 32), :VW]
        qs[pl.ds(pl.multiple_of(32 * p, 32), 32), :] = mine * jnp.asarray(0.125, bf16)

    loop(2 * n, sort)

    def block(j):
        at = pl.ds(aligned(qb * j, qb), qb)
        q2 = two_maps(qs[at, :])

        def scores(kb):
            return dot_nt(q2, ks[pl.ds(aligned(kb_rows * kb, kb_rows), kb_rows), :])

        def lanes(top, s):
            for i in range(kb_rows // 128):
                top = jnp.maximum(top, s[:, 128 * i : 128 * i + 128])
            return top

        def first(kb, top):
            s = scores(kb)
            score[:, pl.ds(aligned(kb_rows * kb, kb_rows), kb_rows)] = s
            return lanes(top, s)

        top = fold(n, j, first, jnp.full((2 * qb, 128), masked_score, f32))
        s = scores(j)
        row = lax.broadcasted_iota(jnp.int32, s.shape, 0)
        row = lax.rem(row, qb)
        allowed = (
            lax.broadcasted_iota(jnp.int32, s.shape, 1)
            <= 64 * (row // 32) + lax.rem(row, 32) + 32 * c
        )
        s = jnp.where(allowed, s, masked_score)
        score[:, pl.ds(aligned(kb_rows * j, kb_rows), kb_rows)] = s
        high = jnp.max(lanes(top, s), axis=1, keepdims=True)
        ones = jnp.ones((kb_rows, VW), bf16)

        def second(kb, acc):
            here = pl.ds(aligned(kb_rows * kb, kb_rows), kb_rows)
            weights = jnp.exp(score[:, here] - high).astype(bf16)
            return acc + dot(weights, jnp.concatenate([vs[here, :], ones], axis=1))

        acc = fold(n, j + 1, second, jnp.zeros((2 * qb, 2 * VW), f32))
        total = acc[:, VW:]
        mixes = acc[:, :VW] / total
        lse[j] = jnp.transpose(high + jnp.log(total))[:8, :]
        mix[0, at, :] = mixes[:qb]
        mix[1, at, :] = mixes[qb:]
        out = mixes[:qb] - lambda_value * mixes[qb:]
        out = (out * rms_scale(out) * gain[...]).astype(bf16)
        for i in range(qb // 32):
            run = order[j * (qb // 32) + i]
            b = pl.multiple_of(32 * lax.rem(run, 2), 32)
            mixed[run // 2, pl.ds(b, 32), :] = out[32 * i : 32 * i + 32]

    spans(n, n * 64 // qb, block)


def attend(place, pos, lam, qkv, gain):
    n = place.n
    rows = 64 * n
    qb = query_rows(n)
    return pl.pallas_call(
        functools.partial(fwd_kernel, n),
        out_shape=[
            jax.ShapeDtypeStruct((n, 64, VW), bf16),
            jax.ShapeDtypeStruct((2, rows, VW), f32),
            jax.ShapeDtypeStruct((rows // qb, 8, 2 * qb), f32),
            jax.ShapeDtypeStruct((rows, VW), bf16),
            jax.ShapeDtypeStruct((2 * rows, VW), bf16),
            jax.ShapeDtypeStruct((2 * rows, VW), bf16),
            jax.ShapeDtypeStruct((2 * n,), jnp.int32),
        ],
        in_specs=[SMEM, SMEM, VMEM, VMEM],
        out_specs=[VMEM] * 6 + [SMEM],
        scratch_shapes=[pltpu.VMEM((2 * qb, 2 * rows), f32)],
        compiler_params=pltpu.CompilerParams(vmem_limit_bytes=vmem_cap),
        cost_estimate=busy(20),
    )(pos, lam, qkv, gain)


def bwd_kernel(
    n,
    lam,
    grad,
    mix,
    lse,
    qs,
    ks,
    vs,
    order,
    gain,
    dq,
    dkv,
    dkv_sib,
    sums,
    dk,
    dv,
):
    qb = query_rows(n)
    kb_rows = 2 * qb
    c = lax.rem(lax.axis_index("seq"), 2)
    lambda_value = lam[0]
    dk[...] = jnp.zeros_like(dk)
    dv[...] = jnp.zeros_like(dv)
    sums[...] = jnp.zeros_like(sums)

    def block(j):
        at = pl.ds(aligned(qb * j, qb), qb)
        pieces = []
        for i in range(qb // 32):
            run = order[j * (qb // 32) + i]
            b = pl.multiple_of(32 * lax.rem(run, 2), 32)
            pieces.append(grad[run // 2, pl.ds(b, 32), :])
        mixed_grad = jnp.concatenate(pieces, axis=0).astype(f32)
        mix_1, mix_2 = mix[0, at, :], mix[1, at, :]
        out = mix_1 - lambda_value * mix_2
        scale = rms_scale(out)
        sums[0:1, :] += jnp.sum(mixed_grad * out * scale, axis=0, keepdims=True) * (
            1.0 - lambda_init
        )
        heads_grad = rms_back(out, scale, gain[...], mixed_grad).astype(bf16)
        grad_f = heads_grad.astype(f32)
        dot_2 = grad_f * mix_2
        sums[1:2, :] += -jnp.sum(dot_2, axis=0, keepdims=True)
        delta_1 = jnp.sum(jnp.transpose(grad_f * mix_1), axis=0, keepdims=True)
        delta_2 = -lambda_value * jnp.sum(jnp.transpose(dot_2), axis=0, keepdims=True)
        q2 = two_maps(qs[at, :])
        lse_now = lse[j][0:1, :]
        q2_t = jnp.transpose(q2)
        grad_t = jnp.transpose(heads_grad)

        def piece(kb, acc, diagonal):
            here = pl.ds(aligned(kb_rows * kb, kb_rows), kb_rows)
            keys = ks[here, :]
            s = dot(keys, q2_t) - lse_now
            if diagonal:
                col = lax.rem(lax.broadcasted_iota(jnp.int32, s.shape, 1), qb)
                allowed = (
                    lax.broadcasted_iota(jnp.int32, s.shape, 0)
                    <= 64 * (col // 32) + lax.rem(col, 32) + 32 * c
                )
                s = jnp.where(allowed, s, masked_score)
            prob = jnp.exp(s)
            prob_1, prob_2 = prob[:, :qb], prob[:, qb:]
            value_dot = dot(vs[here, :], grad_t)
            grads = jnp.concatenate(
                [
                    (prob_1 * (value_dot - delta_1)).astype(bf16),
                    (prob_2 * (-lambda_value * value_dot - delta_2)).astype(bf16),
                ],
                axis=1,
            )
            dv[here, :] += dot((prob_1 - lambda_value * prob_2).astype(bf16), heads_grad)
            dk[here, :] += dot(grads, q2)
            return acc + dot_tn(keys, grads)

        acc = fold(
            n, j, lambda kb, a: piece(kb, a, False), jnp.zeros((VW, 2 * qb), f32)
        )
        acc = jnp.transpose(piece(j, acc, True))
        lane = lax.broadcasted_iota(jnp.int32, (qb, VW), 1)
        done = (jnp.where(lane < HALF, acc[:qb], acc[qb:]) * 0.125).astype(bf16)
        for i in range(qb // 32):
            run = order[j * (qb // 32) + i]
            b = pl.multiple_of(32 * lax.rem(run, 2), 32)
            dq[run // 2, pl.ds(b, 32), :] = done[32 * i : 32 * i + 32]

    spans(n, n * 64 // qb, block)

    def unsort(p):
        run = order[p]
        b = pl.multiple_of(32 * lax.rem(run, 2), 32)
        low = pl.multiple_of(64 * p + 32 * c, 32)
        high = pl.multiple_of(64 * p + 32 * (1 - c), 32)
        dkv[run // 2, pl.ds(b, 32), :VW] = dk[pl.ds(low, 32), :]
        dkv[run // 2, pl.ds(b, 32), VW:] = dv[pl.ds(low, 32), :]
        dkv_sib[run // 2, pl.ds(b, 32), :VW] = dk[pl.ds(high, 32), :].astype(bf16)
        dkv_sib[run // 2, pl.ds(b, 32), VW:] = dv[pl.ds(high, 32), :].astype(bf16)

    loop(2 * n, unsort)


def attend_back(place, lam, grad, saved, gain):
    n = place.n
    rows = 64 * n
    qb = query_rows(n)
    return pl.pallas_call(
        functools.partial(bwd_kernel, n),
        out_shape=[
            jax.ShapeDtypeStruct((n, 64, VW), bf16),
            jax.ShapeDtypeStruct((n, 64, 2 * VW), f32),
            jax.ShapeDtypeStruct((n, 64, 2 * VW), bf16),
            jax.ShapeDtypeStruct((8, VW), f32),
        ],
        in_specs=[SMEM] + [VMEM] * 6 + [SMEM, VMEM],
        out_specs=[VMEM] * 4,
        scratch_shapes=[pltpu.VMEM((2 * rows, VW), f32)] * 2,
        compiler_params=pltpu.CompilerParams(vmem_limit_bytes=vmem_cap),
        cost_estimate=busy(35),
    )(lam, grad, *saved, gain)


def swap_halves(rows):
    count, width = rows.shape
    return rows.reshape(2, 2, count // 4, width).transpose(1, 0, 2, 3).reshape(count, width)


def body(
    place,
    inputs,
    positions,
    attn_gain,
    w_query,
    w_key,
    w_value,
    w_out,
    lambda_params,
    sub_gain,
    ffn_gain,
    w_gate,
    w_up,
    w_down,
    cotangent,
):
    n, tp, seq = place.n, place.tp, place.seq
    s, t, core, head, active = place.me()
    inputs, cotangent = swap_halves(inputs), swap_halves(cotangent)
    row_count, width = inputs.shape
    half = row_count // 2
    part = width // n
    inputs_f = inputs.astype(f32)
    attn_scale = rms_scale(inputs_f)
    first_exp = jnp.exp(jnp.sum(lambda_params[0] * lambda_params[1]))
    second_exp = jnp.exp(jnp.sum(lambda_params[2] * lambda_params[3]))
    lambda_value = first_exp - second_exp + lambda_init
    lam = lambda_value.reshape(1)

    weights = (w_query, w_key, w_value)
    gain_row = attn_gain.reshape(1, width)
    if tp == 4:
        rows_all, pos, qkv = gather_all(
            place, inputs, positions.reshape(1, row_count), gain_row, weights, 1
        )
    else:
        rows_all, pos, qkv = gather_all_plain(
            place, inputs, positions.reshape(1, row_count), gain_row, weights
        )
    cotangent_late, pos = lax.optimization_barrier((cotangent, pos))
    cotangent_all = lax.all_gather(cotangent_late, "tp", axis=0, tiled=True)
    head_gain = (sub_gain * (1.0 - lambda_init)).reshape(1, VW)
    mixed, *saved = attend(place, pos.reshape(n, row_count), lam, qkv, head_gain)
    parts, mixed_all, hidden, middle, middle_grad, branch_grad, mixed_grad, ffn_gain_part = (
        feed_forward(
            place,
            mixed,
            rows_all,
            cotangent_all.reshape(tp, row_count, width),
            ffn_gain.reshape(1, width),
            w_out,
            w_gate,
            w_up,
            w_down,
            2,
        )
    )
    hidden_width = hidden.shape[2]

    def scatter_rows(array):
        return lax.psum_scatter(array, "seq", scatter_dimension=0, tiled=True)

    ffn_grads = scatter_rows(parts)

    def head_block(x, h, c):
        return x.at[
            pl.ds(pl.multiple_of(half * c, half), half), pl.ds(pl.multiple_of(VW * h, VW), VW)
        ]

    def ffn_result(given, made, rest):
        hid, weight = given
        (out,) = made
        for i in range(tp):
            out[i] = dot(hid[i], weight[...]).astype(bf16)

    grad_heads, ffn_out = moves(
        place,
        [Dispatch(place, head_block)],
        [mixed_grad],
        [(n, half, VW)],
        4,
        20,
        work=ffn_result,
        operands=[(hidden, VMEM), (w_down, VMEM)],
        results=[(jax.ShapeDtypeStruct((tp, row_count, width), bf16), VMEM)],
    )
    dq, dkv, dkv_sib, sums = attend_back(place, lam, grad_heads, saved, head_gain)
    input_grad, attn_gain_part, weight_half, out_part = finish_heads(
        place,
        dq,
        dkv,
        dkv_sib,
        rows_all,
        gain_row,
        weights,
        branch_grad,
        mixed_all,
        inputs,
        middle_grad,
        5,
    )
    sums = jnp.where(active, sums, 0.0)
    pad = ((0, 0), (0, 128 - part))
    small = jnp.stack(
        [
            jnp.pad(attn_gain_part.reshape(n, part), pad),
            jnp.pad(ffn_gain_part.reshape(n, part), pad),
            jnp.broadcast_to(sums[0], (n, VW)),
            jnp.broadcast_to(sums[1], (n, VW)),
        ]
        + [jnp.zeros((n, VW), f32)] * 4,
        axis=1,
    )
    (
        output,
        query_grad,
        key_grad,
        value_grad,
        out_grad,
        small_sum,
        lambda_grads,
        lambda_total,
        lambda_norm,
    ) = last_moves(
        place,
        weight_half.reshape(n // 2, part, 3 * VW),
        small,
        ffn_out,
        out_part,
        middle,
        lambda_params,
        6,
    )
    lambda_total, lambda_norm = lambda_total.reshape(()), lambda_norm.reshape(())
    ffn_grads = ffn_grads.astype(f32)
    down_grad = ffn_grads[:, :hidden_width].T
    gate_grad = ffn_grads[:, hidden_width : 2 * hidden_width]
    up_grad = ffn_grads[:, 2 * hidden_width :]
    return (
        output,
        input_grad,
        small_sum[0, :part],
        query_grad,
        key_grad,
        value_grad,
        out_grad,
        lambda_grads,
        small_sum[2],
        small_sum[1, :part],
        gate_grad,
        up_grad,
        down_grad,
        lambda_total,
        lambda_norm,
    )


def solution(mesh):
    place = Place(mesh.shape["seq"], mesh.shape["tp"])
    both = ("seq", "tp")
    placed = (
        P(both, None),
        P(both),
        P(),
        P(),
        P(),
        P(),
        P(),
        P(),
        P(),
        P(),
        P(None, "tp"),
        P(None, "tp"),
        P("tp", None),
        P(both, None),
    )
    return jax.shard_map(
        functools.partial(body, place),
        mesh=mesh,
        in_specs=placed,
        out_specs=(
            P(both, None),
            P(both, None),
            P(both),
            P(both, None),
            P(both, None),
            P(both, None),
            P(both, None),
            P(),
            P(),
            P(both),
            P("seq", "tp"),
            P("seq", "tp"),
            P("tp", "seq"),
            P(),
            P(),
        ),
        check_vma=False,
    )
```
